32 devices in a mesh: section: 2 (over core), dp: 16 (over z, y, x).
Axes of the slice: x: 2, y: 2, z: 4, core: 2. Of those that a mesh axis runs over, the one named last changes fastest.
Arguments:
- tokens: bfloat16 [32, 1024, 768], P('dp'), may hold values from -6 to 6
- segments: int32 [32, 1024], P('dp'), may hold values from 0 to 3, never falling along the last dimension, each value on 1 to 512 neighbouring positions
- cotangent: bfloat16 [32, 1024, 768], P('dp'), may hold values from -6 to 6
- gain_attn: float32 [2, 768], P('section', 'dp'), may hold values from 0.1 to 1.9
- gain_ffn: float32 [2, 768], P('section', 'dp'), may hold values from 0.1 to 1.9
- w_query: float32 [2, 768, 768], P('section', 'dp'), may hold values from -0.21875 to 0.21875
- w_key: float32 [2, 768, 768], P('section', 'dp'), may hold values from -0.21875 to 0.21875
- w_value: float32 [2, 768, 768], P('section', 'dp'), may hold values from -0.21875 to 0.21875
- w_out: float32 [2, 768, 768], P('section', None, 'dp'), may hold values from -0.875 to 0.875
- w_in: float32 [2, 768, 3072], P('section', 'dp'), may hold values from -0.21875 to 0.21875
- w_back: float32 [2, 3072, 768], P('section', None, 'dp'), may hold values from -0.15625 to 0.15625
- mix_logits: float32 [2, 12, 12], P('section'), may hold values from -1.75 to 1.75
- mix_weights: float32 [2, 12, 12], P('section'), may hold values from -1.75 to 1.75
Outputs:
- section_out: bfloat16 [2, 32, 1024, 768], P('section', 'dp')
- section_grad: bfloat16 [2, 32, 1024, 768], P('section', 'dp')
- grad_gain_attn: float32 [2, 768], P('section', 'dp')
- grad_gain_ffn: float32 [2, 768], P('section', 'dp')
- grad_query: float32 [2, 768, 768], P('section', 'dp')
- grad_key: float32 [2, 768, 768], P('section', 'dp')
- grad_value: float32 [2, 768, 768], P('section', 'dp')
- grad_out: float32 [2, 768, 768], P('section', None, 'dp')
- grad_in: float32 [2, 768, 3072], P('section', 'dp')
- grad_back: float32 [2, 3072, 768], P('section', None, 'dp')
- grad_mix_logits: float32 [2, 12, 12], P('section')
- grad_mix_weights: float32 [2, 12, 12], P('section')
The draws below stay inside these ranges and needn't reach their ends.
Inputs may be any that keep to these rules, and one draw needn't show every extreme that they name: `segments`: along each row the segment number never falls; each segment covers at most 512 positions.
All inputs are finite; a program needn't handle non-finite values.
Results may differ from the reference program's by a relative error of at most 0.035.
The reference program's roundings to bfloat16 on the way count: a program that leaves them out, or rounds other values in their place, can miss the bound.
Values may be sent and summed in bfloat16 or wider, within the bound.
No kernel may reach another device: no remote copies, remote signals or barrier semaphores. Data moves between devices by JAX's collectives and lax.ppermute only.
A program may use at most 640 MiB of HBM per device.

```python
import math
import jax
import jax.numpy as jnp
import numpy as np
from jax import lax

D = 768
HEADS = 12
FF = 3072
LEN = 1024
HD = 768
ROWS = 32


def raised(array, key, source, target, shards_of, factor):
    owner, partner = [(jnp.arange(array.shape[dim]) // (array.shape[dim] // shards_of)).reshape([-1 if axis == dim else 1 for axis in range(array.ndim)]) for dim in (source, target)]
    chosen = jax.random.permutation(key, shards_of)[partner]
    strong = (owner == chosen) | (owner == (partner + shards_of // 2) % shards_of)
    return jnp.where(strong, factor * array, array)


def block_scale(key, extent, shards, least, high):
    factor_of, own = 1.0, jax.random.fold_in(key, 6)
    for dim, parts in shards:
        draws = jnp.exp(jax.random.uniform(jax.random.fold_in(own, dim), (parts,), jnp.float32, least / len(shards), high / len(shards)))
        factor_of = factor_of * jnp.repeat(draws, extent[dim] // parts).reshape([-1 if axis == dim else 1 for axis in range(len(extent))])
    return factor_of


def profile(count, total, most, skew):
    portions = [(1 << 20) // math.isqrt(grade ** skew) + 1 for grade in range(2, count + 1)]
    spare, counts = total - most - (count - 1), [1] * (count - 1)
    while spare > 0:
        candidates = [i for i in range(count - 1) if counts[i] < most]
        pool, remaining = sum([portions[i] for i in candidates]), spare
        for i in candidates:
            extra = min(most - counts[i], max(1, remaining * portions[i] // pool), spare)
            counts[i] = counts[i] + extra
            spare = spare - extra
    return np.array([most] + counts)


def uneven_parts(rng, count, total, limit, lean):
    if count == 2:
        one = jax.random.randint(rng, (), max(1, total - limit), min(limit, total - 1) + 1)
        return jnp.stack([one, total - one])
    tallies = jnp.asarray(profile(count, total, limit, lean), jnp.int32)
    couples = (count - 1) // 2
    giver, sink = tallies[1:1 + 2 * couples:2], tallies[2:2 + 2 * couples:2]
    room = jnp.minimum(giver - 1, limit - sink)
    moved = jax.random.randint(jax.random.fold_in(rng, 1), (couples,), 0, 1 << 20) % (room + 1)
    tallies = tallies.at[1:1 + 2 * couples:2].set(giver - moved).at[2:2 + 2 * couples:2].set(sink + moved)
    return tallies[jax.random.permutation(jax.random.fold_in(rng, 2), count)]


def gaussian(key, extent, width, reach, split=(), held_as=jnp.bfloat16):
    loudness = block_scale(key, extent, split, -0.22, 0.18) if split else 1.0
    values = jax.random.normal(key, extent, jnp.float32) * width * loudness
    return jnp.minimum(jnp.maximum(values, -reach), reach).astype(held_as)


def heavy_noise(stream_key, shape, width, limit, split, heavy, kind=jnp.bfloat16):
    result = width * jax.random.normal(stream_key, shape, jnp.float32)
    if split:
        result = result * block_scale(stream_key, shape, split, -0.22, 0.18)
    return jnp.clip(raised(result, jax.random.fold_in(stream_key, 3), *heavy), -limit, limit).astype(kind)


def setup_inputs(seed: int = 0) -> dict:
    splits = jax.random.split(jax.random.key(seed), 14)
    tokens = heavy_noise(splits[0], (ROWS, LEN, D), 1.0, 6.0, ((0, 16),), (0, 2, 16, 2.0))
    segments = jax.vmap(lambda own: jnp.searchsorted(jnp.cumsum(uneven_parts(own, max(4, LEN // 256), LEN, LEN // 2, 1)), jnp.arange(LEN), side="right"))(jax.random.split(splits[1], ROWS)).reshape((ROWS, LEN)).astype(jnp.int32)
    cotangent = heavy_noise(splits[2], (ROWS, LEN, D), 1.0, 6.0, ((0, 16),), (0, 2, 16, 2.0))
    gain_attn = jnp.clip(1.0 + 0.18 * jax.random.normal(splits[3], (2, D), jnp.float32), 0.1, 1.9)
    gain_ffn = jnp.clip(1.0 + 0.18 * jax.random.normal(splits[4], (2, D), jnp.float32), 0.1, 1.9)
    w_query = gaussian(splits[5], (2, D, HD), D ** -0.5, 0.21875, ((0, 2), (1, 16)), jnp.float32)
    w_key = gaussian(splits[6], (2, D, HD), D ** -0.5, 0.21875, ((0, 2), (1, 16)), jnp.float32)
    w_value = gaussian(splits[7], (2, D, HD), D ** -0.5, 0.21875, ((0, 2), (1, 16)), jnp.float32)
    w_out = gaussian(splits[8], (2, HD, D), (HD // 16) ** -0.5, 0.875, ((0, 2), (2, 16)), jnp.float32)
    w_in = gaussian(splits[9], (2, D, FF), D ** -0.5, 0.21875, ((0, 2), (1, 16)), jnp.float32)
    w_back = gaussian(splits[10], (2, FF, D), (FF // 2) ** -0.5, 0.15625, ((0, 2), (2, 16)), jnp.float32)
    mix_logits = gaussian(splits[11], (2, HEADS, HEADS), HEADS ** -0.5, 1.75, ((0, 2),), jnp.float32)
    mix_weights = gaussian(splits[12], (2, HEADS, HEADS), HEADS ** -0.5, 1.75, ((0, 2),), jnp.float32)
    return dict(tokens=tokens, segments=segments, cotangent=cotangent, gain_attn=gain_attn, gain_ffn=gain_ffn, w_query=w_query, w_key=w_key, w_value=w_value, w_out=w_out, w_in=w_in, w_back=w_back, mix_logits=mix_logits, mix_weights=mix_weights)


EPS = 1e-06
HIGH = lax.Precision.HIGHEST

@jax.custom_vjp
def low(v):
    return lax.optimization_barrier(v.astype(jnp.bfloat16)).astype(jnp.float32)

@jax.custom_vjp
def low_back(v):
    return v

def low_keep(v):
    return (low(v), None)

def low_pass(kept, grad):
    return (grad,)

def back_keep(v):
    return (v, None)

def back_low(kept, grad):
    return (low(grad),)
low.defvjp(low_keep, low_pass)
low_back.defvjp(back_keep, back_low)

def product(left, right):
    return jnp.dot(left, right, precision=HIGH, preferred_element_type=jnp.float32)

def rms_scale(values, gain):
    return values * lax.rsqrt(lax.optimization_barrier(jnp.mean(values * values, axis=-1, keepdims=True)) + EPS) * gain

def attention(queries, keys_all, values_all, segment, mix_logits, mix_weights):
    length = queries.shape[0]
    head_count = mix_logits.shape[0]
    head_size = queries.shape[1] // head_count
    query_heads = queries.reshape(length, head_count, head_size)
    key_heads = keys_all.reshape(length, head_count, head_size)
    value_heads = values_all.reshape(length, head_count, head_size)
    scores = low_back(jnp.einsum('qhe,khe->hqk', query_heads, key_heads, precision=HIGH) * head_size ** (-0.5))
    premixed = jnp.einsum('hqk,hg->gqk', scores, mix_logits, precision=HIGH)
    places = jnp.arange(length)
    allowed = (segment[:, None] == segment[None, :]) & (places[None, :] <= places[:, None])
    premixed = jnp.where(allowed[None], premixed, -1e+30)
    softened = jax.nn.softmax(premixed, axis=-1)
    remixed = low(jnp.einsum('gqk,gh->hqk', softened, mix_weights, precision=HIGH))
    attended = jnp.einsum('hqk,khe->qhe', remixed, value_heads, precision=HIGH)
    return low(low_back(attended.reshape(length, head_count * head_size)))

def layer(inputs, segment, params):
    gain_attn, gain_ffn, w_query, w_key, w_value, w_out, w_in, w_back, mix_logits, mix_weights = params
    normed = low(rms_scale(inputs, low(gain_attn)))
    queries = low(low_back(product(normed, low(w_query))))
    keys_all = low(low_back(product(normed, low(w_key))))
    values_all = low(low_back(product(normed, low(w_value))))
    attended = jax.checkpoint(attention)(queries, keys_all, values_all, segment, mix_logits, mix_weights)
    middle = inputs + low_back(product(attended, low(w_out)))
    normed_two = low(rms_scale(middle, low(gain_ffn)))
    before = low_back(product(normed_two, low(w_in)))
    hidden = low(jax.nn.gelu(before))
    return middle + low_back(product(hidden, low(w_back)))

def reference(tokens, segments, cotangent, gain_attn, gain_ffn, w_query, w_key, w_value, w_out, w_in, w_back, mix_logits, mix_weights):
    stacked = (gain_attn, gain_ffn, w_query, w_key, w_value, w_out, w_in, w_back, mix_logits, mix_weights)
    first = tuple((param[0].astype(jnp.float32) for param in stacked))
    second = tuple((param[1].astype(jnp.float32) for param in stacked))
    initial = (tuple((jnp.zeros_like(param) for param in first)), tuple((jnp.zeros_like(param) for param in second)))

    def one_row(carry, row_parts):
        inputs_row, segment_row, cot_row = row_parts
        inputs = inputs_row.astype(jnp.float32)

        def forward(layer_input, params_one, params_two, shift_in):
            out_one = layer(layer_input, segment_row, params_one)
            passed = low(low_back(out_one)) + shift_in
            out_two = layer(passed, segment_row, params_two)
            return (out_one, out_two)
        (out_one, out_two), pull = jax.vjp(forward, inputs, first, second, jnp.zeros_like(inputs))
        grad_input, grad_first, grad_second, grad_shift = pull((jnp.zeros_like(out_one), cot_row.astype(jnp.float32)))
        summed_first = tuple((left + right for left, right in zip(carry[0], grad_first)))
        summed_second = tuple((left + right for left, right in zip(carry[1], grad_second)))
        outputs = (out_one.astype(jnp.bfloat16), out_two.astype(jnp.bfloat16), grad_input.astype(jnp.bfloat16), grad_shift.astype(jnp.bfloat16))
        return ((summed_first, summed_second), outputs)
    totals, (outs_one, outs_two, grads_one, grads_two) = lax.scan(one_row, initial, (tokens, segments, cotangent))
    grads = tuple((jnp.stack([left, right]) for left, right in zip(totals[0], totals[1])))
    section_out = jnp.stack([outs_one, outs_two])
    section_grad = jnp.stack([grads_one, grads_two])
    return (section_out, section_grad, grads[0], grads[1], grads[2], grads[3], grads[4], grads[5], grads[6], grads[7], grads[8], grads[9])
```

```python
import functools
import math

import jax
import jax.numpy as jnp
from jax import lax
from jax.experimental import pallas as pl
from jax.experimental.pallas import tpu as pltpu
from jax.sharding import PartitionSpec as P

EPS = 1e-06
NEGATIVE = -1e30
LOG2E = math.log2(math.e)
BF = jnp.bfloat16
F32 = jnp.float32
QB = 128
REACH = 512
ROWB = 256
VMEM = 60 * 1024 * 1024

SMEM_SPEC = pl.BlockSpec(memory_space=pltpu.SMEM)


def dot(left, right):
    return jnp.dot(left, right, preferred_element_type=F32)


def dot_t(left, right):
    return lax.dot_general(left, right, (((1,), (1,)), ((), ())), preferred_element_type=F32)


def whole(shape):
    return pl.BlockSpec(shape, lambda *_: (0,) * len(shape))


def column(shape, place):
    return pl.BlockSpec(shape, lambda *_: (0, place))


def params():
    return pltpu.CompilerParams(vmem_limit_bytes=VMEM)


def project_kernel(x_ref, gain_ref, wq_ref, wk_ref, wv_ref, normed_ref, q_ref, qt_ref, k_ref, kt_ref, v_ref, vt_ref):
    x = x_ref[...].astype(F32)
    scale = lax.rsqrt(jnp.mean(x * x, axis=-1, keepdims=True) + EPS)
    normed = (x * scale * gain_ref[...]).astype(BF)
    normed_ref[...] = normed
    for w_ref, y_ref, yt_ref in ((wq_ref, q_ref, qt_ref), (wk_ref, k_ref, kt_ref), (wv_ref, v_ref, vt_ref)):
        y = dot(normed, w_ref[...])
        y_ref[...] = y.astype(BF)
        yt_ref[...] = y.T.astype(BF)


def project(x, gain, w, places):
    length, width = x.shape
    rows = pl.BlockSpec((ROWB, width), lambda i: (i, 0))
    cols = pl.BlockSpec((width, ROWB), lambda i: (0, i))
    flat = jax.ShapeDtypeStruct((length, width), BF)
    turned = jax.ShapeDtypeStruct((width, length), BF)
    return pl.pallas_call(
        project_kernel,
        grid=(length // ROWB,),
        in_specs=[rows, whole((1, width))] + [column((width, width), p) for p in places],
        out_specs=[rows, rows, cols, rows, cols, rows, cols],
        out_shape=[flat, flat, turned, flat, turned, flat, turned],
        compiler_params=params(),
        cost_estimate=pl.CostEstimate(flops=6 * length * width * width, bytes_accessed=16 * length * width, transcendentals=0),
        name="project",
    )(x, gain, w, w, w)


def attend_kernel(
    heads, start_ref, mw_ref, ml_ref, qt_ref, k_ref, vt_ref, segc_ref, segr_ref, o_ref, a_ref, mixed_ref, out_acc
):
    block = pl.program_id(0)
    start = start_ref[block]
    size = qt_ref.shape[0] // heads

    def body(blocks):
        span = blocks * QB
        offset = pl.multiple_of(start * QB, QB)
        keys = k_ref[pl.ds(offset, span), :]
        values = vt_ref[:, pl.ds(offset, span)]
        place_k = offset + lax.broadcasted_iota(jnp.int32, (span, QB), 0)
        place_q = block * QB + lax.broadcasted_iota(jnp.int32, (span, QB), 1)
        allowed = (segc_ref[pl.ds(offset, span), :] == segr_ref[...]) & (place_k <= place_q)
        bias = jnp.where(allowed, 0.0, NEGATIVE)
        bias = jnp.concatenate([bias, bias], 1)
        for pair in range(heads // 2):
            parts = []
            for g in (2 * pair, 2 * pair + 1):
                parts.append(
                    jnp.concatenate(
                        [
                            (qt_ref[h * size : (h + 1) * size, :].astype(F32) * ml_ref[h, g]).astype(BF)
                            for h in range(heads)
                        ],
                        0,
                    )
                )
            scores = dot(keys, jnp.concatenate(parts, 1)) + bias
            powers = jnp.exp2(scores - jnp.max(scores, axis=0, keepdims=True))
            soft = (powers * (1.0 / jnp.sum(powers, axis=0, keepdims=True))).astype(BF)
            a_ref[0, pair, 0:span, :] = soft
            mixed = dot(values, soft)
            mixed_ref[2 * pair] = mixed[:, :QB].astype(BF)
            mixed_ref[2 * pair + 1] = mixed[:, QB:].astype(BF)
            for h in range(heads):
                own = slice(h * size, (h + 1) * size)
                term = mixed[own, :QB] * mw_ref[2 * pair, h] + mixed[own, QB:] * mw_ref[2 * pair + 1, h]
                if pair == 0:
                    out_acc[own, :] = term
                else:
                    out_acc[own, :] += term
        o_ref[...] = out_acc[...].T.astype(BF)

    for blocks in range(1, REACH // QB + 2):
        pl.when(block - start + 1 == blocks)(functools.partial(body, blocks))


def attend(start, mw, ml, qt, k, vt, segc, segr):
    width, length = qt.shape
    heads = mw.shape[0]
    steps = length // QB
    most = REACH + QB
    rows = pl.BlockSpec((QB, width), lambda i, s: (i, 0))
    cols = pl.BlockSpec((width, QB), lambda i, s: (0, i))
    return pl.pallas_call(
        functools.partial(attend_kernel, heads),
        grid_spec=pltpu.PrefetchScalarGridSpec(
            num_scalar_prefetch=1,
            grid=(steps,),
            in_specs=[
                SMEM_SPEC,
                SMEM_SPEC,
                cols,
                whole((length, width)),
                whole((width, length)),
                whole((length, 1)),
                pl.BlockSpec((1, QB), lambda i, s: (0, i)),
            ],
            out_specs=[
                rows,
                pl.BlockSpec((1, heads // 2, most, 2 * QB), lambda i, s: (i, 0, 0, 0)),
                pl.BlockSpec((heads, width, QB), lambda i, s: (0, 0, i)),
            ],
            scratch_shapes=[pltpu.VMEM((width, QB), F32)],
        ),
        out_shape=[
            jax.ShapeDtypeStruct((length, width), BF),
            jax.ShapeDtypeStruct((steps, heads // 2, most, 2 * QB), BF),
            jax.ShapeDtypeStruct((heads, width, length), BF),
        ],
        compiler_params=params(),
        cost_estimate=pl.CostEstimate(
            flops=4 * length * most * width * heads, bytes_accessed=40 << 20, transcendentals=length * most * heads
        ),
        name="attend",
    )(start, mw, ml, qt, k, vt, segc, segr)


def attend_back_kernel(
    heads,
    start_ref,
    mw_ref,
    ml_ref,
    mlx_ref,
    mwx_ref,
    q_ref,
    qt_ref,
    do_ref,
    dot_ref,
    kt_ref,
    v_ref,
    a_ref,
    mixed_ref,
    dq_ref,
    dk_ref,
    dv_ref,
    gml_ref,
    gmw_ref,
    dk_acc,
    dv_acc,
    dqt_acc,
    dz_all,
    a_all,
    q_all,
    do_all,
):
    block = pl.program_id(0)
    start = start_ref[block]
    size = qt_ref.shape[0] // heads
    head_rows = [slice(h * size, (h + 1) * size) for h in range(heads)]

    @pl.when(block == 0)
    def _():
        for ref in (dk_acc, dv_acc, gml_ref, gmw_ref):
            ref[...] = jnp.zeros_like(ref)

    def body(blocks):
        span = blocks * QB
        offset = pl.multiple_of(start * QB, QB)
        values = v_ref[pl.ds(offset, span), :]
        keys = kt_ref[:, pl.ds(offset, span)]
        q = q_ref[...].astype(F32)
        do = do_ref[...].astype(F32)
        for pair in range(heads // 2):
            both = (2 * pair, 2 * pair + 1)
            lanes = slice(2 * QB * pair, 2 * QB * (pair + 1))
            parts = []
            for g in both:
                parts.append(
                    jnp.concatenate([(dot_ref[own, :].astype(F32) * mw_ref[g, h]).astype(BF) for h, own in enumerate(head_rows)], 0)
                )
            dsoft = dot(values, jnp.concatenate(parts, 1))
            soft = a_ref[0, pair, 0:span, :]
            wide = soft.astype(F32)
            product = wide * dsoft
            dz = (product - wide * jnp.sum(product, axis=0, keepdims=True)).astype(BF)
            dz_all[0:span, lanes] = dz
            a_all[0:span, lanes] = soft
            for t, g in enumerate(both):
                at = slice((2 * pair + t) * QB, (2 * pair + t + 1) * QB)
                q_all[at, :] = (q * mlx_ref[g : g + 1, :]).astype(BF)
                do_all[at, :] = (do * mwx_ref[g : g + 1, :]).astype(BF)
            side = dot(keys, dz)
            for h, own in enumerate(head_rows):
                terms = (side[own, :QB], side[own, QB:])
                term = terms[0] * ml_ref[h, both[0]] + terms[1] * ml_ref[h, both[1]]
                if pair == 0:
                    dqt_acc[own, :] = term
                else:
                    dqt_acc[own, :] += term
                qth = qt_ref[own, :].astype(F32)
                doth = dot_ref[own, :].astype(F32)
                for g, piece in zip(both, terms):
                    gml_ref[g, h] += jnp.sum((qth * piece).reshape(size // 8, 8, QB), axis=0)
                    gmw_ref[g, h] += jnp.sum((doth * mixed_ref[g, own, :].astype(F32)).reshape(size // 8, 8, QB), axis=0)
        dv_acc[pl.ds(offset, span), :] += dot(a_all[0:span, :], do_all[...])
        dk_acc[pl.ds(offset, span), :] += dot(dz_all[0:span, :], q_all[...])
        dq_ref[...] = dqt_acc[...].T.astype(BF)

    for blocks in range(1, REACH // QB + 2):
        pl.when(block - start + 1 == blocks)(functools.partial(body, blocks))

    @pl.when(block == pl.num_programs(0) - 1)
    def _():
        dk_ref[...] = dk_acc[...].astype(BF)
        dv_ref[...] = dv_acc[...].astype(BF)


def attend_back(start, mw, ml, mlx, mwx, q, qt, do, dot_, kt, v, soft, mixed):
    length, width = q.shape
    heads = mw.shape[0]
    steps = length // QB
    most = REACH + QB
    rows = pl.BlockSpec((QB, width), lambda i, s: (i, 0))
    cols = pl.BlockSpec((width, QB), lambda i, s: (0, i))
    flat = jax.ShapeDtypeStruct((length, width), BF)
    sums = jax.ShapeDtypeStruct((heads, heads, 8, QB), F32)
    return pl.pallas_call(
        functools.partial(attend_back_kernel, heads),
        grid_spec=pltpu.PrefetchScalarGridSpec(
            num_scalar_prefetch=1,
            grid=(steps,),
            in_specs=[
                SMEM_SPEC,
                SMEM_SPEC,
                whole((heads, width)),
                whole((heads, width)),
                rows,
                cols,
                rows,
                cols,
                whole((width, length)),
                whole((length, width)),
                pl.BlockSpec((1, heads // 2, most, 2 * QB), lambda i, s: (i, 0, 0, 0)),
                pl.BlockSpec((heads, width, QB), lambda i, s: (0, 0, i)),
            ],
            out_specs=[rows, whole((length, width)), whole((length, width)), whole(sums.shape), whole(sums.shape)],
            scratch_shapes=[
                pltpu.VMEM((length, width), F32),
                pltpu.VMEM((length, width), F32),
                pltpu.VMEM((width, QB), F32),
                pltpu.VMEM((most, heads * QB), BF),
                pltpu.VMEM((most, heads * QB), BF),
                pltpu.VMEM((heads * QB, width), BF),
                pltpu.VMEM((heads * QB, width), BF),
            ],
        ),
        out_shape=[flat, flat, flat, sums, sums],
        compiler_params=params(),
        cost_estimate=pl.CostEstimate(
            flops=8 * length * most * width * heads, bytes_accessed=50 << 20, transcendentals=0
        ),
        name="attend_back",
    )(start, mw, ml, mlx, mwx, q, qt, do, dot_, kt, v, soft, mixed)


def gelu_both(b):
    root = math.sqrt(2.0 / math.pi)
    square = b * b
    t = jnp.tanh(root * (b + 0.044715 * (square * b)))
    half = 0.5 * (1.0 + t)
    slope = half + 0.5 * b * (1.0 - t * t) * (root * (1.0 + 3.0 * 0.044715 * square))
    return b * half, slope


def feed_kernel(x_ref, o_ref, gain_ref, wo_ref, wi_ref, wb_ref, y_ref, middle_ref, normed_ref, slope_ref, hidden_ref):
    middle = x_ref[...].astype(F32) + dot_t(o_ref[...], wo_ref[...])
    middle_ref[...] = middle
    scale = lax.rsqrt(jnp.mean(middle * middle, axis=-1, keepdims=True) + EPS)
    normed = (middle * scale * gain_ref[...]).astype(BF)
    normed_ref[...] = normed
    wide = wi_ref.shape[1]
    part = wide // 4
    for c in range(4):
        own = slice(c * part, (c + 1) * part)
        hidden, slope = gelu_both(dot(normed, wi_ref[:, own]))
        hidden_ref[:, own] = hidden.astype(BF)
        slope_ref[:, own] = slope.astype(BF)
    y_ref[...] = (middle + dot_t(hidden_ref[...], wb_ref[...])).astype(BF)


def feed(x, o, gain, w, place_out, place_in, place_back):
    length, width = x.shape
    wide = 4 * width
    rows = pl.BlockSpec((ROWB, width), lambda i: (i, 0))
    rows_wide = pl.BlockSpec((ROWB, wide), lambda i: (i, 0))
    flat = jax.ShapeDtypeStruct((length, width), BF)
    flat_wide = jax.ShapeDtypeStruct((length, wide), BF)
    return pl.pallas_call(
        feed_kernel,
        grid=(length // ROWB,),
        in_specs=[
            rows,
            rows,
            whole((1, width)),
            column((width, width), place_out),
            column((width, wide), place_in),
            column((width, wide), place_back),
        ],
        out_specs=[rows, rows, rows, rows_wide, rows_wide],
        out_shape=[flat, jax.ShapeDtypeStruct((length, width), F32), flat, flat_wide, flat_wide],
        compiler_params=params(),
        cost_estimate=pl.CostEstimate(
            flops=18 * length * width * width, bytes_accessed=30 << 20, transcendentals=length * wide
        ),
        name="feed",
    )(x, o, gain, w, w, w)


def norm_back(values, gain, grad):
    scale = lax.rsqrt(jnp.mean(values * values, axis=-1, keepdims=True) + EPS)
    unit = values * scale
    dn = grad * gain
    back = scale * (dn - unit * jnp.mean(dn * unit, axis=-1, keepdims=True))
    return back, jnp.sum(grad * unit, axis=0, keepdims=True)


def feed_back_kernel(
    dy_ref, slope_ref, middle_ref, gain_ref, wo_ref, wi_ref, wb_ref, gf_ref, dmiddle_ref, ga_ref, do_ref, dot_ref, gg_ref
):
    @pl.when(pl.program_id(0) == 0)
    def _():
        gg_ref[...] = jnp.zeros_like(gg_ref)

    dy = dy_ref[...]
    wide = wi_ref.shape[1]
    part = wide // 4
    for c in range(4):
        own = slice(c * part, (c + 1) * part)
        gf_ref[:, own] = (dot(dy, wb_ref[:, own]) * slope_ref[:, own].astype(F32)).astype(BF)
    dnormed = dot_t(gf_ref[...], wi_ref[...])
    back, gg = norm_back(middle_ref[...], gain_ref[...], dnormed)
    gg_ref[...] += gg
    dmiddle = dy.astype(F32) + back
    dmiddle_ref[...] = dmiddle
    ga = dmiddle.astype(BF)
    ga_ref[...] = ga
    do = dot(ga, wo_ref[...])
    do_ref[...] = do.astype(BF)
    dot_ref[...] = do.T.astype(BF)


def feed_back(dy, slope, middle, gain, w, place_out, place_in, place_back):
    length, width = dy.shape
    wide = 4 * width
    rows = pl.BlockSpec((ROWB, width), lambda i: (i, 0))
    rows_wide = pl.BlockSpec((ROWB, wide), lambda i: (i, 0))
    flat = jax.ShapeDtypeStruct((length, width), BF)
    return pl.pallas_call(
        feed_back_kernel,
        grid=(length // ROWB,),
        in_specs=[
            rows,
            rows_wide,
            rows,
            whole((1, width)),
            column((width, width), place_out),
            column((width, wide), place_in),
            column((width, wide), place_back),
        ],
        out_specs=[rows_wide, rows, rows, rows, pl.BlockSpec((width, ROWB), lambda i: (0, i)), whole((1, width))],
        out_shape=[
            jax.ShapeDtypeStruct((length, wide), BF),
            jax.ShapeDtypeStruct((length, width), F32),
            flat,
            flat,
            jax.ShapeDtypeStruct((width, length), BF),
            jax.ShapeDtypeStruct((1, width), F32),
        ],
        compiler_params=params(),
        cost_estimate=pl.CostEstimate(flops=18 * length * width * width, bytes_accessed=40 << 20, transcendentals=0),
        name="feed_back",
    )(dy, slope, middle, gain, w, w, w)


def project_back_kernel(dq_ref, dk_ref, dv_ref, x_ref, dmiddle_ref, gain_ref, wq_ref, wk_ref, wv_ref, dx_ref, gg_ref):
    @pl.when(pl.program_id(0) == 0)
    def _():
        gg_ref[...] = jnp.zeros_like(gg_ref)

    dnormed = dot_t(dq_ref[...], wq_ref[...]) + dot_t(dk_ref[...], wk_ref[...]) + dot_t(dv_ref[...], wv_ref[...])
    back, gg = norm_back(x_ref[...].astype(F32), gain_ref[...], dnormed)
    gg_ref[...] += gg
    dx_ref[...] = (dmiddle_ref[...] + back).astype(BF)


def project_back(dq, dk, dv, x, dmiddle, gain, w, places):
    length, width = x.shape
    rows = pl.BlockSpec((ROWB, width), lambda i: (i, 0))
    return pl.pallas_call(
        project_back_kernel,
        grid=(length // ROWB,),
        in_specs=[rows] * 5 + [whole((1, width))] + [column((width, width), p) for p in places],
        out_specs=[rows, whole((1, width))],
        out_shape=[jax.ShapeDtypeStruct((length, width), BF), jax.ShapeDtypeStruct((1, width), F32)],
        compiler_params=params(),
        cost_estimate=pl.CostEstimate(flops=6 * length * width * width, bytes_accessed=18 << 20, transcendentals=0),
        name="project_back",
    )(dq, dk, dv, x, dmiddle, gain, w, w, w)


def weight_grad(left, right):
    return lax.dot_general(left, right, (((0,), (0,)), ((), ())), preferred_element_type=F32).astype(BF)


def mix_tables(mix_logits, mix_weights, size):
    scaled = mix_logits * (LOG2E * size ** (-0.5))
    wide_logits = jnp.repeat(scaled.T, size, axis=1)
    wide_weights = jnp.repeat(mix_weights, size, axis=1)
    return scaled, mix_logits * size ** (-0.5), wide_logits, wide_weights


def layer_forward(x, seg, weights, tables):
    gains, w_qkv, at_qkv, w_rest, at_rest = weights
    start, segc, segr = seg
    scaled, _, _, mix_weights = tables[:4]
    normed, q, qt, k, kt, v, vt = project(x, gains[0], w_qkv, at_qkv)
    o, soft, mixed = attend(start, tables[4], scaled, qt, k, vt, segc, segr)
    y, middle, normed_two, slope, hidden = feed(x, o, gains[1], w_rest, *at_rest)
    return y, (x, normed, q, qt, kt, v, o, soft, mixed, middle, normed_two, slope, hidden)


def layer_backward(dy, seg, kept, weights, tables):
    gains, w_qkv, at_qkv, w_rest, at_rest = weights
    x, normed, q, qt, kt, v, o, soft, mixed, middle, normed_two, slope, hidden = kept
    start = seg[0]
    _, plain, wide_logits, wide_weights, mix_weights = tables
    gf, dmiddle, ga, do, dot_, gg_ffn = feed_back(dy, slope, middle, gains[1], w_rest, *at_rest)
    grad_back = weight_grad(dy, hidden)
    grad_in = weight_grad(normed_two, gf)
    grad_out = weight_grad(ga, o)
    size = q.shape[1] // mix_weights.shape[0]
    unscaled = wide_logits * (1.0 / LOG2E)
    dq, dk, dv, gml, gmw = attend_back(
        start, mix_weights, plain, unscaled, wide_weights, q, qt, do, dot_, kt, v, soft, mixed
    )
    grads_qkv = [weight_grad(normed, g) for g in (dq, dk, dv)]
    dx, gg_attn = project_back(dq, dk, dv, x, dmiddle, gains[0], w_qkv, at_qkv)
    gml = jnp.sum(gml, axis=(2, 3)).T * size ** (-0.5)
    gmw = jnp.sum(gmw, axis=(2, 3))
    return dx, (grad_in, grad_back, grad_out), grads_qkv, (gg_attn, gg_ffn, gml, gmw)


def windows(seg):
    length = seg.shape[0]
    last = seg[QB - 1 :: QB]
    first = seg[::QB]
    start = jnp.sum((last[None, :] < first[:, None]).astype(jnp.int32), axis=1)
    return start, seg[:, None], seg[None, :]


AXES = ("dp", "section")


def swap(x):
    return lax.ppermute(x, "section", [(0, 1), (1, 0)])


def on_device(
    tokens,
    segments,
    cotangent,
    gain_attn,
    gain_ffn,
    w_query,
    w_key,
    w_value,
    w_out,
    w_in,
    w_back,
    mix_logits,
    mix_weights,
):
    section = lax.axis_index("section")
    first = section == 0
    width = tokens.shape[2]
    heads = mix_logits.shape[1]
    size = width // heads
    share = w_query.shape[1]
    half = share // 2

    x0 = lax.dynamic_index_in_dim(tokens, section, 0, keepdims=False)
    seg = windows(lax.dynamic_index_in_dim(segments, section, 0, keepdims=False))
    cot = lax.dynamic_index_in_dim(cotangent, section, 0, keepdims=False)

    gains = jnp.concatenate([gain_attn, gain_ffn], 0).astype(BF)
    gains = jnp.pad(gains.T, ((0, 0), (0, 126)))
    qkv = jnp.concatenate([w_query[0], w_key[0], w_value[0]], 1).astype(BF)
    early = jnp.concatenate([qkv, gains], 1)
    late = jnp.concatenate([w_in[0].astype(BF), w_back[0].T.astype(BF), w_out[0].T.astype(BF)], 1)

    def halves(own):
        other = swap(jnp.where(first, own[half:], own[:half]))
        return jnp.where(first, own[:half], other), jnp.where(first, other, own[half:])

    early0, early1 = halves(early)
    early_all0 = lax.all_gather(early0, AXES, axis=0, tiled=True)
    late0, late1 = halves(late)
    wide = w_in.shape[2]
    rest = jnp.concatenate(
        [late0[:, : 2 * wide], late1[:, : 2 * wide], late0[:, 2 * wide :], late1[:, 2 * wide :], early1], 1
    )
    rest_all = lax.all_gather(rest, AXES, axis=0, tiled=True)

    own_mix = jnp.concatenate([mix_logits, mix_weights], 0)
    other_mix = swap(own_mix)
    mix0 = jnp.where(first, own_mix, other_mix)
    mix1 = jnp.where(first, other_mix, own_mix)

    def gain_rows(columns):
        rows = columns[:, :2].astype(F32).T
        return rows[0:1], rows[1:2]

    tables = [mix_tables(m[0], m[1], size) + (m[1],) for m in (mix0, mix1)]
    at = 4 * wide // width
    weights0 = (gain_rows(early_all0[:, 3 * width :]), early_all0, (0, 1, 2), rest_all, (at, 0, 1))
    end = 4 * wide + 5 * width
    weights1 = (gain_rows(rest_all[:, end:]), rest_all, (at + 2, at + 3, at + 4), rest_all, (at + 1, 2, 3))

    y0, kept0 = layer_forward(x0, seg, weights0, tables[0])
    y1, kept1 = layer_forward(y0, seg, weights1, tables[1])

    dx1, ffn1, qkv1, small1 = layer_backward(cot, seg, kept1, weights1, tables[1])
    dx0, ffn0, qkv0, small0 = layer_backward(dx1, seg, kept0, weights0, tables[0])

    def scatter(pieces):
        packed = jnp.concatenate(pieces, 1)
        return lax.psum_scatter(packed, AXES, scatter_dimension=0, tiled=True)

    sums1 = scatter(list(ffn1) + qkv1)
    sums0 = jnp.concatenate([scatter(list(ffn0)), scatter(qkv0)], 1)
    other = swap(jnp.where(first, sums1, sums0))
    mine = jnp.where(first, jnp.concatenate([sums0, other], 0), jnp.concatenate([other, sums1], 0)).astype(F32)
    grad_in = mine[:, :wide]
    grad_back = mine[:, wide : 2 * wide].T
    grad_out = mine[:, 2 * wide : 2 * wide + width].T
    grads = [mine[:, 2 * wide + i * width : 2 * wide + (i + 1) * width] for i in (1, 2, 3)]

    small = jnp.stack([jnp.concatenate([s.reshape(-1) for s in parts]) for parts in (small0, small1)])
    small = lax.psum(small, AXES)
    small = jnp.where(first, small[0], small[1])
    place = lax.axis_index("dp") * share
    gg_attn = lax.dynamic_slice_in_dim(small, place, share)[None]
    gg_ffn = lax.dynamic_slice_in_dim(small, width + place, share)[None]
    gml = small[2 * width : 2 * width + heads * heads].reshape(1, heads, heads)
    gmw = small[2 * width + heads * heads :].reshape(1, heads, heads)

    def outputs(own0, own1):
        other = swap(jnp.where(first, own1, own0))
        return jnp.where(first, jnp.stack([own0, other]), jnp.stack([other, own1]))[None]

    return (
        outputs(y0, y1),
        outputs(dx0, dx1),
        gg_attn,
        gg_ffn,
        grads[0][None],
        grads[1][None],
        grads[2][None],
        grad_out[None],
        grad_in[None],
        grad_back[None],
        gml,
        gmw,
    )


def solution(mesh):
    rows = P("dp", None, None)
    by_row = P("section", "dp", None)
    by_column = P("section", None, "dp")
    shared = P("section", None, None)
    gain = P("section", "dp")
    return jax.shard_map(
        on_device,
        mesh=mesh,
        in_specs=(
            rows,
            P("dp", None),
            rows,
            gain,
            gain,
            by_row,
            by_row,
            by_row,
            by_column,
            by_row,
            by_column,
            shared,
            shared,
        ),
        out_specs=(
            P("section", "dp", None, None),
            P("section", "dp", None, None),
            gain,
            gain,
            by_row,
            by_row,
            by_row,
            by_column,
            by_row,
            by_column,
            shared,
            shared,
        ),
        check_vma=False,
    )
```

```python
import functools
import math

import jax
import jax.numpy as jnp
from jax import lax
from jax.experimental import pallas as pl
from jax.experimental.pallas import tpu as pltpu
from jax.sharding import PartitionSpec as P

EPS = 1e-06
NEGATIVE = -1e30
LOG2E = math.log2(math.e)
BF = jnp.bfloat16
F32 = jnp.float32
QB = 128
REACH = 512
ROWB = 256
VMEM = 60 * 1024 * 1024

SMEM_SPEC = pl.BlockSpec(memory_space=pltpu.SMEM)


def dot(left, right):
    return jnp.dot(left, right, preferred_element_type=F32)


def dot_t(left, right):
    return lax.dot_general(left, right, (((1,), (1,)), ((), ())), preferred_element_type=F32)


def whole(shape):
    return pl.BlockSpec(shape, lambda *_: (0,) * len(shape))


def column(shape, place):
    return pl.BlockSpec(shape, lambda *_: (0, place))


def params():
    return pltpu.CompilerParams(vmem_limit_bytes=VMEM)


def two_weights(width, low_ref, high_ref):
    return [
        [(0, low_ref, 0, width)],
        [(0, low_ref, width, width // 2), (width // 2, high_ref, 0, width // 2)],
        [(0, high_ref, width // 2, width)],
    ]


def with_weights(count, width, refs, body):
    if count == 3:
        body([[(0, ref, 0, width)] for ref in refs])
        return
    section_ref, own_ref, other_ref = refs
    pl.when(section_ref[0] == 0)(lambda: body(two_weights(width, own_ref, other_ref)))
    pl.when(section_ref[0] != 0)(lambda: body(two_weights(width, other_ref, own_ref)))


def weight_specs(weights, width):
    kind, operands, places = weights
    if kind == 3:
        return [column((width, width), p) for p in places], list(operands)
    section, own, other = operands
    return [SMEM_SPEC, whole(own.shape), whole(other.shape)], [section, own, other]


def project_kernel(count, *refs):
    x_ref, gain_ref = refs[:2]
    normed_ref, q_ref, qt_ref, k_ref, kt_ref, v_ref, vt_ref = refs[-7:]
    width = x_ref.shape[1]
    x = x_ref[...].astype(F32)
    scale = lax.rsqrt(jnp.mean(x * x, axis=-1, keepdims=True) + EPS)
    normed = (x * scale * gain_ref[...]).astype(BF)
    normed_ref[...] = normed

    def body(pieces):
        for own, y_ref, yt_ref in zip(pieces, (q_ref, k_ref, v_ref), (qt_ref, kt_ref, vt_ref)):
            for at, w_ref, start, columns in own:
                y = dot(normed, w_ref[:, start : start + columns])
                y_ref[:, at : at + columns] = y.astype(BF)
                yt_ref[at : at + columns, :] = y.T.astype(BF)

    with_weights(count, width, refs[2:-7], body)


def project(x, gain, weights):
    length, width = x.shape
    rows = pl.BlockSpec((ROWB, width), lambda i: (i, 0))
    cols = pl.BlockSpec((width, ROWB), lambda i: (0, i))
    flat = jax.ShapeDtypeStruct((length, width), BF)
    turned = jax.ShapeDtypeStruct((width, length), BF)
    specs, operands = weight_specs(weights, width)
    return pl.pallas_call(
        functools.partial(project_kernel, weights[0]),
        grid=(length // ROWB,),
        in_specs=[rows, whole((1, width))] + specs,
        out_specs=[rows, rows, cols, rows, cols, rows, cols],
        out_shape=[flat, flat, turned, flat, turned, flat, turned],
        compiler_params=params(),
        cost_estimate=pl.CostEstimate(flops=6 * length * width * width, bytes_accessed=16 * length * width, transcendentals=0),
        name="project",
    )(x, gain, *operands)


def attend_kernel(
    heads, start_ref, mw_ref, ml_ref, qt_ref, k_ref, vt_ref, segc_ref, segr_ref, o_ref, a_ref, mixed_ref, out_acc
):
    block = pl.program_id(0)
    start = start_ref[block]
    size = qt_ref.shape[0] // heads

    def body(blocks):
        span = blocks * QB
        offset = pl.multiple_of(start * QB, QB)
        keys = k_ref[pl.ds(offset, span), :]
        values = vt_ref[:, pl.ds(offset, span)]
        place_k = offset + lax.broadcasted_iota(jnp.int32, (span, QB), 0)
        place_q = block * QB + lax.broadcasted_iota(jnp.int32, (span, QB), 1)
        allowed = (segc_ref[pl.ds(offset, span), :] == segr_ref[...]) & (place_k <= place_q)
        bias = jnp.where(allowed, 0.0, NEGATIVE)
        bias = jnp.concatenate([bias, bias], 1)
        for pair in range(heads // 2):
            parts = []
            for g in (2 * pair, 2 * pair + 1):
                parts.append(
                    jnp.concatenate(
                        [
                            (qt_ref[h * size : (h + 1) * size, :].astype(F32) * ml_ref[h, g]).astype(BF)
                            for h in range(heads)
                        ],
                        0,
                    )
                )
            scores = dot(keys, jnp.concatenate(parts, 1)) + bias
            powers = jnp.exp2(scores - jnp.max(scores, axis=0, keepdims=True))
            soft = (powers * (1.0 / jnp.sum(powers, axis=0, keepdims=True))).astype(BF)
            a_ref[0, pair, 0:span, :] = soft
            mixed = dot(values, soft)
            mixed_ref[2 * pair] = mixed[:, :QB].astype(BF)
            mixed_ref[2 * pair + 1] = mixed[:, QB:].astype(BF)
            for h in range(heads):
                own = slice(h * size, (h + 1) * size)
                term = mixed[own, :QB] * mw_ref[2 * pair, h] + mixed[own, QB:] * mw_ref[2 * pair + 1, h]
                if pair == 0:
                    out_acc[own, :] = term
                else:
                    out_acc[own, :] += term
        o_ref[...] = out_acc[...].T.astype(BF)

    for blocks in range(1, REACH // QB + 2):
        pl.when(block - start + 1 == blocks)(functools.partial(body, blocks))


def attend(start, mw, ml, qt, k, vt, segc, segr):
    width, length = qt.shape
    heads = mw.shape[0]
    steps = length // QB
    most = REACH + QB
    rows = pl.BlockSpec((QB, width), lambda i, s: (i, 0))
    cols = pl.BlockSpec((width, QB), lambda i, s: (0, i))
    return pl.pallas_call(
        functools.partial(attend_kernel, heads),
        grid_spec=pltpu.PrefetchScalarGridSpec(
            num_scalar_prefetch=1,
            grid=(steps,),
            in_specs=[
                SMEM_SPEC,
                SMEM_SPEC,
                cols,
                whole((length, width)),
                whole((width, length)),
                whole((length, 1)),
                pl.BlockSpec((1, QB), lambda i, s: (0, i)),
            ],
            out_specs=[
                rows,
                pl.BlockSpec((1, heads // 2, most, 2 * QB), lambda i, s: (i, 0, 0, 0)),
                pl.BlockSpec((heads, width, QB), lambda i, s: (0, 0, i)),
            ],
            scratch_shapes=[pltpu.VMEM((width, QB), F32)],
        ),
        out_shape=[
            jax.ShapeDtypeStruct((length, width), BF),
            jax.ShapeDtypeStruct((steps, heads // 2, most, 2 * QB), BF),
            jax.ShapeDtypeStruct((heads, width, length), BF),
        ],
        compiler_params=params(),
        cost_estimate=pl.CostEstimate(
            flops=4 * length * most * width * heads, bytes_accessed=40 << 20, transcendentals=length * most * heads
        ),
        name="attend",
    )(start, mw, ml, qt, k, vt, segc, segr)


def attend_back_kernel(
    heads,
    start_ref,
    mw_ref,
    ml_ref,
    mlx_ref,
    mwx_ref,
    q_ref,
    qt_ref,
    do_ref,
    dot_ref,
    kt_ref,
    v_ref,
    a_ref,
    mixed_ref,
    dqkv_ref,
    gml_ref,
    gmw_ref,
    dk_acc,
    dv_acc,
    dqt_acc,
    dz_all,
    a_all,
    q_all,
    do_all,
):
    block = pl.program_id(0)
    start = start_ref[block]
    width = qt_ref.shape[0]
    size = width // heads
    head_rows = [slice(h * size, (h + 1) * size) for h in range(heads)]

    @pl.when(block == 0)
    def _():
        for ref in (dk_acc, dv_acc, gml_ref, gmw_ref):
            ref[...] = jnp.zeros_like(ref)

    def body(blocks):
        span = blocks * QB
        offset = pl.multiple_of(start * QB, QB)
        values = v_ref[pl.ds(offset, span), :]
        keys = kt_ref[:, pl.ds(offset, span)]
        q = q_ref[...].astype(F32)
        do = do_ref[...].astype(F32)
        for pair in range(heads // 2):
            both = (2 * pair, 2 * pair + 1)
            lanes = slice(2 * QB * pair, 2 * QB * (pair + 1))
            parts = []
            for g in both:
                parts.append(
                    jnp.concatenate([(dot_ref[own, :].astype(F32) * mw_ref[g, h]).astype(BF) for h, own in enumerate(head_rows)], 0)
                )
            dsoft = dot(values, jnp.concatenate(parts, 1))
            soft = a_ref[0, pair, 0:span, :]
            wide = soft.astype(F32)
            product = wide * dsoft
            dz = (product - wide * jnp.sum(product, axis=0, keepdims=True)).astype(BF)
            dz_all[0:span, lanes] = dz
            a_all[0:span, lanes] = soft
            for t, g in enumerate(both):
                at = slice((2 * pair + t) * QB, (2 * pair + t + 1) * QB)
                q_all[at, :] = (q * mlx_ref[g : g + 1, :]).astype(BF)
                do_all[at, :] = (do * mwx_ref[g : g + 1, :]).astype(BF)
            side = dot(keys, dz)
            for h, own in enumerate(head_rows):
                terms = (side[own, :QB], side[own, QB:])
                term = terms[0] * ml_ref[h, both[0]] + terms[1] * ml_ref[h, both[1]]
                if pair == 0:
                    dqt_acc[own, :] = term
                else:
                    dqt_acc[own, :] += term
                qth = qt_ref[own, :].astype(F32)
                doth = dot_ref[own, :].astype(F32)
                for g, piece in zip(both, terms):
                    gml_ref[g, h] += jnp.sum((qth * piece).reshape(size // 8, 8, QB), axis=0)
                    gmw_ref[g, h] += jnp.sum((doth * mixed_ref[g, own, :].astype(F32)).reshape(size // 8, 8, QB), axis=0)
        dv_acc[pl.ds(offset, span), :] += dot(a_all[0:span, :], do_all[...])
        dk_acc[pl.ds(offset, span), :] += dot(dz_all[0:span, :], q_all[...])
        dqkv_ref[pl.ds(pl.multiple_of(block * QB, QB), QB), 0:width] = dqt_acc[...].T.astype(BF)

    for blocks in range(1, REACH // QB + 2):
        pl.when(block - start + 1 == blocks)(functools.partial(body, blocks))

    @pl.when(block == pl.num_programs(0) - 1)
    def _():
        dqkv_ref[:, width : 2 * width] = dk_acc[...].astype(BF)
        dqkv_ref[:, 2 * width :] = dv_acc[...].astype(BF)


def attend_back(start, mw, ml, mlx, mwx, q, qt, do, dot_, kt, v, soft, mixed):
    length, width = q.shape
    heads = mw.shape[0]
    steps = length // QB
    most = REACH + QB
    rows = pl.BlockSpec((QB, width), lambda i, s: (i, 0))
    cols = pl.BlockSpec((width, QB), lambda i, s: (0, i))
    sums = jax.ShapeDtypeStruct((heads, heads, 8, QB), F32)
    return pl.pallas_call(
        functools.partial(attend_back_kernel, heads),
        grid_spec=pltpu.PrefetchScalarGridSpec(
            num_scalar_prefetch=1,
            grid=(steps,),
            in_specs=[
                SMEM_SPEC,
                SMEM_SPEC,
                whole((heads, width)),
                whole((heads, width)),
                rows,
                cols,
                rows,
                cols,
                whole((width, length)),
                whole((length, width)),
                pl.BlockSpec((1, heads // 2, most, 2 * QB), lambda i, s: (i, 0, 0, 0)),
                pl.BlockSpec((heads, width, QB), lambda i, s: (0, 0, i)),
            ],
            out_specs=[whole((length, 3 * width)), whole(sums.shape), whole(sums.shape)],
            scratch_shapes=[
                pltpu.VMEM((length, width), F32),
                pltpu.VMEM((length, width), F32),
                pltpu.VMEM((width, QB), F32),
                pltpu.VMEM((most, heads * QB), BF),
                pltpu.VMEM((most, heads * QB), BF),
                pltpu.VMEM((heads * QB, width), BF),
                pltpu.VMEM((heads * QB, width), BF),
            ],
        ),
        out_shape=[jax.ShapeDtypeStruct((length, 3 * width), BF), sums, sums],
        compiler_params=params(),
        cost_estimate=pl.CostEstimate(
            flops=8 * length * most * width * heads, bytes_accessed=50 << 20, transcendentals=0
        ),
        name="attend_back",
    )(start, mw, ml, mlx, mwx, q, qt, do, dot_, kt, v, soft, mixed)


def gelu_both(b):
    root = math.sqrt(2.0 / math.pi)
    square = b * b
    t = jnp.tanh(root * (b + 0.044715 * (square * b)))
    half = 0.5 * (1.0 + t)
    slope = half + 0.5 * b * (1.0 - t * t) * (root * (1.0 + 3.0 * 0.044715 * square))
    return b * half, slope


def feed_kernel(x_ref, o_ref, gain_ref, wo_ref, wi_ref, wb_ref, y_ref, middle_ref, normed_ref, slope_ref, hidden_ref):
    middle = x_ref[...].astype(F32) + dot_t(o_ref[...], wo_ref[...])
    middle_ref[...] = middle
    scale = lax.rsqrt(jnp.mean(middle * middle, axis=-1, keepdims=True) + EPS)
    normed = (middle * scale * gain_ref[...]).astype(BF)
    normed_ref[...] = normed
    wide = wi_ref.shape[1]
    part = wide // 4
    for c in range(4):
        own = slice(c * part, (c + 1) * part)
        hidden, slope = gelu_both(dot(normed, wi_ref[:, own]))
        hidden_ref[:, own] = hidden.astype(BF)
        slope_ref[:, own] = slope.astype(BF)
    y_ref[...] = (middle + dot_t(hidden_ref[...], wb_ref[...])).astype(BF)


def feed(x, o, gain, w, place_out, place_in, place_back):
    length, width = x.shape
    wide = 4 * width
    rows = pl.BlockSpec((ROWB, width), lambda i: (i, 0))
    rows_wide = pl.BlockSpec((ROWB, wide), lambda i: (i, 0))
    flat = jax.ShapeDtypeStruct((length, width), BF)
    flat_wide = jax.ShapeDtypeStruct((length, wide), BF)
    return pl.pallas_call(
        feed_kernel,
        grid=(length // ROWB,),
        in_specs=[
            rows,
            rows,
            whole((1, width)),
            column((width, width), place_out),
            column((width, wide), place_in),
            column((width, wide), place_back),
        ],
        out_specs=[rows, rows, rows, rows_wide, rows_wide],
        out_shape=[flat, jax.ShapeDtypeStruct((length, width), F32), flat, flat_wide, flat_wide],
        compiler_params=params(),
        cost_estimate=pl.CostEstimate(
            flops=18 * length * width * width, bytes_accessed=30 << 20, transcendentals=length * wide
        ),
        name="feed",
    )(x, o, gain, w, w, w)


def norm_back(values, gain, grad):
    scale = lax.rsqrt(jnp.mean(values * values, axis=-1, keepdims=True) + EPS)
    unit = values * scale
    dn = grad * gain
    return scale * (dn - unit * jnp.mean(dn * unit, axis=-1, keepdims=True))


def feed_back_kernel(
    dy_ref, slope_ref, middle_ref, gain_ref, wo_ref, wi_ref, wb_ref, gf_ref, dmiddle_ref, ga_ref, do_ref, dot_ref
):
    dy = dy_ref[...]
    wide = wi_ref.shape[1]
    part = wide // 4
    for c in range(4):
        own = slice(c * part, (c + 1) * part)
        gf_ref[:, own] = (dot(dy, wb_ref[:, own]) * slope_ref[:, own].astype(F32)).astype(BF)
    dnormed = dot_t(gf_ref[...], wi_ref[...])
    dmiddle = dy.astype(F32) + norm_back(middle_ref[...], gain_ref[...], dnormed)
    dmiddle_ref[...] = dmiddle
    ga = dmiddle.astype(BF)
    ga_ref[...] = ga
    do = dot(ga, wo_ref[...])
    do_ref[...] = do.astype(BF)
    dot_ref[...] = do.T.astype(BF)


def feed_back(dy, slope, middle, gain, w, place_out, place_in, place_back):
    length, width = dy.shape
    wide = 4 * width
    rows = pl.BlockSpec((ROWB, width), lambda i: (i, 0))
    rows_wide = pl.BlockSpec((ROWB, wide), lambda i: (i, 0))
    flat = jax.ShapeDtypeStruct((length, width), BF)
    return pl.pallas_call(
        feed_back_kernel,
        grid=(length // ROWB,),
        in_specs=[
            rows,
            rows_wide,
            rows,
            whole((1, width)),
            column((width, width), place_out),
            column((width, wide), place_in),
            column((width, wide), place_back),
        ],
        out_specs=[rows_wide, rows, rows, rows, pl.BlockSpec((width, ROWB), lambda i: (0, i))],
        out_shape=[
            jax.ShapeDtypeStruct((length, wide), BF),
            jax.ShapeDtypeStruct((length, width), F32),
            flat,
            flat,
            jax.ShapeDtypeStruct((width, length), BF),
        ],
        compiler_params=params(),
        cost_estimate=pl.CostEstimate(flops=18 * length * width * width, bytes_accessed=40 << 20, transcendentals=0),
        name="feed_back",
    )(dy, slope, middle, gain, w, w, w)


def project_back_kernel(count, dqkv_ref, x_ref, dmiddle_ref, gain_ref, *refs):
    dx_ref = refs[-1]
    width = x_ref.shape[1]

    def body(pieces):
        dnormed = None
        for i, own in enumerate(pieces):
            for at, w_ref, start, columns in own:
                first = i * width + at
                term = dot_t(dqkv_ref[:, first : first + columns], w_ref[:, start : start + columns])
                dnormed = term if dnormed is None else dnormed + term
        dx_ref[...] = (dmiddle_ref[...] + norm_back(x_ref[...].astype(F32), gain_ref[...], dnormed)).astype(BF)

    with_weights(count, width, refs[:-1], body)


def project_back(dqkv, x, dmiddle, gain, weights):
    length, width = x.shape
    rows = pl.BlockSpec((ROWB, width), lambda i: (i, 0))
    specs, operands = weight_specs(weights, width)
    return pl.pallas_call(
        functools.partial(project_back_kernel, weights[0]),
        grid=(length // ROWB,),
        in_specs=[pl.BlockSpec((ROWB, 3 * width), lambda i: (i, 0)), rows, rows, whole((1, width))] + specs,
        out_specs=rows,
        out_shape=jax.ShapeDtypeStruct((length, width), BF),
        compiler_params=params(),
        cost_estimate=pl.CostEstimate(flops=6 * length * width * width, bytes_accessed=18 << 20, transcendentals=0),
        name="project_back",
    )(dqkv, x, dmiddle, gain, *operands)


def weight_grad(left, right):
    return lax.dot_general(left, right, (((0,), (0,)), ((), ())), preferred_element_type=F32)


def mix_tables(mix_logits, mix_weights, size):
    plain = mix_logits * size ** (-0.5)
    return mix_weights, plain * LOG2E, plain, jnp.repeat(plain.T, size, axis=1), jnp.repeat(mix_weights, size, axis=1)


def layer_forward(x, seg, weights, tables):
    gains, w_qkv, w_rest, places = weights
    start, segc, segr = seg
    normed, q, qt, k, kt, v, vt = project(x, gains[0], w_qkv)
    o, soft, mixed = attend(start, tables[0], tables[1], qt, k, vt, segc, segr)
    y, middle, normed_two, slope, hidden = feed(x, o, gains[1], w_rest, *places)
    return y, (x, normed, q, qt, kt, v, o, soft, mixed, middle, normed_two, slope, hidden)


def windows(seg):
    length = seg.shape[0]
    last = seg[QB - 1 :: QB]
    first = seg[::QB]
    start = jnp.sum((last[None, :] < first[:, None]).astype(jnp.int32), axis=1)
    return start, seg[:, None], seg[None, :]


AXES = ("dp", "section")


def swap(x):
    return lax.ppermute(x, "section", [(0, 1), (1, 0)])


def partners(x, mask):
    return lax.ppermute(x, "dp", [(i, i ^ mask) for i in range(lax.axis_size("dp"))])


def bit_groups():
    bits = lax.axis_size("dp").bit_length() - 1
    return [(at, 1 << min(2, bits - at)) for at in range(0, bits, 2)]


def gather_rows(own):
    share, columns = own.shape
    place = lax.axis_index("dp")
    done = own[None]
    for shift, members in reversed(bit_groups()):
        me = (place >> shift) & (members - 1)
        out = jnp.zeros((done.shape[0], members, share, columns), own.dtype)
        for other in range(members):
            piece = done if other == 0 else partners(done, other << shift)
            out = lax.dynamic_update_slice(out, piece[:, None], (0, me ^ other, 0, 0))
        done = out.reshape(-1, share, columns)
    return done.reshape(-1, columns)


def reduce_rows(whole_rows):
    size = lax.axis_size("dp")
    columns = whole_rows.shape[1]
    share = whole_rows.shape[0] // size
    place = lax.axis_index("dp")
    held = whole_rows.reshape(size, share, columns)
    for shift, members in bit_groups():
        me = (place >> shift) & (members - 1)
        held = held.astype(BF).reshape(-1, members, share, columns)
        total = lax.dynamic_index_in_dim(held, me, 1, keepdims=False).astype(F32)
        for other in range(1, members):
            piece = lax.dynamic_index_in_dim(held, me ^ other, 1, keepdims=False)
            total = total + partners(piece, other << shift).astype(F32)
        held = total
    return held.reshape(share, columns)


def sum_everywhere(x):
    for bit in range(lax.axis_size("dp").bit_length() - 1):
        x = x + partners(x, 1 << bit)
    return x + swap(x)


def on_device(
    tokens,
    segments,
    cotangent,
    gain_attn,
    gain_ffn,
    w_query,
    w_key,
    w_value,
    w_out,
    w_in,
    w_back,
    mix_logits,
    mix_weights,
):
    section = lax.axis_index("section")
    first = section == 0
    width = tokens.shape[2]
    heads = mix_logits.shape[1]
    size = width // heads
    share = w_query.shape[1]
    half = share // 2
    wide = w_in.shape[2]
    middle = 3 * width // 2

    x0 = lax.dynamic_index_in_dim(tokens, section, 0, keepdims=False)
    seg = windows(lax.dynamic_index_in_dim(segments, section, 0, keepdims=False))
    cot = lax.dynamic_index_in_dim(cotangent, section, 0, keepdims=False)

    gains = jnp.concatenate([gain_attn, gain_ffn], 0).astype(BF)
    gain_columns = jnp.pad(gains.T, ((0, 0), (0, 126)))
    qkv = jnp.concatenate([w_query[0], w_key[0], w_value[0]], 1).astype(BF)
    low = jnp.concatenate([qkv[:, :middle], gain_columns], 1)
    high = jnp.concatenate([qkv[:, middle:], gain_columns], 1)
    from_first = swap(high)
    own_half = gather_rows(jnp.where(first, low, from_first))
    other_half = swap(own_half)

    late = jnp.concatenate([w_in[0].astype(BF), w_back[0].T.astype(BF), w_out[0].T.astype(BF)], 1)

    def halves(own):
        other = swap(jnp.where(first, own[half:], own[:half]))
        return jnp.where(first, own[:half], other), jnp.where(first, other, own[half:])

    late0, late1 = halves(late)
    early1 = halves(jnp.concatenate([qkv, gain_columns], 1))[1]
    second = lax.all_gather(jnp.concatenate([late0, early1], 1), AXES, axis=0, tiled=True)
    third = lax.all_gather(late1, AXES, axis=0, tiled=True)

    own_mix = jnp.concatenate([mix_logits, mix_weights], 0)
    other_mix = swap(own_mix)
    mix0 = jnp.where(first, own_mix, other_mix)
    mix1 = jnp.where(first, other_mix, own_mix)
    tables = [mix_tables(m[0], m[1], size) for m in (mix0, mix1)]

    def gain_rows(columns):
        rows = columns[:, :2].astype(F32).T
        return rows[0:1], rows[1:2]

    at_out = 2 * wide // width
    end = 2 * wide + 4 * width
    qkv0 = (2, (section.astype(jnp.int32).reshape(1), own_half, other_half), ())
    qkv1 = (3, (second,) * 3, (at_out + 1, at_out + 2, at_out + 3))
    weights0 = (gain_rows(own_half[:, middle:]), qkv0, second, (at_out, 0, 1))
    weights1 = (gain_rows(second[:, end:]), qkv1, third, (at_out, 0, 1))

    y0, kept0 = layer_forward(x0, seg, weights0, tables[0])
    y1, kept1 = layer_forward(y0, seg, weights1, tables[1])

    def back_feed(dy, kept, weights):
        slope, middle_rows = kept[11], kept[9]
        return feed_back(dy, slope, middle_rows, weights[0][1], weights[2], *weights[3])

    def back_attend(do, dot_, kept, table):
        _, _, q, qt, kt, v, _, soft, mixed = kept[:9]
        mix, _, plain, wide_logits, wide_weights = table
        dqkv, gml, gmw = attend_back(
            seg[0], mix, plain, wide_logits, wide_weights, q, qt, do, dot_, kt, v, soft, mixed
        )
        return dqkv, jnp.stack([jnp.sum(gml, axis=(2, 3)).T * size ** (-0.5), jnp.sum(gmw, axis=(2, 3))])

    gf, dmiddle, ga, do, dot_ = back_feed(cot, kept1, weights1)
    grads1 = [weight_grad(cot, kept1[12]), weight_grad(kept1[10], gf), weight_grad(ga, kept1[6])]
    grads1 = [grads1[1], grads1[0], grads1[2]]
    dqkv, mix_sums1 = back_attend(do, dot_, kept1, tables[1])
    grads1.append(weight_grad(kept1[1], dqkv))
    packed1 = jnp.concatenate([g.astype(BF) for g in grads1], 1)
    dx1 = project_back(dqkv, kept1[0], dmiddle, weights1[0][0], qkv1)
    dx1, packed1 = lax.optimization_barrier((dx1, packed1))
    sums1 = lax.psum_scatter(packed1, AXES, scatter_dimension=0, tiled=True)

    def shared_grad(left, right):
        columns = right.shape[1] // 2
        away = lax.dynamic_slice_in_dim(right, (1 - section) * columns, columns, 1)
        here = lax.dynamic_slice_in_dim(right, section * columns, columns, 1)
        arrived = swap(weight_grad(left, away).astype(BF))
        return (weight_grad(left, here) + arrived.astype(F32)).astype(BF)

    gf, dmiddle, ga, do, dot_ = back_feed(dx1, kept0, weights0)
    packed0 = jnp.concatenate(
        [shared_grad(kept0[10], gf), shared_grad(dx1, kept0[12]), shared_grad(ga, kept0[6])], 1
    )
    do, packed0 = lax.optimization_barrier((do, packed0))
    ffn0 = reduce_rows(packed0)
    dqkv, mix_sums0 = back_attend(do, dot_, kept0, tables[0])
    proj0 = reduce_rows(shared_grad(kept0[1], dqkv))
    dx0 = project_back(dqkv, kept0[0], dmiddle, weights0[0][0], qkv0)

    ffn0_other = lax.ppermute(ffn0, "section", [(1, 0)])
    proj0_other = lax.ppermute(proj0, "section", [(1, 0)])
    sums1_other = lax.ppermute(sums1, "section", [(0, 1)])
    sums1 = jnp.concatenate([sums1_other, sums1], 0).astype(F32)
    cuts = (0, wide // 2, wide, wide + width // 2)

    def join(i):
        return jnp.concatenate([ffn0[:, cuts[i] : cuts[i + 1]], ffn0_other[:, cuts[i] : cuts[i + 1]]], 1)

    grad_in = jnp.where(first, join(0), sums1[:, :wide])
    grad_back = jnp.where(first, join(1), sums1[:, wide : 2 * wide])
    grad_out = jnp.where(first, join(2), sums1[:, 2 * wide : 2 * wide + width])
    grad_qkv = jnp.where(first, jnp.concatenate([proj0, proj0_other], 1), sums1[:, 2 * wide + width :])

    def gain_grad(pairs, gain):
        total = sum(jnp.sum(w.astype(BF).astype(F32) * g, axis=1) for w, g in pairs)
        return (total / gain[0].astype(BF).astype(F32))[None]

    parts = [grad_qkv[:, i * width : (i + 1) * width] for i in range(3)]
    gg_attn = gain_grad(list(zip((w_query[0], w_key[0], w_value[0]), parts)), gain_attn)
    gg_ffn = gain_grad([(w_in[0], grad_in)], gain_ffn)

    mix_sums = sum_everywhere(jnp.stack([mix_sums0, mix_sums1]))
    mix_sums = jnp.where(first, mix_sums[0], mix_sums[1])

    def outputs(own0, own1):
        other = swap(jnp.where(first, own1, own0))
        return jnp.where(first, jnp.stack([own0, other]), jnp.stack([other, own1]))[None]

    return (
        outputs(y0, y1),
        outputs(dx0, dx1),
        gg_attn,
        gg_ffn,
        parts[0][None],
        parts[1][None],
        parts[2][None],
        grad_out.T[None],
        grad_in[None],
        grad_back.T[None],
        mix_sums[0][None],
        mix_sums[1][None],
    )


def solution(mesh):
    rows = P("dp", None, None)
    by_row = P("section", "dp", None)
    by_column = P("section", None, "dp")
    shared = P("section", None, None)
    gain = P("section", "dp")
    return jax.shard_map(
        on_device,
        mesh=mesh,
        in_specs=(
            rows,
            P("dp", None),
            rows,
            gain,
            gain,
            by_row,
            by_row,
            by_row,
            by_column,
            by_row,
            by_column,
            shared,
            shared,
        ),
        out_specs=(
            P("section", "dp", None, None),
            P("section", "dp", None, None),
            gain,
            gain,
            by_row,
            by_row,
            by_row,
            by_column,
            by_row,
            by_column,
            shared,
            shared,
        ),
        check_vma=False,
    )
```

```python
import functools
import math

import jax
import jax.numpy as jnp
from jax import lax
from jax.experimental import pallas as pl
from jax.experimental.pallas import tpu as pltpu
from jax.sharding import PartitionSpec as P

EPS = 1e-06
NEGATIVE = -1e30
LOG2E = math.log2(math.e)
BF = jnp.bfloat16
F32 = jnp.float32
QB = 128
REACH = 512
ROWB = 256
VMEM = 60 * 1024 * 1024

SMEM_SPEC = pl.BlockSpec(memory_space=pltpu.SMEM)


def dot(left, right):
    return jnp.dot(left, right, preferred_element_type=F32)


def dot_t(left, right):
    return lax.dot_general(left, right, (((1,), (1,)), ((), ())), preferred_element_type=F32)


def whole(shape):
    return pl.BlockSpec(shape, lambda *_: (0,) * len(shape))


def column(shape, place):
    return pl.BlockSpec(shape, lambda *_: (0, place))


def params():
    return pltpu.CompilerParams(vmem_limit_bytes=VMEM)


def two_weights(width, low_ref, high_ref):
    return [
        [(0, low_ref, 0, width)],
        [(0, low_ref, width, width // 2), (width // 2, high_ref, 0, width // 2)],
        [(0, high_ref, width // 2, width)],
    ]


def with_weights(count, width, refs, body):
    if count == 3:
        body([[(0, ref, 0, width)] for ref in refs])
        return
    section_ref, own_ref, other_ref = refs
    pl.when(section_ref[0] == 0)(lambda: body(two_weights(width, own_ref, other_ref)))
    pl.when(section_ref[0] != 0)(lambda: body(two_weights(width, other_ref, own_ref)))


def weight_specs(weights, width):
    kind, operands, places = weights
    if kind == 3:
        return [column((width, width), p) for p in places], list(operands)
    section, own, other = operands
    return [SMEM_SPEC, whole(own.shape), whole(other.shape)], [section, own, other]


def project_kernel(count, *refs):
    x_ref, gain_ref = refs[:2]
    normed_ref, q_ref, qt_ref, k_ref, kt_ref, v_ref, vt_ref = refs[-7:]
    width = x_ref.shape[1]
    x = x_ref[...].astype(F32)
    scale = lax.rsqrt(jnp.mean(x * x, axis=-1, keepdims=True) + EPS)
    normed = (x * scale * gain_ref[...]).astype(BF)
    normed_ref[...] = normed

    def body(pieces):
        for own, y_ref, yt_ref in zip(pieces, (q_ref, k_ref, v_ref), (qt_ref, kt_ref, vt_ref)):
            for at, w_ref, start, columns in own:
                y = dot(normed, w_ref[:, start : start + columns])
                y_ref[:, at : at + columns] = y.astype(BF)
                yt_ref[at : at + columns, :] = y.T.astype(BF)

    with_weights(count, width, refs[2:-7], body)


def project(x, gain, weights):
    length, width = x.shape
    rows = pl.BlockSpec((ROWB, width), lambda i: (i, 0))
    cols = pl.BlockSpec((width, ROWB), lambda i: (0, i))
    flat = jax.ShapeDtypeStruct((length, width), BF)
    turned = jax.ShapeDtypeStruct((width, length), BF)
    specs, operands = weight_specs(weights, width)
    return pl.pallas_call(
        functools.partial(project_kernel, weights[0]),
        grid=(length // ROWB,),
        in_specs=[rows, whole((1, width))] + specs,
        out_specs=[rows, rows, cols, rows, cols, rows, cols],
        out_shape=[flat, flat, turned, flat, turned, flat, turned],
        compiler_params=params(),
        cost_estimate=pl.CostEstimate(flops=6 * length * width * width, bytes_accessed=16 * length * width, transcendentals=0),
        name="project",
    )(x, gain, *operands)


def attend_kernel(
    heads, start_ref, mw_ref, ml_ref, qt_ref, k_ref, vt_ref, segc_ref, segr_ref, o_ref, a_ref, mixed_ref, out_acc
):
    block = pl.program_id(0)
    start = start_ref[block]
    size = qt_ref.shape[0] // heads

    def body(blocks):
        span = blocks * QB
        offset = pl.multiple_of(start * QB, QB)
        keys = k_ref[pl.ds(offset, span), :]
        values = vt_ref[:, pl.ds(offset, span)]
        place_k = offset + lax.broadcasted_iota(jnp.int32, (span, QB), 0)
        place_q = block * QB + lax.broadcasted_iota(jnp.int32, (span, QB), 1)
        allowed = (segc_ref[pl.ds(offset, span), :] == segr_ref[...]) & (place_k <= place_q)
        bias = jnp.where(allowed, 0.0, NEGATIVE)
        bias = jnp.concatenate([bias, bias], 1)
        for pair in range(heads // 2):
            parts = []
            for g in (2 * pair, 2 * pair + 1):
                parts.append(
                    jnp.concatenate(
                        [
                            (qt_ref[h * size : (h + 1) * size, :].astype(F32) * ml_ref[h, g]).astype(BF)
                            for h in range(heads)
                        ],
                        0,
                    )
                )
            scores = dot(keys, jnp.concatenate(parts, 1)) + bias
            powers = jnp.exp2(scores - jnp.max(scores, axis=0, keepdims=True))
            soft = (powers * (1.0 / jnp.sum(powers, axis=0, keepdims=True))).astype(BF)
            a_ref[0, pair, 0:span, :] = soft
            mixed = dot(values, soft)
            mixed_ref[2 * pair] = mixed[:, :QB].astype(BF)
            mixed_ref[2 * pair + 1] = mixed[:, QB:].astype(BF)
            for h in range(heads):
                own = slice(h * size, (h + 1) * size)
                term = mixed[own, :QB] * mw_ref[2 * pair, h] + mixed[own, QB:] * mw_ref[2 * pair + 1, h]
                if pair == 0:
                    out_acc[own, :] = term
                else:
                    out_acc[own, :] += term
        o_ref[...] = out_acc[...].T.astype(BF)

    for blocks in range(1, REACH // QB + 2):
        pl.when(block - start + 1 == blocks)(functools.partial(body, blocks))


def attend(start, mw, ml, qt, k, vt, segc, segr):
    width, length = qt.shape
    heads = mw.shape[0]
    steps = length // QB
    most = REACH + QB
    rows = pl.BlockSpec((QB, width), lambda i, s: (i, 0))
    cols = pl.BlockSpec((width, QB), lambda i, s: (0, i))
    return pl.pallas_call(
        functools.partial(attend_kernel, heads),
        grid_spec=pltpu.PrefetchScalarGridSpec(
            num_scalar_prefetch=1,
            grid=(steps,),
            in_specs=[
                SMEM_SPEC,
                SMEM_SPEC,
                cols,
                whole((length, width)),
                whole((width, length)),
                whole((length, 1)),
                pl.BlockSpec((1, QB), lambda i, s: (0, i)),
            ],
            out_specs=[
                rows,
                pl.BlockSpec((1, heads // 2, most, 2 * QB), lambda i, s: (i, 0, 0, 0)),
                pl.BlockSpec((heads, width, QB), lambda i, s: (0, 0, i)),
            ],
            scratch_shapes=[pltpu.VMEM((width, QB), F32)],
        ),
        out_shape=[
            jax.ShapeDtypeStruct((length, width), BF),
            jax.ShapeDtypeStruct((steps, heads // 2, most, 2 * QB), BF),
            jax.ShapeDtypeStruct((heads, width, length), BF),
        ],
        compiler_params=params(),
        cost_estimate=pl.CostEstimate(
            flops=4 * length * most * width * heads, bytes_accessed=40 << 20, transcendentals=length * most * heads
        ),
        name="attend",
    )(start, mw, ml, qt, k, vt, segc, segr)


def attend_back_kernel(
    heads,
    start_ref,
    mw_ref,
    ml_ref,
    mlx_ref,
    mwx_ref,
    q_ref,
    qt_ref,
    do_ref,
    dot_ref,
    kt_ref,
    v_ref,
    a_ref,
    mixed_ref,
    dqkv_ref,
    gml_ref,
    gmw_ref,
    dk_acc,
    dv_acc,
    dqt_acc,
    dz_all,
    a_all,
    q_all,
    do_all,
):
    block = pl.program_id(0)
    start = start_ref[block]
    width = qt_ref.shape[0]
    size = width // heads
    head_rows = [slice(h * size, (h + 1) * size) for h in range(heads)]

    @pl.when(block == 0)
    def _():
        for ref in (dk_acc, dv_acc, gml_ref, gmw_ref):
            ref[...] = jnp.zeros_like(ref)

    def body(blocks):
        span = blocks * QB
        offset = pl.multiple_of(start * QB, QB)
        values = v_ref[pl.ds(offset, span), :]
        keys = kt_ref[:, pl.ds(offset, span)]
        q = q_ref[...].astype(F32)
        do = do_ref[...].astype(F32)
        for pair in range(heads // 2):
            both = (2 * pair, 2 * pair + 1)
            lanes = slice(2 * QB * pair, 2 * QB * (pair + 1))
            parts = []
            for g in both:
                parts.append(
                    jnp.concatenate([(dot_ref[own, :].astype(F32) * mw_ref[g, h]).astype(BF) for h, own in enumerate(head_rows)], 0)
                )
            dsoft = dot(values, jnp.concatenate(parts, 1))
            soft = a_ref[0, pair, 0:span, :]
            wide = soft.astype(F32)
            product = wide * dsoft
            dz = (product - wide * jnp.sum(product, axis=0, keepdims=True)).astype(BF)
            dz_all[0:span, lanes] = dz
            a_all[0:span, lanes] = soft
            for t, g in enumerate(both):
                at = slice((2 * pair + t) * QB, (2 * pair + t + 1) * QB)
                q_all[at, :] = (q * mlx_ref[g : g + 1, :]).astype(BF)
                do_all[at, :] = (do * mwx_ref[g : g + 1, :]).astype(BF)
            side = dot(keys, dz)
            for h, own in enumerate(head_rows):
                terms = (side[own, :QB], side[own, QB:])
                term = terms[0] * ml_ref[h, both[0]] + terms[1] * ml_ref[h, both[1]]
                if pair == 0:
                    dqt_acc[own, :] = term
                else:
                    dqt_acc[own, :] += term
                qth = qt_ref[own, :].astype(F32)
                doth = dot_ref[own, :].astype(F32)
                for g, piece in zip(both, terms):
                    gml_ref[g, h] += jnp.sum((qth * piece).reshape(size // 8, 8, QB), axis=0)
                    gmw_ref[g, h] += jnp.sum((doth * mixed_ref[g, own, :].astype(F32)).reshape(size // 8, 8, QB), axis=0)
        dv_acc[pl.ds(offset, span), :] += dot(a_all[0:span, :], do_all[...])
        dk_acc[pl.ds(offset, span), :] += dot(dz_all[0:span, :], q_all[...])
        dqkv_ref[pl.ds(pl.multiple_of(block * QB, QB), QB), 0:width] = dqt_acc[...].T.astype(BF)

    for blocks in range(1, REACH // QB + 2):
        pl.when(block - start + 1 == blocks)(functools.partial(body, blocks))

    @pl.when(block == pl.num_programs(0) - 1)
    def _():
        dqkv_ref[:, width : 2 * width] = dk_acc[...].astype(BF)
        dqkv_ref[:, 2 * width :] = dv_acc[...].astype(BF)


def attend_back(start, mw, ml, mlx, mwx, q, qt, do, dot_, kt, v, soft, mixed):
    length, width = q.shape
    heads = mw.shape[0]
    steps = length // QB
    most = REACH + QB
    rows = pl.BlockSpec((QB, width), lambda i, s: (i, 0))
    cols = pl.BlockSpec((width, QB), lambda i, s: (0, i))
    sums = jax.ShapeDtypeStruct((heads, heads, 8, QB), F32)
    return pl.pallas_call(
        functools.partial(attend_back_kernel, heads),
        grid_spec=pltpu.PrefetchScalarGridSpec(
            num_scalar_prefetch=1,
            grid=(steps,),
            in_specs=[
                SMEM_SPEC,
                SMEM_SPEC,
                whole((heads, width)),
                whole((heads, width)),
                rows,
                cols,
                rows,
                cols,
                whole((width, length)),
                whole((length, width)),
                pl.BlockSpec((1, heads // 2, most, 2 * QB), lambda i, s: (i, 0, 0, 0)),
                pl.BlockSpec((heads, width, QB), lambda i, s: (0, 0, i)),
            ],
            out_specs=[whole((length, 3 * width)), whole(sums.shape), whole(sums.shape)],
            scratch_shapes=[
                pltpu.VMEM((length, width), F32),
                pltpu.VMEM((length, width), F32),
                pltpu.VMEM((width, QB), F32),
                pltpu.VMEM((most, heads * QB), BF),
                pltpu.VMEM((most, heads * QB), BF),
                pltpu.VMEM((heads * QB, width), BF),
                pltpu.VMEM((heads * QB, width), BF),
            ],
        ),
        out_shape=[jax.ShapeDtypeStruct((length, 3 * width), BF), sums, sums],
        compiler_params=params(),
        cost_estimate=pl.CostEstimate(
            flops=length * most * width * heads, bytes_accessed=8 << 20, transcendentals=0
        ),
        name="attend_back",
    )(start, mw, ml, mlx, mwx, q, qt, do, dot_, kt, v, soft, mixed)


def gelu_both(b):
    root = math.sqrt(2.0 / math.pi)
    square = b * b
    t = jnp.tanh(b * (root + (root * 0.044715) * square))
    half = 0.5 * t + 0.5
    value = b * half
    return value, half + (value * (1.0 - t)) * (root + (3.0 * root * 0.044715) * square)


FFB = 512


def feed_kernel(
    x_ref, o_ref, gain_ref, wo_ref, wi_ref, wb_ref, y_ref, middle_ref, normed_ref, slope_ref, hidden_ref, total
):
    blocks = [slice(r, r + ROWB) for r in range(0, x_ref.shape[0], ROWB)]

    @pl.when(pl.program_id(0) == 0)
    def _():
        for own in blocks:
            middle = x_ref[own, :].astype(F32) + dot_t(o_ref[own, :], wo_ref[...])
            middle_ref[own, :] = middle
            total[own, :] = middle
            scale = lax.rsqrt(jnp.mean(middle * middle, axis=-1, keepdims=True) + EPS)
            normed_ref[own, :] = (middle * scale * gain_ref[...]).astype(BF)

    before = dot(normed_ref[blocks[0], :], wi_ref[...])
    for n, own in enumerate(blocks):
        following = dot(normed_ref[blocks[n + 1], :], wi_ref[...]) if n + 1 < len(blocks) else None
        hidden, slope = gelu_both(before)
        hidden = hidden.astype(BF)
        hidden_ref[own, :] = hidden
        slope_ref[own, :] = slope.astype(BF)
        total[own, :] += dot_t(hidden, wb_ref[...])
        before = following

    @pl.when(pl.program_id(0) == pl.num_programs(0) - 1)
    def _():
        y_ref[...] = total[...].astype(BF)


def feed(x, o, gain, w, place_out, place_in, place_back):
    length, width = x.shape
    wide = 4 * width
    steps = wide // FFB
    chunk = pl.BlockSpec((length, FFB), lambda i: (0, i))
    flat = jax.ShapeDtypeStruct((length, width), BF)
    flat_wide = jax.ShapeDtypeStruct((length, wide), BF)
    all_rows = whole((length, width))
    return pl.pallas_call(
        feed_kernel,
        grid=(steps,),
        in_specs=[
            all_rows,
            all_rows,
            whole((1, width)),
            column((width, width), place_out),
            pl.BlockSpec((width, FFB), lambda i: (0, place_in * steps + i)),
            pl.BlockSpec((width, FFB), lambda i: (0, place_back * steps + i)),
        ],
        out_specs=[all_rows, all_rows, all_rows, chunk, chunk],
        out_shape=[flat, jax.ShapeDtypeStruct((length, width), F32), flat, flat_wide, flat_wide],
        scratch_shapes=[pltpu.VMEM((length, width), F32)],
        compiler_params=params(),
        cost_estimate=pl.CostEstimate(
            flops=18 * length * width * width, bytes_accessed=30 << 20, transcendentals=length * wide
        ),
        name="feed",
    )(x, o, gain, w, w, w)


def norm_back(values, gain, grad):
    scale = lax.rsqrt(jnp.mean(values * values, axis=-1, keepdims=True) + EPS)
    unit = values * scale
    dn = grad * gain
    return scale * (dn - unit * jnp.mean(dn * unit, axis=-1, keepdims=True))


def feed_back_kernel(
    dy_ref, slope_ref, middle_ref, gain_ref, wo_ref, wi_ref, wb_ref, gf_ref, dmiddle_ref, ga_ref, do_ref, dot_ref, total
):
    blocks = [slice(r, r + ROWB) for r in range(0, dy_ref.shape[0], ROWB)]

    @pl.when(pl.program_id(0) == 0)
    def _():
        total[...] = jnp.zeros_like(total)

    before = dot(dy_ref[blocks[0], :], wb_ref[...])
    for n, own in enumerate(blocks):
        following = dot(dy_ref[blocks[n + 1], :], wb_ref[...]) if n + 1 < len(blocks) else None
        gf = (before * slope_ref[own, :].astype(F32)).astype(BF)
        gf_ref[own, :] = gf
        total[own, :] += dot_t(gf, wi_ref[...])
        before = following

    @pl.when(pl.program_id(0) == pl.num_programs(0) - 1)
    def _():
        for own in blocks:
            dmiddle = dy_ref[own, :].astype(F32) + norm_back(middle_ref[own, :], gain_ref[...], total[own, :])
            dmiddle_ref[own, :] = dmiddle
            ga = dmiddle.astype(BF)
            ga_ref[own, :] = ga
            do = dot(ga, wo_ref[...])
            do_ref[own, :] = do.astype(BF)
            dot_ref[:, own] = do.T.astype(BF)


def feed_back(dy, slope, middle, gain, w, place_out, place_in, place_back):
    length, width = dy.shape
    wide = 4 * width
    steps = wide // FFB
    chunk = pl.BlockSpec((length, FFB), lambda i: (0, i))
    all_rows = whole((length, width))
    flat = jax.ShapeDtypeStruct((length, width), BF)
    return pl.pallas_call(
        feed_back_kernel,
        grid=(steps,),
        in_specs=[
            all_rows,
            chunk,
            all_rows,
            whole((1, width)),
            column((width, width), place_out),
            pl.BlockSpec((width, FFB), lambda i: (0, place_in * steps + i)),
            pl.BlockSpec((width, FFB), lambda i: (0, place_back * steps + i)),
        ],
        out_specs=[chunk, all_rows, all_rows, all_rows, whole((width, length))],
        out_shape=[
            jax.ShapeDtypeStruct((length, wide), BF),
            jax.ShapeDtypeStruct((length, width), F32),
            flat,
            flat,
            jax.ShapeDtypeStruct((width, length), BF),
        ],
        scratch_shapes=[pltpu.VMEM((length, width), F32)],
        compiler_params=params(),
        cost_estimate=pl.CostEstimate(flops=18 * length * width * width, bytes_accessed=40 << 20, transcendentals=0),
        name="feed_back",
    )(dy, slope, middle, gain, w, w, w)


def project_back_kernel(count, dqkv_ref, x_ref, dmiddle_ref, gain_ref, *refs):
    dx_ref = refs[-1]
    width = x_ref.shape[1]

    def body(pieces):
        dnormed = None
        for i, own in enumerate(pieces):
            for at, w_ref, start, columns in own:
                first = i * width + at
                term = dot_t(dqkv_ref[:, first : first + columns], w_ref[:, start : start + columns])
                dnormed = term if dnormed is None else dnormed + term
        dx_ref[...] = (dmiddle_ref[...] + norm_back(x_ref[...].astype(F32), gain_ref[...], dnormed)).astype(BF)

    with_weights(count, width, refs[:-1], body)


def project_back(dqkv, x, dmiddle, gain, weights):
    length, width = x.shape
    rows = pl.BlockSpec((ROWB, width), lambda i: (i, 0))
    specs, operands = weight_specs(weights, width)
    return pl.pallas_call(
        functools.partial(project_back_kernel, weights[0]),
        grid=(length // ROWB,),
        in_specs=[pl.BlockSpec((ROWB, 3 * width), lambda i: (i, 0)), rows, rows, whole((1, width))] + specs,
        out_specs=rows,
        out_shape=jax.ShapeDtypeStruct((length, width), BF),
        compiler_params=params(),
        cost_estimate=pl.CostEstimate(flops=6 * length * width * width, bytes_accessed=18 << 20, transcendentals=0),
        name="project_back",
    )(dqkv, x, dmiddle, gain, *operands)


def grads_kernel(jobs, tiled, half_ref, *refs):
    out_ref = refs[-1]
    step = pl.program_id(0)
    first, at = 0, 0
    for n, (columns, tiles) in enumerate(jobs):
        left, right = refs[2 * n], refs[2 * n + 1]

        def body(left=left, right=right, first=first, at=at, columns=columns):
            grad = lax.dot_general(
                left[...], right[...], (((0,), (0,)), ((), ())), preferred_element_type=F32
            ).astype(BF)
            if tiled:
                out_ref[...] = grad
            else:
                place = pl.multiple_of(at + (step - first) * columns, 128)
                out_ref[:, pl.ds(place, columns)] = grad

        pl.when((step >= first) & (step < first + tiles))(body)
        first += tiles
        at += columns * tiles


def packed_grads(jobs, half, name):
    length, width = jobs[0][0].shape
    total = sum(columns * tiles for _, _, columns, tiles in jobs)
    steps = sum(tiles for _, _, _, tiles in jobs)
    tiled = len({columns for _, _, columns, _ in jobs}) == 1
    specs, operands, first = [], [], 0
    for left, right, columns, tiles in jobs:
        specs.append(whole((length, width)))
        specs.append(
            pl.BlockSpec(
                (length, columns),
                lambda i, h, first=first, tiles=tiles: (0, h[0] * tiles + jnp.clip(i - first, 0, tiles - 1)),
            )
        )
        operands += [left, right]
        first += tiles
    out_spec = pl.BlockSpec((width, jobs[0][2]), lambda i, h: (0, i)) if tiled else whole((width, total))
    return pl.pallas_call(
        functools.partial(grads_kernel, [(columns, tiles) for _, _, columns, tiles in jobs], tiled),
        grid_spec=pltpu.PrefetchScalarGridSpec(num_scalar_prefetch=1, grid=(steps,), in_specs=specs, out_specs=out_spec),
        out_shape=jax.ShapeDtypeStruct((width, total), BF),
        compiler_params=params(),
        cost_estimate=pl.CostEstimate(
            flops=2 * length * width * total, bytes_accessed=2 * (length + width) * (total + width), transcendentals=0
        ),
        name=name,
    )(half, *operands)


def mix_tables(mix_logits, mix_weights, size):
    plain = mix_logits * size ** (-0.5)
    return mix_weights, plain * LOG2E, plain, jnp.repeat(plain.T, size, axis=1), jnp.repeat(mix_weights, size, axis=1)


def layer_forward(x, seg, weights, tables):
    gains, w_qkv, w_rest, places = weights
    start, segc, segr = seg
    normed, q, qt, k, kt, v, vt = project(x, gains[0], w_qkv)
    o, soft, mixed = attend(start, tables[0], tables[1], qt, k, vt, segc, segr)
    y, middle, normed_two, slope, hidden = feed(x, o, gains[1], w_rest, *places)
    return y, (x, normed, q, qt, kt, v, o, soft, mixed, middle, normed_two, slope, hidden)


def windows(seg):
    length = seg.shape[0]
    last = seg[QB - 1 :: QB]
    first = seg[::QB]
    start = jnp.sum((last[None, :] < first[:, None]).astype(jnp.int32), axis=1)
    return start, seg[:, None], seg[None, :]


AXES = ("dp", "section")


def swap(x):
    return lax.ppermute(x, "section", [(0, 1), (1, 0)])


def partners(x, mask):
    return lax.ppermute(x, "dp", [(i, i ^ mask) for i in range(lax.axis_size("dp"))])


def bit_groups():
    bits = lax.axis_size("dp").bit_length() - 1
    return [(at, 1 << min(2, bits - at)) for at in range(0, bits, 2)]


def gather_rows(own, meanwhile):
    share, columns = own.shape
    place = lax.axis_index("dp")
    done = own[None]
    for n, (shift, members) in enumerate(reversed(bit_groups())):
        if n == 1:
            done, meanwhile = lax.optimization_barrier((done, meanwhile))
        me = (place >> shift) & (members - 1)
        out = jnp.zeros((done.shape[0], members, share, columns), own.dtype)
        for other in range(members):
            piece = done if other == 0 else partners(done, other << shift)
            out = lax.dynamic_update_slice(out, piece[:, None], (0, me ^ other, 0, 0))
        done = out.reshape(-1, share, columns)
    return done.reshape(-1, columns), meanwhile


def send_parts(held, group):
    shift, members = group
    share, columns = held.shape[1:]
    me = (lax.axis_index("dp") >> shift) & (members - 1)
    held = held.reshape(-1, members, share, columns)
    parts = [lax.dynamic_index_in_dim(held, me ^ other, 1, keepdims=False) for other in range(members)]
    return [parts[0]] + [partners(part.astype(BF), other << shift) for other, part in enumerate(parts) if other]


def add_parts(parts):
    return sum(part.astype(F32) for part in parts)


def shares_of(rows):
    size = lax.axis_size("dp")
    return rows.reshape(size, rows.shape[0] // size, rows.shape[1])


def finish_sum(parts, groups):
    total = add_parts(parts)
    for group in groups:
        total = add_parts(send_parts(total, group))
    return total[0]


def sum_masks(x, masks):
    for mask in masks:
        x = x + partners(x, mask)
    return x


def on_device(
    tokens,
    segments,
    cotangent,
    gain_attn,
    gain_ffn,
    w_query,
    w_key,
    w_value,
    w_out,
    w_in,
    w_back,
    mix_logits,
    mix_weights,
):
    section = lax.axis_index("section")
    first = section == 0
    width = tokens.shape[2]
    heads = mix_logits.shape[1]
    size = width // heads
    share = w_query.shape[1]
    half = share // 2
    wide = w_in.shape[2]
    middle = 3 * width // 2

    x0 = lax.dynamic_index_in_dim(tokens, section, 0, keepdims=False)
    seg = windows(lax.dynamic_index_in_dim(segments, section, 0, keepdims=False))
    cot = lax.dynamic_index_in_dim(cotangent, section, 0, keepdims=False)

    gains = jnp.concatenate([gain_attn, gain_ffn], 0).astype(BF)
    gain_columns = jnp.pad(gains.T, ((0, 0), (0, 126)))
    qkv = jnp.concatenate([w_query[0], w_key[0], w_value[0]], 1).astype(BF)
    low = jnp.concatenate([qkv[:, :middle], gain_columns], 1)
    high = jnp.concatenate([qkv[:, middle:], gain_columns], 1)
    from_first = swap(high)
    own_half, (x0, seg, cot) = gather_rows(jnp.where(first, low, from_first), (x0, seg, cot))
    other_half = swap(own_half)

    late = jnp.concatenate([w_in[0].astype(BF), w_back[0].T.astype(BF), w_out[0].T.astype(BF)], 1)

    def halves(own):
        other = swap(jnp.where(first, own[half:], own[:half]))
        return jnp.where(first, own[:half], other), jnp.where(first, other, own[half:])

    late0, late1 = halves(late)
    early1 = halves(jnp.concatenate([qkv, gain_columns], 1))[1]
    second = lax.all_gather(jnp.concatenate([late0, early1], 1), AXES, axis=0, tiled=True)
    third = lax.all_gather(late1, AXES, axis=0, tiled=True)

    own_mix = jnp.concatenate([mix_logits, mix_weights], 0)
    other_mix = swap(own_mix)
    mix0 = jnp.where(first, own_mix, other_mix)
    mix1 = jnp.where(first, other_mix, own_mix)
    tables = [mix_tables(m[0], m[1], size) for m in (mix0, mix1)]

    def gain_rows(columns):
        rows = columns[:, :2].astype(F32).T
        return rows[0:1], rows[1:2]

    at_out = 2 * wide // width
    end = 2 * wide + 4 * width
    qkv0 = (2, (section.astype(jnp.int32).reshape(1), own_half, other_half), ())
    qkv1 = (3, (second,) * 3, (at_out + 1, at_out + 2, at_out + 3))
    weights0 = (gain_rows(own_half[:, middle:]), qkv0, second, (at_out, 0, 1))
    weights1 = (gain_rows(second[:, end:]), qkv1, third, (at_out, 0, 1))

    y0, kept0 = layer_forward(x0, seg, weights0, tables[0])
    y1, kept1 = layer_forward(y0, seg, weights1, tables[1])

    def back_feed(dy, kept, weights):
        slope, middle_rows = kept[11], kept[9]
        return feed_back(dy, slope, middle_rows, weights[0][1], weights[2], *weights[3])

    def back_attend(do, dot_, kept, table):
        _, _, q, qt, kt, v, _, soft, mixed = kept[:9]
        mix, _, plain, wide_logits, wide_weights = table
        return attend_back(seg[0], mix, plain, wide_logits, wide_weights, q, qt, do, dot_, kt, v, soft, mixed)

    def mix_sums(gml, gmw):
        return jnp.stack([jnp.sum(gml, axis=(2, 3)).T * size ** (-0.5), jnp.sum(gmw, axis=(2, 3))])

    groups = bit_groups()
    masks = [1 << bit for bit in range(lax.axis_size("dp").bit_length() - 1)]
    barrier = lax.optimization_barrier
    here = section.astype(jnp.int32).reshape(1)
    away = 1 - here

    def outputs(own0, own1):
        other = swap(jnp.where(first, own1, own0))
        return jnp.where(first, jnp.stack([own0, other]), jnp.stack([other, own1]))[None]

    def both_halves(jobs, name):
        arrived = swap(packed_grads(jobs, away, name + "_away"))
        return packed_grads(jobs, here, name + "_here"), arrived

    def added(halves):
        return shares_of(halves[0].astype(F32) + halves[1].astype(F32))

    def projection_jobs(normed, dqkv):
        return [(normed, dqkv, dqkv.shape[1] // 6, 3)]

    gf, dmiddle, ga, do, dot_ = back_feed(cot, kept1, weights1)
    packed1 = packed_grads(
        [(kept1[10], gf, width, 4), (cot, kept1[12], width, 4), (ga, kept1[6], width, 1)],
        jnp.zeros((1,), jnp.int32),
        "grads_feed",
    )
    do, packed1 = barrier((do, packed1))
    sums1 = lax.psum_scatter(packed1, AXES, scatter_dimension=0, tiled=True)
    dqkv, gml1, gmw1 = back_attend(do, dot_, kept1, tables[1])
    halves = both_halves(projection_jobs(kept1[1], dqkv), "grads_project")
    dx1 = project_back(dqkv, kept1[0], dmiddle, weights1[0][0], qkv1)
    dx1, halves = barrier((dx1, halves))
    parts1 = send_parts(added(halves), groups[0])

    fed, parts1 = barrier((back_feed(dx1, kept0, weights0), parts1))
    gf, dmiddle, ga, do, dot_ = fed
    parts1 = send_parts(add_parts(parts1), groups[1])
    halves = both_halves(
        [(kept0[10], gf, width, 2), (dx1, kept0[12], width, 2), (ga, kept0[6], width // 2, 1)], "grads_feed"
    )
    do, halves, parts1 = barrier((do, halves, parts1))
    proj1 = finish_sum(parts1, groups[2:])
    held = added(halves).astype(BF)
    do, held, proj1 = barrier((do, held, proj1))
    parts0 = send_parts(held, groups[0])
    (dqkv, gml0, gmw0), parts0, sums1, gml1, gmw1 = barrier(
        (back_attend(do, dot_, kept0, tables[0]), parts0, sums1, gml1, gmw1)
    )
    held = add_parts(parts0).astype(BF)
    parts0 = send_parts(held, groups[1])
    gone = packed_grads(projection_jobs(kept0[1], dqkv), away, "grads_project_away")
    dqkv, gone, held = barrier((dqkv, gone, held))
    halves = packed_grads(projection_jobs(kept0[1], dqkv), here, "grads_project_here"), swap(gone)
    held = added(halves).astype(BF)
    dqkv, held, mixes, y0, y1, sums1 = barrier((dqkv, held, (gml0, gmw0, gml1, gmw1), y0, y1, sums1))
    parts = send_parts(held, groups[0])
    ffn0 = finish_sum(parts0, groups[2:])
    dx0 = project_back(dqkv, kept0[0], dmiddle, weights0[0][0], qkv0)
    mixes = jnp.stack([mix_sums(*mixes[:2]), mix_sums(*mixes[2:])])
    mixes = sum_masks(mixes + swap(mixes), masks[:2])
    section_out = outputs(y0, y1)
    dx0, parts, mixes, section_out, ffn0, sums1 = barrier((dx0, parts, mixes, section_out, ffn0, sums1))
    mixes = sum_masks(mixes, masks[2:])
    mixes = jnp.where(first, mixes[0], mixes[1])
    proj0 = finish_sum(parts, groups[1:])

    ffn0_other = lax.ppermute(ffn0, "section", [(1, 0)])
    sums1_other = lax.ppermute(sums1, "section", [(0, 1)])
    proj_other = swap(jnp.where(first, proj1, proj0))
    sums1 = jnp.concatenate([sums1_other, sums1], 0).astype(F32)
    cuts = (0, wide // 2, wide, wide + width // 2)

    def join(i):
        return jnp.concatenate([ffn0[:, cuts[i] : cuts[i + 1]], ffn0_other[:, cuts[i] : cuts[i + 1]]], 1)

    grad_in = jnp.where(first, join(0), sums1[:, :wide])
    grad_back = jnp.where(first, join(1), sums1[:, wide : 2 * wide])
    grad_out = jnp.where(first, join(2), sums1[:, 2 * wide :])
    grad_qkv = jnp.concatenate([jnp.where(first, proj0, proj_other), jnp.where(first, proj_other, proj1)], 1)

    def gain_grad(pairs, gain):
        total = sum(jnp.sum(w.astype(BF).astype(F32) * g, axis=1) for w, g in pairs)
        return (total / gain[0].astype(BF).astype(F32))[None]

    parts = [grad_qkv[:, i * width : (i + 1) * width] for i in range(3)]
    gg_attn = gain_grad(list(zip((w_query[0], w_key[0], w_value[0]), parts)), gain_attn)
    gg_ffn = gain_grad([(w_in[0], grad_in)], gain_ffn)

    return (
        section_out,
        outputs(dx0, dx1),
        gg_attn,
        gg_ffn,
        parts[0][None],
        parts[1][None],
        parts[2][None],
        grad_out.T[None],
        grad_in[None],
        grad_back.T[None],
        mixes[0][None],
        mixes[1][None],
    )


def solution(mesh):
    rows = P("dp", None, None)
    by_row = P("section", "dp", None)
    by_column = P("section", None, "dp")
    shared = P("section", None, None)
    gain = P("section", "dp")
    return jax.shard_map(
        on_device,
        mesh=mesh,
        in_specs=(
            rows,
            P("dp", None),
            rows,
            gain,
            gain,
            by_row,
            by_row,
            by_row,
            by_column,
            by_row,
            by_column,
            shared,
            shared,
        ),
        out_specs=(
            P("section", "dp", None, None),
            P("section", "dp", None, None),
            gain,
            gain,
            by_row,
            by_row,
            by_row,
            by_column,
            by_row,
            by_column,
            shared,
            shared,
        ),
        check_vma=False,
    )
```

```python
import functools
import math

import jax
import jax.numpy as jnp
from jax import lax
from jax.experimental import pallas as pl
from jax.experimental.pallas import tpu as pltpu
from jax.sharding import PartitionSpec as P

EPS = 1e-06
NEGATIVE = -1e30
LOG2E = math.log2(math.e)
BF = jnp.bfloat16
F32 = jnp.float32
QB = 128
REACH = 512
ROWB = 256
VMEM = 60 * 1024 * 1024

SMEM_SPEC = pl.BlockSpec(memory_space=pltpu.SMEM)


def dot(left, right):
    return jnp.dot(left, right, preferred_element_type=F32)


def dot_t(left, right):
    return lax.dot_general(left, right, (((1,), (1,)), ((), ())), preferred_element_type=F32)


def whole(shape):
    return pl.BlockSpec(shape, lambda *_: (0,) * len(shape))


def column(shape, place):
    return pl.BlockSpec(shape, lambda *_: (0, place))


def params():
    return pltpu.CompilerParams(vmem_limit_bytes=VMEM)


def two_weights(width, low_ref, high_ref):
    return [
        [(0, low_ref, 0, width)],
        [(0, low_ref, width, width // 2), (width // 2, high_ref, 0, width // 2)],
        [(0, high_ref, width // 2, width)],
    ]


def with_weights(count, width, refs, body):
    if count == 3:
        body([[(0, ref, 0, width)] for ref in refs])
        return
    section_ref, own_ref, other_ref = refs
    pl.when(section_ref[0] == 0)(lambda: body(two_weights(width, own_ref, other_ref)))
    pl.when(section_ref[0] != 0)(lambda: body(two_weights(width, other_ref, own_ref)))


def weight_specs(weights, width):
    kind, operands, places = weights
    if kind == 3:
        return [column((width, width), p) for p in places], list(operands)
    section, own, other = operands
    return [SMEM_SPEC, whole(own.shape), whole(other.shape)], [section, own, other]


def project_kernel(count, *refs):
    x_ref, gain_ref = refs[:2]
    normed_ref, q_ref, qt_ref, k_ref, kt_ref, v_ref, vt_ref = refs[-7:]
    width = x_ref.shape[1]
    x = x_ref[...].astype(F32)
    scale = lax.rsqrt(jnp.mean(x * x, axis=-1, keepdims=True) + EPS)
    normed = (x * scale * gain_ref[...]).astype(BF)
    normed_ref[...] = normed

    def body(pieces):
        for own, y_ref, yt_ref in zip(pieces, (q_ref, k_ref, v_ref), (qt_ref, kt_ref, vt_ref)):
            for at, w_ref, start, columns in own:
                y = dot(normed, w_ref[:, start : start + columns])
                y_ref[:, at : at + columns] = y.astype(BF)
                yt_ref[at : at + columns, :] = y.T.astype(BF)

    with_weights(count, width, refs[2:-7], body)


def project(x, gain, weights):
    length, width = x.shape
    rows = pl.BlockSpec((ROWB, width), lambda i: (i, 0))
    cols = pl.BlockSpec((width, ROWB), lambda i: (0, i))
    flat = jax.ShapeDtypeStruct((length, width), BF)
    turned = jax.ShapeDtypeStruct((width, length), BF)
    specs, operands = weight_specs(weights, width)
    return pl.pallas_call(
        functools.partial(project_kernel, weights[0]),
        grid=(length // ROWB,),
        in_specs=[rows, whole((1, width))] + specs,
        out_specs=[rows, rows, cols, rows, cols, rows, cols],
        out_shape=[flat, flat, turned, flat, turned, flat, turned],
        compiler_params=params(),
        cost_estimate=pl.CostEstimate(flops=6 * length * width * width, bytes_accessed=16 * length * width, transcendentals=0),
        name="project",
    )(x, gain, *operands)


def attend_kernel(
    heads, start_ref, mw_ref, ml_ref, qt_ref, k_ref, vt_ref, segc_ref, segr_ref, o_ref, a_ref, mixed_ref, out_acc
):
    block = pl.program_id(0)
    start = start_ref[block]
    size = qt_ref.shape[0] // heads

    def body(blocks):
        span = blocks * QB
        offset = pl.multiple_of(start * QB, QB)
        keys = k_ref[pl.ds(offset, span), :]
        values = vt_ref[:, pl.ds(offset, span)]
        place_k = offset + lax.broadcasted_iota(jnp.int32, (span, QB), 0)
        place_q = block * QB + lax.broadcasted_iota(jnp.int32, (span, QB), 1)
        allowed = (segc_ref[pl.ds(offset, span), :] == segr_ref[...]) & (place_k <= place_q)
        bias = jnp.where(allowed, 0.0, NEGATIVE)
        bias = jnp.concatenate([bias, bias], 1)
        for pair in range(heads // 2):
            parts = []
            for g in (2 * pair, 2 * pair + 1):
                parts.append(
                    jnp.concatenate(
                        [
                            (qt_ref[h * size : (h + 1) * size, :].astype(F32) * ml_ref[h, g]).astype(BF)
                            for h in range(heads)
                        ],
                        0,
                    )
                )
            scores = dot(keys, jnp.concatenate(parts, 1)) + bias
            powers = jnp.exp2(scores - jnp.max(scores, axis=0, keepdims=True))
            soft = (powers * (1.0 / jnp.sum(powers, axis=0, keepdims=True))).astype(BF)
            a_ref[0, pair, 0:span, :] = soft
            mixed = dot(values, soft)
            mixed_ref[2 * pair] = mixed[:, :QB].astype(BF)
            mixed_ref[2 * pair + 1] = mixed[:, QB:].astype(BF)
            for h in range(heads):
                own = slice(h * size, (h + 1) * size)
                term = mixed[own, :QB] * mw_ref[2 * pair, h] + mixed[own, QB:] * mw_ref[2 * pair + 1, h]
                if pair == 0:
                    out_acc[own, :] = term
                else:
                    out_acc[own, :] += term
        o_ref[...] = out_acc[...].T.astype(BF)

    for blocks in range(1, REACH // QB + 2):
        pl.when(block - start + 1 == blocks)(functools.partial(body, blocks))


def attend(start, mw, ml, qt, k, vt, segc, segr):
    width, length = qt.shape
    heads = mw.shape[0]
    steps = length // QB
    most = REACH + QB
    rows = pl.BlockSpec((QB, width), lambda i, s: (i, 0))
    cols = pl.BlockSpec((width, QB), lambda i, s: (0, i))
    return pl.pallas_call(
        functools.partial(attend_kernel, heads),
        grid_spec=pltpu.PrefetchScalarGridSpec(
            num_scalar_prefetch=1,
            grid=(steps,),
            in_specs=[
                SMEM_SPEC,
                SMEM_SPEC,
                cols,
                whole((length, width)),
                whole((width, length)),
                whole((length, 1)),
                pl.BlockSpec((1, QB), lambda i, s: (0, i)),
            ],
            out_specs=[
                rows,
                pl.BlockSpec((1, heads // 2, most, 2 * QB), lambda i, s: (i, 0, 0, 0)),
                pl.BlockSpec((heads, width, QB), lambda i, s: (0, 0, i)),
            ],
            scratch_shapes=[pltpu.VMEM((width, QB), F32)],
        ),
        out_shape=[
            jax.ShapeDtypeStruct((length, width), BF),
            jax.ShapeDtypeStruct((steps, heads // 2, most, 2 * QB), BF),
            jax.ShapeDtypeStruct((heads, width, length), BF),
        ],
        compiler_params=params(),
        cost_estimate=pl.CostEstimate(
            flops=4 * length * most * width * heads, bytes_accessed=40 << 20, transcendentals=length * most * heads
        ),
        name="attend",
    )(start, mw, ml, qt, k, vt, segc, segr)


def attend_back_kernel(
    heads,
    start_ref,
    mw_ref,
    ml_ref,
    mlx_ref,
    mwx_ref,
    q_ref,
    qt_ref,
    do_ref,
    dot_ref,
    kt_ref,
    v_ref,
    a_ref,
    mixed_ref,
    dqkv_ref,
    sums_ref,
    gml_ref,
    gmw_ref,
    dk_acc,
    dv_acc,
    dqt_acc,
    dz_all,
    a_all,
    q_all,
    do_all,
):
    block = pl.program_id(0)
    start = start_ref[block]
    width = qt_ref.shape[0]
    size = width // heads
    head_rows = [slice(h * size, (h + 1) * size) for h in range(heads)]

    @pl.when(block == 0)
    def _():
        for ref in (dk_acc, dv_acc, gml_ref, gmw_ref):
            ref[...] = jnp.zeros_like(ref)

    def body(blocks):
        span = blocks * QB
        offset = pl.multiple_of(start * QB, QB)
        values = v_ref[pl.ds(offset, span), :]
        keys = kt_ref[:, pl.ds(offset, span)]
        q = q_ref[...].astype(F32)
        do = do_ref[...].astype(F32)
        for pair in range(heads // 2):
            both = (2 * pair, 2 * pair + 1)
            lanes = slice(2 * QB * pair, 2 * QB * (pair + 1))
            parts = []
            for g in both:
                parts.append(
                    jnp.concatenate([(dot_ref[own, :].astype(F32) * mw_ref[g, h]).astype(BF) for h, own in enumerate(head_rows)], 0)
                )
            dsoft = dot(values, jnp.concatenate(parts, 1))
            soft = a_ref[0, pair, 0:span, :]
            wide = soft.astype(F32)
            product = wide * dsoft
            dz = (product - wide * jnp.sum(product, axis=0, keepdims=True)).astype(BF)
            dz_all[0:span, lanes] = dz
            a_all[0:span, lanes] = soft
            for t, g in enumerate(both):
                at = slice((2 * pair + t) * QB, (2 * pair + t + 1) * QB)
                q_all[at, :] = (q * mlx_ref[g : g + 1, :]).astype(BF)
                do_all[at, :] = (do * mwx_ref[g : g + 1, :]).astype(BF)
            side = dot(keys, dz)
            for h, own in enumerate(head_rows):
                terms = (side[own, :QB], side[own, QB:])
                term = terms[0] * ml_ref[h, both[0]] + terms[1] * ml_ref[h, both[1]]
                if pair == 0:
                    dqt_acc[own, :] = term
                else:
                    dqt_acc[own, :] += term
                qth = qt_ref[own, :].astype(F32)
                doth = dot_ref[own, :].astype(F32)
                for g, piece in zip(both, terms):
                    gml_ref[g, h] += jnp.sum((qth * piece).reshape(size // 8, 8, QB), axis=0)
                    gmw_ref[g, h] += jnp.sum((doth * mixed_ref[g, own, :].astype(F32)).reshape(size // 8, 8, QB), axis=0)
        dv_acc[pl.ds(offset, span), :] += dot(a_all[0:span, :], do_all[...])
        dk_acc[pl.ds(offset, span), :] += dot(dz_all[0:span, :], q_all[...])
        dqkv_ref[pl.ds(pl.multiple_of(block * QB, QB), QB), 0:width] = dqt_acc[...].T.astype(BF)

    for blocks in range(1, REACH // QB + 2):
        pl.when(block - start + 1 == blocks)(functools.partial(body, blocks))

    @pl.when(block == pl.num_programs(0) - 1)
    def _():
        dqkv_ref[:, width : 2 * width] = dk_acc[...].astype(BF)
        dqkv_ref[:, 2 * width :] = dv_acc[...].astype(BF)
        for g in range(heads):
            sums_ref[0, g] = jnp.sum(gml_ref[g], axis=1)
            sums_ref[1, g] = jnp.sum(gmw_ref[g], axis=1)


def attend_back(start, mw, ml, mlx, mwx, q, qt, do, dot_, kt, v, soft, mixed):
    length, width = q.shape
    heads = mw.shape[0]
    steps = length // QB
    most = REACH + QB
    rows = pl.BlockSpec((QB, width), lambda i, s: (i, 0))
    cols = pl.BlockSpec((width, QB), lambda i, s: (0, i))
    sums = jax.ShapeDtypeStruct((2, heads, heads, QB), F32)
    return pl.pallas_call(
        functools.partial(attend_back_kernel, heads),
        grid_spec=pltpu.PrefetchScalarGridSpec(
            num_scalar_prefetch=1,
            grid=(steps,),
            in_specs=[
                SMEM_SPEC,
                SMEM_SPEC,
                whole((heads, width)),
                whole((heads, width)),
                rows,
                cols,
                rows,
                cols,
                whole((width, length)),
                whole((length, width)),
                pl.BlockSpec((1, heads // 2, most, 2 * QB), lambda i, s: (i, 0, 0, 0)),
                pl.BlockSpec((heads, width, QB), lambda i, s: (0, 0, i)),
            ],
            out_specs=[whole((length, 3 * width)), whole(sums.shape)],
            scratch_shapes=[
                pltpu.VMEM((heads, heads, 8, QB), F32),
                pltpu.VMEM((heads, heads, 8, QB), F32),
                pltpu.VMEM((length, width), F32),
                pltpu.VMEM((length, width), F32),
                pltpu.VMEM((width, QB), F32),
                pltpu.VMEM((most, heads * QB), BF),
                pltpu.VMEM((most, heads * QB), BF),
                pltpu.VMEM((heads * QB, width), BF),
                pltpu.VMEM((heads * QB, width), BF),
            ],
        ),
        out_shape=[jax.ShapeDtypeStruct((length, 3 * width), BF), sums],
        compiler_params=params(),
        cost_estimate=pl.CostEstimate(
            flops=length * most * width * heads, bytes_accessed=8 << 20, transcendentals=0
        ),
        name="attend_back",
    )(start, mw, ml, mlx, mwx, q, qt, do, dot_, kt, v, soft, mixed)


def gelu_both(b):
    root = math.sqrt(2.0 / math.pi)
    square = b * b
    t = jnp.tanh(b * (root + (root * 0.044715) * square))
    half = 0.5 * t + 0.5
    value = b * half
    return value, half + (value * (1.0 - t)) * (root + (3.0 * root * 0.044715) * square)


FFB = 512


def feed_kernel(
    x_ref, o_ref, gain_ref, wo_ref, wi_ref, wb_ref, y_ref, middle_ref, normed_ref, slope_ref, hidden_ref, total
):
    blocks = [slice(r, r + ROWB) for r in range(0, x_ref.shape[0], ROWB)]

    @pl.when(pl.program_id(0) == 0)
    def _():
        for own in blocks:
            middle = x_ref[own, :].astype(F32) + dot_t(o_ref[own, :], wo_ref[...])
            middle_ref[own, :] = middle
            total[own, :] = middle
            scale = lax.rsqrt(jnp.mean(middle * middle, axis=-1, keepdims=True) + EPS)
            normed_ref[own, :] = (middle * scale * gain_ref[...]).astype(BF)

    before = dot(normed_ref[blocks[0], :], wi_ref[...])
    for n, own in enumerate(blocks):
        following = dot(normed_ref[blocks[n + 1], :], wi_ref[...]) if n + 1 < len(blocks) else None
        hidden, slope = gelu_both(before)
        hidden = hidden.astype(BF)
        hidden_ref[own, :] = hidden
        slope_ref[own, :] = slope.astype(BF)
        total[own, :] += dot_t(hidden, wb_ref[...])
        before = following

    @pl.when(pl.program_id(0) == pl.num_programs(0) - 1)
    def _():
        y_ref[...] = total[...].astype(BF)


def feed(x, o, gain, w, place_out, place_in, place_back):
    length, width = x.shape
    wide = 4 * width
    steps = wide // FFB
    chunk = pl.BlockSpec((length, FFB), lambda i: (0, i))
    flat = jax.ShapeDtypeStruct((length, width), BF)
    flat_wide = jax.ShapeDtypeStruct((length, wide), BF)
    all_rows = whole((length, width))
    return pl.pallas_call(
        feed_kernel,
        grid=(steps,),
        in_specs=[
            all_rows,
            all_rows,
            whole((1, width)),
            column((width, width), place_out),
            pl.BlockSpec((width, FFB), lambda i: (0, place_in * steps + i)),
            pl.BlockSpec((width, FFB), lambda i: (0, place_back * steps + i)),
        ],
        out_specs=[all_rows, all_rows, all_rows, chunk, chunk],
        out_shape=[flat, jax.ShapeDtypeStruct((length, width), F32), flat, flat_wide, flat_wide],
        scratch_shapes=[pltpu.VMEM((length, width), F32)],
        compiler_params=params(),
        cost_estimate=pl.CostEstimate(
            flops=18 * length * width * width, bytes_accessed=30 << 20, transcendentals=length * wide
        ),
        name="feed",
    )(x, o, gain, w, w, w)


def norm_back(values, gain, grad):
    scale = lax.rsqrt(jnp.mean(values * values, axis=-1, keepdims=True) + EPS)
    unit = values * scale
    dn = grad * gain
    return scale * (dn - unit * jnp.mean(dn * unit, axis=-1, keepdims=True))


def feed_back_kernel(
    dy_ref, slope_ref, middle_ref, gain_ref, wo_ref, wi_ref, wb_ref, gf_ref, dmiddle_ref, ga_ref, do_ref, dot_ref, total
):
    blocks = [slice(r, r + ROWB) for r in range(0, dy_ref.shape[0], ROWB)]

    @pl.when(pl.program_id(0) == 0)
    def _():
        total[...] = jnp.zeros_like(total)

    before = dot(dy_ref[blocks[0], :], wb_ref[...])
    for n, own in enumerate(blocks):
        following = dot(dy_ref[blocks[n + 1], :], wb_ref[...]) if n + 1 < len(blocks) else None
        gf = (before * slope_ref[own, :].astype(F32)).astype(BF)
        gf_ref[own, :] = gf
        total[own, :] += dot_t(gf, wi_ref[...])
        before = following

    @pl.when(pl.program_id(0) == pl.num_programs(0) - 1)
    def _():
        for own in blocks:
            dmiddle = dy_ref[own, :].astype(F32) + norm_back(middle_ref[own, :], gain_ref[...], total[own, :])
            dmiddle_ref[own, :] = dmiddle
            ga = dmiddle.astype(BF)
            ga_ref[own, :] = ga
            do = dot(ga, wo_ref[...])
            do_ref[own, :] = do.astype(BF)
            dot_ref[:, own] = do.T.astype(BF)


def feed_back(dy, slope, middle, gain, w, place_out, place_in, place_back):
    length, width = dy.shape
    wide = 4 * width
    steps = wide // FFB
    chunk = pl.BlockSpec((length, FFB), lambda i: (0, i))
    all_rows = whole((length, width))
    flat = jax.ShapeDtypeStruct((length, width), BF)
    return pl.pallas_call(
        feed_back_kernel,
        grid=(steps,),
        in_specs=[
            all_rows,
            chunk,
            all_rows,
            whole((1, width)),
            column((width, width), place_out),
            pl.BlockSpec((width, FFB), lambda i: (0, place_in * steps + i)),
            pl.BlockSpec((width, FFB), lambda i: (0, place_back * steps + i)),
        ],
        out_specs=[chunk, all_rows, all_rows, all_rows, whole((width, length))],
        out_shape=[
            jax.ShapeDtypeStruct((length, wide), BF),
            jax.ShapeDtypeStruct((length, width), F32),
            flat,
            flat,
            jax.ShapeDtypeStruct((width, length), BF),
        ],
        scratch_shapes=[pltpu.VMEM((length, width), F32)],
        compiler_params=params(),
        cost_estimate=pl.CostEstimate(flops=18 * length * width * width, bytes_accessed=40 << 20, transcendentals=0),
        name="feed_back",
    )(dy, slope, middle, gain, w, w, w)


def project_back_kernel(count, dqkv_ref, x_ref, dmiddle_ref, gain_ref, *refs):
    dx_ref = refs[-1]
    width = x_ref.shape[1]

    def body(pieces):
        dnormed = None
        for i, own in enumerate(pieces):
            for at, w_ref, start, columns in own:
                first = i * width + at
                term = dot_t(dqkv_ref[:, first : first + columns], w_ref[:, start : start + columns])
                dnormed = term if dnormed is None else dnormed + term
        dx_ref[...] = (dmiddle_ref[...] + norm_back(x_ref[...].astype(F32), gain_ref[...], dnormed)).astype(BF)

    with_weights(count, width, refs[:-1], body)


def project_back(dqkv, x, dmiddle, gain, weights):
    length, width = x.shape
    rows = pl.BlockSpec((ROWB, width), lambda i: (i, 0))
    specs, operands = weight_specs(weights, width)
    return pl.pallas_call(
        functools.partial(project_back_kernel, weights[0]),
        grid=(length // ROWB,),
        in_specs=[pl.BlockSpec((ROWB, 3 * width), lambda i: (i, 0)), rows, rows, whole((1, width))] + specs,
        out_specs=rows,
        out_shape=jax.ShapeDtypeStruct((length, width), BF),
        compiler_params=params(),
        cost_estimate=pl.CostEstimate(flops=length * width, bytes_accessed=1 << 16, transcendentals=0),
        name="project_back",
    )(dqkv, x, dmiddle, gain, *operands)


def grads_kernel(jobs, tiled, half_ref, *refs):
    out_ref = refs[-1]
    step = pl.program_id(0)
    first, at = 0, 0
    for n, (columns, tiles) in enumerate(jobs):
        left, right = refs[2 * n], refs[2 * n + 1]

        def body(left=left, right=right, first=first, at=at, columns=columns):
            grad = lax.dot_general(
                left[...], right[...], (((0,), (0,)), ((), ())), preferred_element_type=F32
            ).astype(BF)
            if tiled:
                out_ref[...] = grad
            else:
                place = pl.multiple_of(at + (step - first) * columns, 128)
                out_ref[:, pl.ds(place, columns)] = grad

        pl.when((step >= first) & (step < first + tiles))(body)
        first += tiles
        at += columns * tiles


def packed_grads(jobs, half, name):
    length, width = jobs[0][0].shape
    total = sum(columns * tiles for _, _, columns, tiles in jobs)
    steps = sum(tiles for _, _, _, tiles in jobs)
    tiled = len({columns for _, _, columns, _ in jobs}) == 1
    specs, operands, first = [], [], 0
    for left, right, columns, tiles in jobs:
        specs.append(whole((length, width)))
        specs.append(
            pl.BlockSpec(
                (length, columns),
                lambda i, h, first=first, tiles=tiles: (0, h[0] * tiles + jnp.clip(i - first, 0, tiles - 1)),
            )
        )
        operands += [left, right]
        first += tiles
    out_spec = pl.BlockSpec((width, jobs[0][2]), lambda i, h: (0, i)) if tiled else whole((width, total))
    return pl.pallas_call(
        functools.partial(grads_kernel, [(columns, tiles) for _, _, columns, tiles in jobs], tiled),
        grid_spec=pltpu.PrefetchScalarGridSpec(num_scalar_prefetch=1, grid=(steps,), in_specs=specs, out_specs=out_spec),
        out_shape=jax.ShapeDtypeStruct((width, total), BF),
        compiler_params=params(),
        cost_estimate=pl.CostEstimate(
            flops=2 * length * width * total, bytes_accessed=2 * (length + width) * (total + width), transcendentals=0
        ),
        name=name,
    )(half, *operands)


def mix_tables(mix_logits, mix_weights, size):
    plain = mix_logits * size ** (-0.5)
    return mix_weights, plain * LOG2E, plain, jnp.repeat(plain.T, size, axis=1), jnp.repeat(mix_weights, size, axis=1)


def layer_forward(x, seg, weights, tables):
    gains, w_qkv, w_rest, places = weights
    start, segc, segr = seg
    normed, q, qt, k, kt, v, vt = project(x, gains[0], w_qkv)
    o, soft, mixed = attend(start, tables[0], tables[1], qt, k, vt, segc, segr)
    y, middle, normed_two, slope, hidden = feed(x, o, gains[1], w_rest, *places)
    return y, (x, normed, q, qt, kt, v, o, soft, mixed, middle, normed_two, slope, hidden)


def windows(seg):
    length = seg.shape[0]
    last = seg[QB - 1 :: QB]
    first = seg[::QB]
    start = jnp.sum((last[None, :] < first[:, None]).astype(jnp.int32), axis=1)
    return start, seg[:, None], seg[None, :]


AXES = ("dp", "section")


def swap(x):
    return lax.ppermute(x, "section", [(0, 1), (1, 0)])


def partners(x, mask):
    return lax.ppermute(x, "dp", [(i, i ^ mask) for i in range(lax.axis_size("dp"))])


def bit_groups():
    bits = lax.axis_size("dp").bit_length() - 1
    return [(at, 1 << min(2, bits - at)) for at in range(0, bits, 2)]


def gather_rows(own, meanwhile):
    share, columns = own.shape
    place = lax.axis_index("dp")
    done = own[None]
    for n, (shift, members) in enumerate(reversed(bit_groups())):
        if n == 1:
            done, meanwhile = lax.optimization_barrier((done, meanwhile))
        me = (place >> shift) & (members - 1)
        out = jnp.zeros((done.shape[0], members, share, columns), own.dtype)
        for other in range(members):
            piece = done if other == 0 else partners(done, other << shift)
            out = lax.dynamic_update_slice(out, piece[:, None], (0, me ^ other, 0, 0))
        done = out.reshape(-1, share, columns)
    return done.reshape(-1, columns), meanwhile


def send_parts(held, group):
    shift, members = group
    share, columns = held.shape[1:]
    me = (lax.axis_index("dp") >> shift) & (members - 1)
    held = held.reshape(-1, members, share, columns)
    parts = [lax.dynamic_index_in_dim(held, me ^ other, 1, keepdims=False) for other in range(members)]
    return [parts[0]] + [partners(part.astype(BF), other << shift) for other, part in enumerate(parts) if other]


def add_parts(parts):
    return sum(part.astype(F32) for part in parts)


def shares_of(rows):
    size = lax.axis_size("dp")
    return rows.reshape(size, rows.shape[0] // size, rows.shape[1])


def finish_sum(parts, groups):
    total = add_parts(parts)
    for group in groups:
        total = add_parts(send_parts(total, group))
    return total[0]


def sum_masks(x, masks):
    for mask in masks:
        x = x + partners(x, mask)
    return x


def on_device(
    tokens,
    segments,
    cotangent,
    gain_attn,
    gain_ffn,
    w_query,
    w_key,
    w_value,
    w_out,
    w_in,
    w_back,
    mix_logits,
    mix_weights,
):
    section = lax.axis_index("section")
    first = section == 0
    width = tokens.shape[2]
    heads = mix_logits.shape[1]
    size = width // heads
    share = w_query.shape[1]
    half = share // 2
    wide = w_in.shape[2]
    middle = 3 * width // 2

    x0 = lax.dynamic_index_in_dim(tokens, section, 0, keepdims=False)
    seg = windows(lax.dynamic_index_in_dim(segments, section, 0, keepdims=False))
    cot = lax.dynamic_index_in_dim(cotangent, section, 0, keepdims=False)

    gains = jnp.concatenate([gain_attn, gain_ffn], 0).astype(BF)
    gain_columns = jnp.pad(gains.T, ((0, 0), (0, 126)))
    qkv = jnp.concatenate([w_query[0], w_key[0], w_value[0]], 1).astype(BF)
    low = jnp.concatenate([qkv[:, :middle], gain_columns], 1)
    high = jnp.concatenate([qkv[:, middle:], gain_columns], 1)
    from_first = swap(high)
    own_half, (x0, seg, cot) = gather_rows(jnp.where(first, low, from_first), (x0, seg, cot))
    other_half = swap(own_half)

    late = jnp.concatenate([w_in[0].astype(BF), w_back[0].T.astype(BF), w_out[0].T.astype(BF)], 1)

    def halves(own):
        other = swap(jnp.where(first, own[half:], own[:half]))
        return jnp.where(first, own[:half], other), jnp.where(first, other, own[half:])

    late0, late1 = halves(late)
    early1 = halves(jnp.concatenate([qkv, gain_columns], 1))[1]
    second = lax.all_gather(jnp.concatenate([late0, early1], 1), AXES, axis=0, tiled=True)
    third = lax.all_gather(late1, AXES, axis=0, tiled=True)

    own_mix = jnp.concatenate([mix_logits, mix_weights], 0)
    other_mix = swap(own_mix)
    mix0 = jnp.where(first, own_mix, other_mix)
    mix1 = jnp.where(first, other_mix, own_mix)
    tables = [mix_tables(m[0], m[1], size) for m in (mix0, mix1)]

    def gain_rows(columns):
        rows = columns[:, :2].astype(F32).T
        return rows[0:1], rows[1:2]

    at_out = 2 * wide // width
    end = 2 * wide + 4 * width
    qkv0 = (2, (section.astype(jnp.int32).reshape(1), own_half, other_half), ())
    qkv1 = (3, (second,) * 3, (at_out + 1, at_out + 2, at_out + 3))
    weights0 = (gain_rows(own_half[:, middle:]), qkv0, second, (at_out, 0, 1))
    weights1 = (gain_rows(second[:, end:]), qkv1, third, (at_out, 0, 1))

    y0, kept0 = layer_forward(x0, seg, weights0, tables[0])
    y1, kept1 = layer_forward(y0, seg, weights1, tables[1])

    def back_feed(dy, kept, weights):
        slope, middle_rows = kept[11], kept[9]
        return feed_back(dy, slope, middle_rows, weights[0][1], weights[2], *weights[3])

    def back_attend(do, dot_, kept, table):
        _, _, q, qt, kt, v, _, soft, mixed = kept[:9]
        mix, _, plain, wide_logits, wide_weights = table
        return attend_back(seg[0], mix, plain, wide_logits, wide_weights, q, qt, do, dot_, kt, v, soft, mixed)

    groups = bit_groups()
    masks = [1 << bit for bit in range(lax.axis_size("dp").bit_length() - 1)]
    barrier = lax.optimization_barrier
    here = section.astype(jnp.int32).reshape(1)
    away = 1 - here

    def outputs(own0, own1, other0, other1):
        return jnp.where(first, jnp.stack([own0, other0]), jnp.stack([other1, own1]))[None]

    def to_first(x):
        return lax.ppermute(x, "section", [(1, 0)])

    def to_second(x):
        return lax.ppermute(x, "section", [(0, 1)])

    def both_halves(jobs, name):
        arrived = swap(packed_grads(jobs, away, name + "_away"))
        return packed_grads(jobs, here, name + "_here"), arrived

    def added(halves):
        return shares_of(halves[0].astype(F32) + halves[1].astype(F32))

    def projection_jobs(normed, dqkv):
        return [(normed, dqkv, dqkv.shape[1] // 6, 3)]

    gf, dmiddle, ga, do, dot_ = back_feed(cot, kept1, weights1)
    packed1 = packed_grads(
        [(kept1[10], gf, width, 4), (cot, kept1[12], width, 4), (ga, kept1[6], width, 1)],
        jnp.zeros((1,), jnp.int32),
        "grads_feed",
    )
    do, packed1 = barrier((do, packed1))
    sums1 = lax.psum_scatter(packed1, AXES, scatter_dimension=0, tiled=True)
    dqkv, sums_mix1 = back_attend(do, dot_, kept1, tables[1])
    halves = both_halves(projection_jobs(kept1[1], dqkv), "grads_project")
    dx1 = project_back(dqkv, kept1[0], dmiddle, weights1[0][0], qkv1)
    dx1, halves = barrier((dx1, halves))
    parts1 = send_parts(added(halves), groups[0])

    fed, parts1 = barrier((back_feed(dx1, kept0, weights0), parts1))
    gf, dmiddle, ga, do, dot_ = fed
    parts1 = send_parts(add_parts(parts1), groups[1])
    halves = both_halves(
        [(kept0[10], gf, width, 2), (dx1, kept0[12], width, 2), (ga, kept0[6], width // 2, 1)], "grads_feed"
    )
    do, halves, parts1 = barrier((do, halves, parts1))
    proj1 = finish_sum(parts1, groups[2:])
    held = added(halves).astype(BF)
    do, held, proj1 = barrier((do, held, proj1))
    parts0 = send_parts(held, groups[0])
    y_other = to_first(y0), to_second(y1)
    dx1_other = to_second(dx1)
    (dqkv, sums_mix0), parts0[:2], sums1, y_other, dx1_other = barrier(
        (back_attend(do, dot_, kept0, tables[0]), parts0[:2], sums1, y_other, dx1_other)
    )
    mixes = jnp.sum(jnp.stack([sums_mix0, sums_mix1]), axis=4)
    mixes = sum_masks(mixes + swap(mixes), masks[:2])
    dqkv, parts0, mixes = barrier((dqkv, parts0, mixes))
    held = add_parts(parts0).astype(BF)
    parts0 = send_parts(held, groups[1])
    gone = packed_grads(projection_jobs(kept0[1], dqkv), away, "grads_project_away")
    dqkv, gone, held = barrier((dqkv, gone, held))
    halves = packed_grads(projection_jobs(kept0[1], dqkv), here, "grads_project_here"), swap(gone)
    held = added(halves).astype(BF)
    dqkv, held = barrier((dqkv, held))
    parts = send_parts(held, groups[0])
    dx0 = project_back(dqkv, kept0[0], dmiddle, weights0[0][0], qkv0)
    dx0, y0, y1, y_other, mixes, sums1 = barrier((dx0, y0, y1, y_other, mixes, sums1))
    section_out = outputs(y0, y1, *y_other)
    dx0, parts, parts0, section_out, mixes = barrier((dx0, parts, parts0, section_out, mixes))
    held = add_parts(parts).astype(BF)
    dx0, held, parts0, mixes, sums1 = barrier((dx0, held, parts0, mixes, sums1))
    parts = send_parts(held, groups[1])
    parts[:2], dx0, parts0, mixes, sums1 = barrier((parts[:2], dx0, parts0, mixes, sums1))
    dx0_other = to_first(dx0)
    ffn0 = finish_sum(parts0, groups[2:])
    mixes = sum_masks(mixes, masks[2:])
    mixes = jnp.where(first, mixes[0], mixes[1])
    proj0 = finish_sum(parts, groups[2:])

    ffn0_other = lax.ppermute(ffn0, "section", [(1, 0)])
    sums1_other = lax.ppermute(sums1, "section", [(0, 1)])
    proj_other = swap(jnp.where(first, proj1, proj0))
    sums1 = jnp.concatenate([sums1_other, sums1], 0).astype(F32)
    cuts = (0, wide // 2, wide, wide + width // 2)

    def join(i):
        return jnp.concatenate([ffn0[:, cuts[i] : cuts[i + 1]], ffn0_other[:, cuts[i] : cuts[i + 1]]], 1)

    grad_in = jnp.where(first, join(0), sums1[:, :wide])
    grad_back = jnp.where(first, join(1), sums1[:, wide : 2 * wide])
    grad_out = jnp.where(first, join(2), sums1[:, 2 * wide :])
    grad_qkv = jnp.concatenate([jnp.where(first, proj0, proj_other), jnp.where(first, proj_other, proj1)], 1)

    def gain_grad(pairs, gain):
        total = sum(jnp.sum(w.astype(BF).astype(F32) * g, axis=1) for w, g in pairs)
        return (total / gain[0].astype(BF).astype(F32))[None]

    parts = [grad_qkv[:, i * width : (i + 1) * width] for i in range(3)]
    gg_attn = gain_grad(list(zip((w_query[0], w_key[0], w_value[0]), parts)), gain_attn)
    gg_ffn = gain_grad([(w_in[0], grad_in)], gain_ffn)

    return (
        section_out,
        outputs(dx0, dx1, dx0_other, dx1_other),
        gg_attn,
        gg_ffn,
        parts[0][None],
        parts[1][None],
        parts[2][None],
        grad_out.T[None],
        grad_in[None],
        grad_back.T[None],
        mixes[0].T[None] * size ** (-0.5),
        mixes[1][None],
    )


def solution(mesh):
    rows = P("dp", None, None)
    by_row = P("section", "dp", None)
    by_column = P("section", None, "dp")
    shared = P("section", None, None)
    gain = P("section", "dp")
    return jax.shard_map(
        on_device,
        mesh=mesh,
        in_specs=(
            rows,
            P("dp", None),
            rows,
            gain,
            gain,
            by_row,
            by_row,
            by_row,
            by_column,
            by_row,
            by_column,
            shared,
            shared,
        ),
        out_specs=(
            P("section", "dp", None, None),
            P("section", "dp", None, None),
            gain,
            gain,
            by_row,
            by_row,
            by_row,
            by_column,
            by_row,
            by_column,
            shared,
            shared,
        ),
        check_vma=False,
    )
```

```python
import functools
import math

import jax
import jax.numpy as jnp
from jax import lax
from jax.experimental import pallas as pl
from jax.experimental.pallas import tpu as pltpu
from jax.sharding import PartitionSpec as P

EPS = 1e-06
NEGATIVE = -1e30
LOG2E = math.log2(math.e)
BF = jnp.bfloat16
F32 = jnp.float32
QB = 128
REACH = 512
ROWB = 256
VMEM = 60 * 1024 * 1024

SMEM_SPEC = pl.BlockSpec(memory_space=pltpu.SMEM)


def dot(left, right):
    return jnp.dot(left, right, preferred_element_type=F32)


def dot_t(left, right):
    return lax.dot_general(left, right, (((1,), (1,)), ((), ())), preferred_element_type=F32)


def whole(shape):
    return pl.BlockSpec(shape, lambda *_: (0,) * len(shape))


def column(shape, place):
    return pl.BlockSpec(shape, lambda *_: (0, place))


def params():
    return pltpu.CompilerParams(vmem_limit_bytes=VMEM)


def two_weights(width, low_ref, high_ref):
    return [
        [(0, low_ref, 0, width)],
        [(0, low_ref, width, width // 2), (width // 2, high_ref, 0, width // 2)],
        [(0, high_ref, width // 2, width)],
    ]


def with_weights(count, width, refs, body):
    if count == 3:
        body([[(0, ref, 0, width)] for ref in refs])
        return
    section_ref, own_ref, other_ref = refs
    pl.when(section_ref[0] == 0)(lambda: body(two_weights(width, own_ref, other_ref)))
    pl.when(section_ref[0] != 0)(lambda: body(two_weights(width, other_ref, own_ref)))


def weight_specs(weights, width):
    kind, operands, places = weights
    if kind == 3:
        return [column((width, width), p) for p in places], list(operands)
    section, own, other = operands
    return [SMEM_SPEC, whole(own.shape), whole(other.shape)], [section, own, other]


def project_kernel(count, *refs):
    x_ref, gain_ref = refs[:2]
    normed_ref, q_ref, k_ref, v_ref = refs[-4:]
    width = x_ref.shape[1]
    x = x_ref[...].astype(F32)
    scale = lax.rsqrt(jnp.mean(x * x, axis=-1, keepdims=True) + EPS)
    normed = (x * scale * gain_ref[...]).astype(BF)
    normed_ref[...] = normed

    def body(pieces):
        for own, y_ref in zip(pieces, (q_ref, k_ref, v_ref)):
            for at, w_ref, start, columns in own:
                y = dot(normed, w_ref[:, start : start + columns])
                y_ref[:, at : at + columns] = y.astype(BF)

    with_weights(count, width, refs[2:-4], body)


def project(x, gain, weights):
    length, width = x.shape
    rows = pl.BlockSpec((ROWB, width), lambda i: (i, 0))
    flat = jax.ShapeDtypeStruct((length, width), BF)
    specs, operands = weight_specs(weights, width)
    return pl.pallas_call(
        functools.partial(project_kernel, weights[0]),
        grid=(length // ROWB,),
        in_specs=[rows, whole((1, width))] + specs,
        out_specs=[rows] * 4,
        out_shape=[flat] * 4,
        compiler_params=params(),
        cost_estimate=pl.CostEstimate(flops=6 * length * width * width, bytes_accessed=16 * length * width, transcendentals=0),
        name="project",
    )(x, gain, *operands)


GROUP = 6


def dot_l(left, right):
    return lax.dot_general(left, right, (((0,), (0,)), ((), ())), preferred_element_type=F32)


def stacked(rows, scale_ref, first):
    return jnp.concatenate([(rows * scale_ref[g : g + 1, :]).astype(BF) for g in range(first, first + GROUP)], 0)


def attend_kernel(heads, start_ref, mwx_ref, mlx_ref, q_ref, k_ref, v_ref, segc_ref, segr_ref, o_ref, a_ref, mixed_ref, out_acc):
    block = pl.program_id(0)
    start = start_ref[block]

    def body(blocks):
        span = blocks * QB
        offset = pl.multiple_of(start * QB, QB)
        keys = k_ref[pl.ds(offset, span), :]
        values = v_ref[pl.ds(offset, span), :]
        place_k = offset + lax.broadcasted_iota(jnp.int32, (QB, span), 1)
        place_q = block * QB + lax.broadcasted_iota(jnp.int32, (QB, span), 0)
        allowed = (segc_ref[...] == segr_ref[:, pl.ds(offset, span)]) & (place_k <= place_q)
        bias = jnp.where(allowed, 0.0, NEGATIVE)
        q = q_ref[...].astype(F32)

        def score(first):
            return dot_t(stacked(q, mlx_ref, first), keys)

        def finish(first, mixed):
            total = None
            for n in range(GROUP):
                own = mixed[n * QB : (n + 1) * QB, :]
                mixed_ref[first + n] = own.astype(BF)
                term = own * mwx_ref[first + n : first + n + 1, :]
                total = term if total is None else total + term
            if first == 0:
                out_acc[...] = total
            else:
                out_acc[...] += total

        scores = score(0)
        before = None
        for first in range(0, heads, GROUP):
            following = score(first + GROUP) if first + GROUP < heads else None
            masked = scores.reshape(GROUP, QB, span) + bias[None]
            powers = jnp.exp2(masked - jnp.max(masked, axis=-1, keepdims=True))
            soft = (powers * (1.0 / jnp.sum(powers, axis=-1, keepdims=True))).astype(BF).reshape(GROUP * QB, span)
            a_ref[0, first * QB : (first + GROUP) * QB, 0:span] = soft
            mixed = dot(soft, values)
            if before is not None:
                finish(first - GROUP, before)
            before = mixed
            scores = following
        finish(heads - GROUP, before)
        o_ref[...] = out_acc[...].astype(BF)

    for blocks in range(1, REACH // QB + 2):
        pl.when(block - start + 1 == blocks)(functools.partial(body, blocks))


def attend(start, mwx, mlx, q, k, v, segc, segr):
    length, width = q.shape
    heads = mwx.shape[0]
    steps = length // QB
    most = REACH + QB
    rows = pl.BlockSpec((QB, width), lambda i, s: (i, 0))
    return pl.pallas_call(
        functools.partial(attend_kernel, heads),
        grid_spec=pltpu.PrefetchScalarGridSpec(
            num_scalar_prefetch=1,
            grid=(steps,),
            in_specs=[
                whole((heads, width)),
                whole((heads, width)),
                rows,
                whole((length, width)),
                whole((length, width)),
                pl.BlockSpec((QB, 1), lambda i, s: (i, 0)),
                whole((1, length)),
            ],
            out_specs=[
                rows,
                pl.BlockSpec((1, heads * QB, most), lambda i, s: (i, 0, 0)),
                pl.BlockSpec((heads, QB, width), lambda i, s: (0, i, 0)),
            ],
            scratch_shapes=[pltpu.VMEM((QB, width), F32)],
        ),
        out_shape=[
            jax.ShapeDtypeStruct((length, width), BF),
            jax.ShapeDtypeStruct((steps, heads * QB, most), BF),
            jax.ShapeDtypeStruct((heads, length, width), BF),
        ],
        compiler_params=params(),
        cost_estimate=pl.CostEstimate(
            flops=4 * length * most * width * heads, bytes_accessed=40 << 20, transcendentals=length * most * heads
        ),
        name="attend",
    )(start, mwx, mlx, q, k, v, segc, segr)


def attend_back_kernel(
    heads,
    start_ref,
    mlx_ref,
    mwx_ref,
    q_ref,
    do_ref,
    k_ref,
    v_ref,
    a_ref,
    mixed_ref,
    dqkv_ref,
    sums_ref,
    gml_ref,
    gmw_ref,
    dk_acc,
    dv_acc,
    dq_acc,
    dz_all,
    q_all,
    do_all,
):
    block = pl.program_id(0)
    start = start_ref[block]
    width = q_ref.shape[1]

    @pl.when(block == 0)
    def _():
        for ref in (dk_acc, dv_acc, gml_ref, gmw_ref):
            ref[...] = jnp.zeros_like(ref)

    def body(blocks):
        span = blocks * QB
        offset = pl.multiple_of(start * QB, QB)
        values = v_ref[pl.ds(offset, span), :]
        keys = k_ref[pl.ds(offset, span), :]
        q = q_ref[...].astype(F32)
        do = do_ref[...].astype(F32)

        def fold(x):
            return jnp.sum(x.reshape(QB // 8, 8, width), axis=0)

        def dsoft(first):
            part = stacked(do, mwx_ref, first)
            do_all[first * QB : (first + GROUP) * QB, :] = part
            return dot_t(part, values)

        def finish(first, side):
            total = None
            for n in range(GROUP):
                g = first + n
                own = side[n * QB : (n + 1) * QB, :]
                term = own * mlx_ref[g : g + 1, :]
                total = term if total is None else total + term
                gml_ref[g] += fold(q * own)
                gmw_ref[g] += fold(do * mixed_ref[g].astype(F32))
            if first == 0:
                dq_acc[...] = total
            else:
                dq_acc[...] += total

        grads = dsoft(0)
        before = None
        for first in range(0, heads, GROUP):
            rows = slice(first * QB, (first + GROUP) * QB)
            following = dsoft(first + GROUP) if first + GROUP < heads else None
            wide = a_ref[0, rows, 0:span].astype(F32)
            product = wide * grads
            dz = (product - wide * jnp.sum(product, axis=-1, keepdims=True)).astype(BF)
            dz_all[rows, 0:span] = dz
            q_all[rows, :] = stacked(q, mlx_ref, first)
            side = dot(dz, keys)
            if before is not None:
                finish(first - GROUP, before)
            before = side
            grads = following
        dv_acc[pl.ds(offset, span), :] += dot_l(a_ref[0, :, 0:span], do_all[...])
        finish(heads - GROUP, before)
        dk_acc[pl.ds(offset, span), :] += dot_l(dz_all[:, 0:span], q_all[...])
        dqkv_ref[pl.ds(pl.multiple_of(block * QB, QB), QB), 0:width] = dq_acc[...].astype(BF)

    for blocks in range(1, REACH // QB + 2):
        pl.when(block - start + 1 == blocks)(functools.partial(body, blocks))

    @pl.when(block == pl.num_programs(0) - 1)
    def _():
        dqkv_ref[:, width : 2 * width] = dk_acc[...].astype(BF)
        dqkv_ref[:, 2 * width :] = dv_acc[...].astype(BF)
        for g in range(heads):
            sums_ref[0, g : g + 1, :] = jnp.sum(gml_ref[g], axis=0, keepdims=True)
            sums_ref[1, g : g + 1, :] = jnp.sum(gmw_ref[g], axis=0, keepdims=True)


def attend_back(start, mlx, mwx, q, do, k, v, soft, mixed):
    length, width = q.shape
    heads = mlx.shape[0]
    steps = length // QB
    most = REACH + QB
    rows = pl.BlockSpec((QB, width), lambda i, s: (i, 0))
    return pl.pallas_call(
        functools.partial(attend_back_kernel, heads),
        grid_spec=pltpu.PrefetchScalarGridSpec(
            num_scalar_prefetch=1,
            grid=(steps,),
            in_specs=[
                whole((heads, width)),
                whole((heads, width)),
                rows,
                rows,
                whole((length, width)),
                whole((length, width)),
                pl.BlockSpec((1, heads * QB, most), lambda i, s: (i, 0, 0)),
                pl.BlockSpec((heads, QB, width), lambda i, s: (0, i, 0)),
            ],
            out_specs=[whole((length, 3 * width)), whole((2, heads, width))],
            scratch_shapes=[
                pltpu.VMEM((heads, 8, width), F32),
                pltpu.VMEM((heads, 8, width), F32),
                pltpu.VMEM((length, width), F32),
                pltpu.VMEM((length, width), F32),
                pltpu.VMEM((QB, width), F32),
                pltpu.VMEM((heads * QB, most), BF),
                pltpu.VMEM((heads * QB, width), BF),
                pltpu.VMEM((heads * QB, width), BF),
            ],
        ),
        out_shape=[
            jax.ShapeDtypeStruct((length, 3 * width), BF),
            jax.ShapeDtypeStruct((2, heads, width), F32),
        ],
        compiler_params=params(),
        cost_estimate=pl.CostEstimate(
            flops=length * most * width * heads, bytes_accessed=8 << 20, transcendentals=0
        ),
        name="attend_back",
    )(start, mlx, mwx, q, do, k, v, soft, mixed)


def gelu_both(b):
    root = math.sqrt(2.0 / math.pi)
    square = b * b
    t = jnp.tanh(b * (root + (root * 0.044715) * square))
    half = 0.5 * t + 0.5
    value = b * half
    return value, half + (value * (1.0 - t)) * (root + (3.0 * root * 0.044715) * square)


FFB = 512


def feed_kernel(
    x_ref, o_ref, gain_ref, wo_ref, wi_ref, wb_ref, y_ref, middle_ref, normed_ref, slope_ref, hidden_ref, total
):
    blocks = [slice(r, r + ROWB) for r in range(0, x_ref.shape[0], ROWB)]

    @pl.when(pl.program_id(0) == 0)
    def _():
        for own in blocks:
            middle = x_ref[own, :].astype(F32) + dot_t(o_ref[own, :], wo_ref[...])
            middle_ref[own, :] = middle
            total[own, :] = middle
            scale = lax.rsqrt(jnp.mean(middle * middle, axis=-1, keepdims=True) + EPS)
            normed_ref[own, :] = (middle * scale * gain_ref[...]).astype(BF)

    before = dot(normed_ref[blocks[0], :], wi_ref[...])
    for n, own in enumerate(blocks):
        following = dot(normed_ref[blocks[n + 1], :], wi_ref[...]) if n + 1 < len(blocks) else None
        hidden, slope = gelu_both(before)
        hidden = hidden.astype(BF)
        hidden_ref[own, :] = hidden
        slope_ref[own, :] = slope.astype(BF)
        total[own, :] += dot_t(hidden, wb_ref[...])
        before = following

    @pl.when(pl.program_id(0) == pl.num_programs(0) - 1)
    def _():
        y_ref[...] = total[...].astype(BF)


def feed(x, o, gain, w, place_out, place_in, place_back):
    length, width = x.shape
    wide = 4 * width
    steps = wide // FFB
    chunk = pl.BlockSpec((length, FFB), lambda i: (0, i))
    flat = jax.ShapeDtypeStruct((length, width), BF)
    flat_wide = jax.ShapeDtypeStruct((length, wide), BF)
    all_rows = whole((length, width))
    return pl.pallas_call(
        feed_kernel,
        grid=(steps,),
        in_specs=[
            all_rows,
            all_rows,
            whole((1, width)),
            column((width, width), place_out),
            pl.BlockSpec((width, FFB), lambda i: (0, place_in * steps + i)),
            pl.BlockSpec((width, FFB), lambda i: (0, place_back * steps + i)),
        ],
        out_specs=[all_rows, all_rows, all_rows, chunk, chunk],
        out_shape=[flat, jax.ShapeDtypeStruct((length, width), F32), flat, flat_wide, flat_wide],
        scratch_shapes=[pltpu.VMEM((length, width), F32)],
        compiler_params=params(),
        cost_estimate=pl.CostEstimate(
            flops=18 * length * width * width, bytes_accessed=30 << 20, transcendentals=length * wide
        ),
        name="feed",
    )(x, o, gain, w, w, w)


def norm_back(values, gain, grad):
    scale = lax.rsqrt(jnp.mean(values * values, axis=-1, keepdims=True) + EPS)
    unit = values * scale
    dn = grad * gain
    return scale * (dn - unit * jnp.mean(dn * unit, axis=-1, keepdims=True))


def feed_back_kernel(
    dy_ref, slope_ref, middle_ref, gain_ref, wo_ref, wi_ref, wb_ref, gf_ref, dmiddle_ref, ga_ref, do_ref, total
):
    blocks = [slice(r, r + ROWB) for r in range(0, dy_ref.shape[0], ROWB)]

    @pl.when(pl.program_id(0) == 0)
    def _():
        total[...] = jnp.zeros_like(total)

    before = dot(dy_ref[blocks[0], :], wb_ref[...])
    for n, own in enumerate(blocks):
        following = dot(dy_ref[blocks[n + 1], :], wb_ref[...]) if n + 1 < len(blocks) else None
        gf = (before * slope_ref[own, :].astype(F32)).astype(BF)
        gf_ref[own, :] = gf
        total[own, :] += dot_t(gf, wi_ref[...])
        before = following

    @pl.when(pl.program_id(0) == pl.num_programs(0) - 1)
    def _():
        for own in blocks:
            dmiddle = dy_ref[own, :].astype(F32) + norm_back(middle_ref[own, :], gain_ref[...], total[own, :])
            dmiddle_ref[own, :] = dmiddle
            ga = dmiddle.astype(BF)
            ga_ref[own, :] = ga
            do_ref[own, :] = dot(ga, wo_ref[...]).astype(BF)


def feed_back(dy, slope, middle, gain, w, place_out, place_in, place_back):
    length, width = dy.shape
    wide = 4 * width
    steps = wide // FFB
    chunk = pl.BlockSpec((length, FFB), lambda i: (0, i))
    all_rows = whole((length, width))
    flat = jax.ShapeDtypeStruct((length, width), BF)
    return pl.pallas_call(
        feed_back_kernel,
        grid=(steps,),
        in_specs=[
            all_rows,
            chunk,
            all_rows,
            whole((1, width)),
            column((width, width), place_out),
            pl.BlockSpec((width, FFB), lambda i: (0, place_in * steps + i)),
            pl.BlockSpec((width, FFB), lambda i: (0, place_back * steps + i)),
        ],
        out_specs=[chunk, all_rows, all_rows, all_rows],
        out_shape=[
            jax.ShapeDtypeStruct((length, wide), BF),
            jax.ShapeDtypeStruct((length, width), F32),
            flat,
            flat,
        ],
        scratch_shapes=[pltpu.VMEM((length, width), F32)],
        compiler_params=params(),
        cost_estimate=pl.CostEstimate(flops=18 * length * width * width, bytes_accessed=40 << 20, transcendentals=0),
        name="feed_back",
    )(dy, slope, middle, gain, w, w, w)


def project_back_kernel(count, dqkv_ref, x_ref, dmiddle_ref, gain_ref, *refs):
    dx_ref = refs[-1]
    width = x_ref.shape[1]

    def body(pieces):
        dnormed = None
        for i, own in enumerate(pieces):
            for at, w_ref, start, columns in own:
                first = i * width + at
                term = dot_t(dqkv_ref[:, first : first + columns], w_ref[:, start : start + columns])
                dnormed = term if dnormed is None else dnormed + term
        dx_ref[...] = (dmiddle_ref[...] + norm_back(x_ref[...].astype(F32), gain_ref[...], dnormed)).astype(BF)

    with_weights(count, width, refs[:-1], body)


def project_back(dqkv, x, dmiddle, gain, weights):
    length, width = x.shape
    rows = pl.BlockSpec((ROWB, width), lambda i: (i, 0))
    specs, operands = weight_specs(weights, width)
    return pl.pallas_call(
        functools.partial(project_back_kernel, weights[0]),
        grid=(length // ROWB,),
        in_specs=[pl.BlockSpec((ROWB, 3 * width), lambda i: (i, 0)), rows, rows, whole((1, width))] + specs,
        out_specs=rows,
        out_shape=jax.ShapeDtypeStruct((length, width), BF),
        compiler_params=params(),
        cost_estimate=pl.CostEstimate(flops=length * width, bytes_accessed=1 << 16, transcendentals=0),
        name="project_back",
    )(dqkv, x, dmiddle, gain, *operands)


def grads_kernel(jobs, tiled, half_ref, *refs):
    out_ref = refs[-1]
    step = pl.program_id(0)
    first, at = 0, 0
    for n, (columns, tiles) in enumerate(jobs):
        left, right = refs[2 * n], refs[2 * n + 1]

        def body(left=left, right=right, first=first, at=at, columns=columns):
            grad = lax.dot_general(
                left[...], right[...], (((0,), (0,)), ((), ())), preferred_element_type=F32
            ).astype(BF)
            if tiled:
                out_ref[...] = grad
            else:
                place = pl.multiple_of(at + (step - first) * columns, 128)
                out_ref[:, pl.ds(place, columns)] = grad

        pl.when((step >= first) & (step < first + tiles))(body)
        first += tiles
        at += columns * tiles


def packed_grads(jobs, half, name):
    length, width = jobs[0][0].shape
    total = sum(columns * tiles for _, _, columns, tiles in jobs)
    steps = sum(tiles for _, _, _, tiles in jobs)
    tiled = len({columns for _, _, columns, _ in jobs}) == 1
    specs, operands, first = [], [], 0
    for left, right, columns, tiles in jobs:
        specs.append(whole((length, width)))
        specs.append(
            pl.BlockSpec(
                (length, columns),
                lambda i, h, first=first, tiles=tiles: (0, h[0] * tiles + jnp.clip(i - first, 0, tiles - 1)),
            )
        )
        operands += [left, right]
        first += tiles
    out_spec = pl.BlockSpec((width, jobs[0][2]), lambda i, h: (0, i)) if tiled else whole((width, total))
    return pl.pallas_call(
        functools.partial(grads_kernel, [(columns, tiles) for _, _, columns, tiles in jobs], tiled),
        grid_spec=pltpu.PrefetchScalarGridSpec(num_scalar_prefetch=1, grid=(steps,), in_specs=specs, out_specs=out_spec),
        out_shape=jax.ShapeDtypeStruct((width, total), BF),
        compiler_params=params(),
        cost_estimate=pl.CostEstimate(
            flops=2 * length * width * total, bytes_accessed=2 * (length + width) * (total + width), transcendentals=0
        ),
        name=name,
    )(half, *operands)


def mix_tables(mix_logits, mix_weights, size):
    logits = jnp.repeat(mix_logits.T * size ** (-0.5), size, axis=1)
    return logits * LOG2E, logits, jnp.repeat(mix_weights, size, axis=1)


def layer_forward(x, seg, weights, tables):
    gains, w_qkv, w_rest, places = weights
    start, segc, segr = seg
    normed, q, k, v = project(x, gains[0], w_qkv)
    o, soft, mixed = attend(start, tables[2], tables[0], q, k, v, segc, segr)
    y, middle, normed_two, slope, hidden = feed(x, o, gains[1], w_rest, *places)
    return y, (x, normed, q, None, k, v, o, soft, mixed, middle, normed_two, slope, hidden)


def windows(seg):
    length = seg.shape[0]
    last = seg[QB - 1 :: QB]
    first = seg[::QB]
    start = jnp.sum((last[None, :] < first[:, None]).astype(jnp.int32), axis=1)
    return start, seg[:, None], seg[None, :]


AXES = ("dp", "section")


def swap(x):
    return lax.ppermute(x, "section", [(0, 1), (1, 0)])


def partners(x, mask):
    return lax.ppermute(x, "dp", [(i, i ^ mask) for i in range(lax.axis_size("dp"))])


def bit_groups():
    bits = lax.axis_size("dp").bit_length() - 1
    return [(at, 1 << min(2, bits - at)) for at in range(0, bits, 2)]


def gather_rows(own, meanwhile):
    share, columns = own.shape
    place = lax.axis_index("dp")
    done = own[None]
    for n, (shift, members) in enumerate(reversed(bit_groups())):
        if n == 1:
            done, meanwhile = lax.optimization_barrier((done, meanwhile))
        me = (place >> shift) & (members - 1)
        out = jnp.zeros((done.shape[0], members, share, columns), own.dtype)
        for other in range(members):
            piece = done if other == 0 else partners(done, other << shift)
            out = lax.dynamic_update_slice(out, piece[:, None], (0, me ^ other, 0, 0))
        done = out.reshape(-1, share, columns)
    return done.reshape(-1, columns), meanwhile


def send_parts(held, group):
    shift, members = group
    share, columns = held.shape[1:]
    me = (lax.axis_index("dp") >> shift) & (members - 1)
    held = held.reshape(-1, members, share, columns)
    parts = [lax.dynamic_index_in_dim(held, me ^ other, 1, keepdims=False) for other in range(members)]
    return [parts[0]] + [partners(part.astype(BF), other << shift) for other, part in enumerate(parts) if other]


def add_parts(parts):
    return sum(part.astype(F32) for part in parts)


def shares_of(rows):
    size = lax.axis_size("dp")
    return rows.reshape(size, rows.shape[0] // size, rows.shape[1])


def finish_sum(parts, groups):
    total = add_parts(parts)
    for group in groups:
        total = add_parts(send_parts(total, group))
    return total[0]


def sum_masks(x, masks):
    for mask in masks:
        x = x + partners(x, mask)
    return x


def on_device(
    tokens,
    segments,
    cotangent,
    gain_attn,
    gain_ffn,
    w_query,
    w_key,
    w_value,
    w_out,
    w_in,
    w_back,
    mix_logits,
    mix_weights,
):
    section = lax.axis_index("section")
    first = section == 0
    width = tokens.shape[2]
    heads = mix_logits.shape[1]
    size = width // heads
    share = w_query.shape[1]
    half = share // 2
    wide = w_in.shape[2]
    middle = 3 * width // 2

    x0 = lax.dynamic_index_in_dim(tokens, section, 0, keepdims=False)
    seg = windows(lax.dynamic_index_in_dim(segments, section, 0, keepdims=False))
    cot = lax.dynamic_index_in_dim(cotangent, section, 0, keepdims=False)

    gains = jnp.concatenate([gain_attn, gain_ffn], 0).astype(BF)
    gain_columns = jnp.pad(gains.T, ((0, 0), (0, 126)))
    qkv = jnp.concatenate([w_query[0], w_key[0], w_value[0]], 1).astype(BF)
    low = jnp.concatenate([qkv[:, :middle], gain_columns], 1)
    high = jnp.concatenate([qkv[:, middle:], gain_columns], 1)
    from_first = swap(high)
    own_half, (x0, seg, cot) = gather_rows(jnp.where(first, low, from_first), (x0, seg, cot))
    other_half = swap(own_half)

    late = jnp.concatenate([w_in[0].astype(BF), w_back[0].T.astype(BF), w_out[0].T.astype(BF)], 1)

    def halves(own):
        other = swap(jnp.where(first, own[half:], own[:half]))
        return jnp.where(first, own[:half], other), jnp.where(first, other, own[half:])

    late0, late1 = halves(late)
    early1 = halves(jnp.concatenate([qkv, gain_columns], 1))[1]
    second = lax.all_gather(jnp.concatenate([late0, early1], 1), AXES, axis=0, tiled=True)
    third = lax.all_gather(late1, AXES, axis=0, tiled=True)

    own_mix = jnp.concatenate([mix_logits, mix_weights], 0)
    other_mix = swap(own_mix)
    mix0 = jnp.where(first, own_mix, other_mix)
    mix1 = jnp.where(first, other_mix, own_mix)
    tables = [mix_tables(m[0], m[1], size) for m in (mix0, mix1)]

    def gain_rows(columns):
        rows = columns[:, :2].astype(F32).T
        return rows[0:1], rows[1:2]

    at_out = 2 * wide // width
    end = 2 * wide + 4 * width
    qkv0 = (2, (section.astype(jnp.int32).reshape(1), own_half, other_half), ())
    qkv1 = (3, (second,) * 3, (at_out + 1, at_out + 2, at_out + 3))
    weights0 = (gain_rows(own_half[:, middle:]), qkv0, second, (at_out, 0, 1))
    weights1 = (gain_rows(second[:, end:]), qkv1, third, (at_out, 0, 1))

    y0, kept0 = layer_forward(x0, seg, weights0, tables[0])
    y1, kept1 = layer_forward(y0, seg, weights1, tables[1])

    def back_feed(dy, kept, weights):
        slope, middle_rows = kept[11], kept[9]
        return feed_back(dy, slope, middle_rows, weights[0][1], weights[2], *weights[3])

    def back_attend(do, kept, table):
        _, _, q, _, k, v, _, soft, mixed = kept[:9]
        return attend_back(seg[0], table[1], table[2], q, do, k, v, soft, mixed)

    groups = bit_groups()
    masks = [1 << bit for bit in range(lax.axis_size("dp").bit_length() - 1)]
    barrier = lax.optimization_barrier
    here = section.astype(jnp.int32).reshape(1)
    away = 1 - here

    def outputs(own0, own1, other0, other1):
        return jnp.where(first, jnp.stack([own0, other0]), jnp.stack([other1, own1]))[None]

    def to_first(x):
        return lax.ppermute(x, "section", [(1, 0)])

    def to_second(x):
        return lax.ppermute(x, "section", [(0, 1)])

    def both_halves(jobs, name):
        arrived = swap(packed_grads(jobs, away, name + "_away"))
        return packed_grads(jobs, here, name + "_here"), arrived

    def added(halves):
        return shares_of(halves[0].astype(F32) + halves[1].astype(F32))

    def projection_jobs(normed, dqkv):
        return [(normed, dqkv, dqkv.shape[1] // 6, 3)]

    y_other = to_first(y0), to_second(y1)
    (gf, dmiddle, ga, do), y_other = barrier((back_feed(cot, kept1, weights1), y_other))
    packed1 = packed_grads(
        [(kept1[10], gf, width, 4), (cot, kept1[12], width, 4), (ga, kept1[6], width, 1)],
        jnp.zeros((1,), jnp.int32),
        "grads_feed",
    )
    do, packed1 = barrier((do, packed1))
    sums1 = lax.psum_scatter(packed1, AXES, scatter_dimension=0, tiled=True)
    dqkv, sums_mix1 = back_attend(do, kept1, tables[1])
    halves = both_halves(projection_jobs(kept1[1], dqkv), "grads_project")
    dx1 = project_back(dqkv, kept1[0], dmiddle, weights1[0][0], qkv1)
    dx1, halves = barrier((dx1, halves))
    parts1 = send_parts(added(halves), groups[0])

    dx1_other = to_second(dx1)
    fed, parts1, dx1_other = barrier((back_feed(dx1, kept0, weights0), parts1, dx1_other))
    gf, dmiddle, ga, do = fed
    parts1 = send_parts(add_parts(parts1), groups[1])
    halves = both_halves(
        [(kept0[10], gf, width, 2), (dx1, kept0[12], width, 2), (ga, kept0[6], width // 2, 1)], "grads_feed"
    )
    do, halves, parts1 = barrier((do, halves, parts1))
    proj1 = finish_sum(parts1, groups[2:])
    held = added(halves).astype(BF)
    do, held, proj1 = barrier((do, held, proj1))
    parts0 = send_parts(held, groups[0])
    (dqkv, sums_mix0), parts0[:2], sums1 = barrier((back_attend(do, kept0, tables[0]), parts0[:2], sums1))
    mixes = jnp.sum(jnp.stack([sums_mix0, sums_mix1]).reshape(2, 2, heads, heads, size), axis=4)
    mixes = sum_masks(mixes + swap(mixes), masks[:2])
    dqkv, parts0, mixes = barrier((dqkv, parts0, mixes))
    held = add_parts(parts0).astype(BF)
    parts0 = send_parts(held, groups[1])
    gone = packed_grads(projection_jobs(kept0[1], dqkv), away, "grads_project_away")
    dqkv, gone, held = barrier((dqkv, gone, held))
    halves = packed_grads(projection_jobs(kept0[1], dqkv), here, "grads_project_here"), swap(gone)
    held = added(halves).astype(BF)
    dqkv, held = barrier((dqkv, held))
    parts = send_parts(held, groups[0])
    dx0 = project_back(dqkv, kept0[0], dmiddle, weights0[0][0], qkv0)
    dx0, y0, y1, y_other, mixes, sums1 = barrier((dx0, y0, y1, y_other, mixes, sums1))
    section_out = outputs(y0, y1, *y_other)
    dx0, parts, parts0, section_out, mixes = barrier((dx0, parts, parts0, section_out, mixes))
    held = add_parts(parts).astype(BF)
    dx0, held, parts0, mixes, sums1 = barrier((dx0, held, parts0, mixes, sums1))
    parts = send_parts(held, groups[1])
    parts[:2], dx0, parts0, mixes, sums1 = barrier((parts[:2], dx0, parts0, mixes, sums1))
    dx0_other = to_first(dx0)
    ffn0 = finish_sum(parts0, groups[2:])
    mixes = sum_masks(mixes, masks[2:])
    mixes = jnp.where(first, mixes[0], mixes[1])
    proj0 = finish_sum(parts, groups[2:])

    ffn0_other = lax.ppermute(ffn0, "section", [(1, 0)])
    sums1_other = lax.ppermute(sums1, "section", [(0, 1)])
    proj_other = swap(jnp.where(first, proj1, proj0))
    sums1 = jnp.concatenate([sums1_other, sums1], 0).astype(F32)
    cuts = (0, wide // 2, wide, wide + width // 2)

    def join(i):
        return jnp.concatenate([ffn0[:, cuts[i] : cuts[i + 1]], ffn0_other[:, cuts[i] : cuts[i + 1]]], 1)

    grad_in = jnp.where(first, join(0), sums1[:, :wide])
    grad_back = jnp.where(first, join(1), sums1[:, wide : 2 * wide])
    grad_out = jnp.where(first, join(2), sums1[:, 2 * wide :])
    grad_qkv = jnp.concatenate([jnp.where(first, proj0, proj_other), jnp.where(first, proj_other, proj1)], 1)

    def gain_grad(pairs, gain):
        total = sum(jnp.sum(w.astype(BF).astype(F32) * g, axis=1) for w, g in pairs)
        return (total / gain[0].astype(BF).astype(F32))[None]

    parts = [grad_qkv[:, i * width : (i + 1) * width] for i in range(3)]
    gg_attn = gain_grad(list(zip((w_query[0], w_key[0], w_value[0]), parts)), gain_attn)
    gg_ffn = gain_grad([(w_in[0], grad_in)], gain_ffn)

    return (
        section_out,
        outputs(dx0, dx1, dx0_other, dx1_other),
        gg_attn,
        gg_ffn,
        parts[0][None],
        parts[1][None],
        parts[2][None],
        grad_out.T[None],
        grad_in[None],
        grad_back.T[None],
        mixes[0].T[None] * size ** (-0.5),
        mixes[1][None],
    )


def solution(mesh):
    rows = P("dp", None, None)
    by_row = P("section", "dp", None)
    by_column = P("section", None, "dp")
    shared = P("section", None, None)
    gain = P("section", "dp")
    return jax.shard_map(
        on_device,
        mesh=mesh,
        in_specs=(
            rows,
            P("dp", None),
            rows,
            gain,
            gain,
            by_row,
            by_row,
            by_row,
            by_column,
            by_row,
            by_column,
            shared,
            shared,
        ),
        out_specs=(
            P("section", "dp", None, None),
            P("section", "dp", None, None),
            gain,
            gain,
            by_row,
            by_row,
            by_row,
            by_column,
            by_row,
            by_column,
            shared,
            shared,
        ),
        check_vma=False,
    )
```

```python
import functools
import math

import jax
import jax.numpy as jnp
from jax import lax
from jax.experimental import pallas as pl
from jax.experimental.pallas import tpu as pltpu
from jax.sharding import PartitionSpec as P

EPS = 1e-06
NEGATIVE = -1e30
LOG2E = math.log2(math.e)
BF = jnp.bfloat16
F32 = jnp.float32
QB = 128
REACH = 512
ROWB = 256
VMEM = 60 * 1024 * 1024

SMEM_SPEC = pl.BlockSpec(memory_space=pltpu.SMEM)


def dot(left, right):
    return jnp.dot(left, right, preferred_element_type=F32)


def dot_t(left, right):
    return lax.dot_general(left, right, (((1,), (1,)), ((), ())), preferred_element_type=F32)


def whole(shape):
    return pl.BlockSpec(shape, lambda *_: (0,) * len(shape))


def column(shape, place):
    return pl.BlockSpec(shape, lambda *_: (0, place))


def params():
    return pltpu.CompilerParams(vmem_limit_bytes=VMEM)


def two_weights(width, low_ref, high_ref):
    return [
        [(0, low_ref, 0, width)],
        [(0, low_ref, width, width // 2), (width // 2, high_ref, 0, width // 2)],
        [(0, high_ref, width // 2, width)],
    ]


def with_weights(count, width, refs, body):
    if count == 3:
        body([[(0, ref, 0, width)] for ref in refs])
        return
    section_ref, own_ref, other_ref = refs
    pl.when(section_ref[0] == 0)(lambda: body(two_weights(width, own_ref, other_ref)))
    pl.when(section_ref[0] != 0)(lambda: body(two_weights(width, other_ref, own_ref)))


def weight_specs(weights, width):
    kind, operands, places = weights
    if kind == 3:
        return [column((width, width), p) for p in places], list(operands)
    section, own, other = operands
    return [SMEM_SPEC, whole(own.shape), whole(other.shape)], [section, own, other]


def project_kernel(count, *refs):
    x_ref, gain_ref = refs[:2]
    normed_ref, q_ref, k_ref, v_ref = refs[-4:]
    width = x_ref.shape[1]
    x = x_ref[...].astype(F32)
    scale = lax.rsqrt(jnp.mean(x * x, axis=-1, keepdims=True) + EPS)
    normed = (x * scale * gain_ref[...]).astype(BF)
    normed_ref[...] = normed

    def body(pieces):
        for own, y_ref in zip(pieces, (q_ref, k_ref, v_ref)):
            for at, w_ref, start, columns in own:
                y = dot(normed, w_ref[:, start : start + columns])
                y_ref[:, at : at + columns] = y.astype(BF)

    with_weights(count, width, refs[2:-4], body)


def project(x, gain, weights):
    length, width = x.shape
    rows = pl.BlockSpec((ROWB, width), lambda i: (i, 0))
    flat = jax.ShapeDtypeStruct((length, width), BF)
    specs, operands = weight_specs(weights, width)
    return pl.pallas_call(
        functools.partial(project_kernel, weights[0]),
        grid=(length // ROWB,),
        in_specs=[rows, whole((1, width))] + specs,
        out_specs=[rows] * 4,
        out_shape=[flat] * 4,
        compiler_params=params(),
        cost_estimate=pl.CostEstimate(flops=6 * length * width * width, bytes_accessed=16 * length * width, transcendentals=0),
        name="project",
    )(x, gain, *operands)


GROUP = 6


def dot_l(left, right):
    return lax.dot_general(left, right, (((0,), (0,)), ((), ())), preferred_element_type=F32)


def stacked(rows, scale_ref, first):
    return jnp.concatenate([(rows * scale_ref[g : g + 1, :]).astype(BF) for g in range(first, first + GROUP)], 0)


def attend_kernel(heads, start_ref, mwx_ref, mlx_ref, q_ref, k_ref, v_ref, segc_ref, segr_ref, o_ref, a_ref, mixed_ref, out_acc):
    block = pl.program_id(0)
    start = start_ref[block]

    def body(blocks):
        span = blocks * QB
        offset = pl.multiple_of(start * QB, QB)
        keys = k_ref[pl.ds(offset, span), :]
        values = v_ref[pl.ds(offset, span), :]
        place_k = offset + lax.broadcasted_iota(jnp.int32, (QB, span), 1)
        place_q = block * QB + lax.broadcasted_iota(jnp.int32, (QB, span), 0)
        allowed = (segc_ref[...] == segr_ref[:, pl.ds(offset, span)]) & (place_k <= place_q)
        bias = jnp.where(allowed, 0.0, NEGATIVE)
        q = q_ref[...].astype(F32)

        def score(first):
            return dot_t(stacked(q, mlx_ref, first), keys)

        def finish(first, mixed):
            total = None
            for n in range(GROUP):
                own = mixed[n * QB : (n + 1) * QB, :]
                mixed_ref[first + n] = own.astype(BF)
                term = own * mwx_ref[first + n : first + n + 1, :]
                total = term if total is None else total + term
            if first == 0:
                out_acc[...] = total
            else:
                out_acc[...] += total

        scores = score(0)
        before = None
        for first in range(0, heads, GROUP):
            following = score(first + GROUP) if first + GROUP < heads else None
            masked = scores.reshape(GROUP, QB, span) + bias[None]
            powers = jnp.exp2(masked - jnp.max(masked, axis=-1, keepdims=True))
            soft = (powers * (1.0 / jnp.sum(powers, axis=-1, keepdims=True))).astype(BF).reshape(GROUP * QB, span)
            a_ref[0, first * QB : (first + GROUP) * QB, 0:span] = soft
            mixed = dot(soft, values)
            if before is not None:
                finish(first - GROUP, before)
            before = mixed
            scores = following
        finish(heads - GROUP, before)
        o_ref[...] = out_acc[...].astype(BF)

    for blocks in range(1, REACH // QB + 2):
        pl.when(block - start + 1 == blocks)(functools.partial(body, blocks))


def attend(start, mwx, mlx, q, k, v, segc, segr):
    length, width = q.shape
    heads = mwx.shape[0]
    steps = length // QB
    most = REACH + QB
    rows = pl.BlockSpec((QB, width), lambda i, s: (i, 0))
    return pl.pallas_call(
        functools.partial(attend_kernel, heads),
        grid_spec=pltpu.PrefetchScalarGridSpec(
            num_scalar_prefetch=1,
            grid=(steps,),
            in_specs=[
                whole((heads, width)),
                whole((heads, width)),
                rows,
                whole((length, width)),
                whole((length, width)),
                pl.BlockSpec((QB, 1), lambda i, s: (i, 0)),
                whole((1, length)),
            ],
            out_specs=[
                rows,
                pl.BlockSpec((1, heads * QB, most), lambda i, s: (i, 0, 0)),
                pl.BlockSpec((heads, QB, width), lambda i, s: (0, i, 0)),
            ],
            scratch_shapes=[pltpu.VMEM((QB, width), F32)],
        ),
        out_shape=[
            jax.ShapeDtypeStruct((length, width), BF),
            jax.ShapeDtypeStruct((steps, heads * QB, most), BF),
            jax.ShapeDtypeStruct((heads, length, width), BF),
        ],
        compiler_params=params(),
        cost_estimate=pl.CostEstimate(
            flops=4 * length * most * width * heads, bytes_accessed=40 << 20, transcendentals=length * most * heads
        ),
        name="attend",
    )(start, mwx, mlx, q, k, v, segc, segr)


def attend_back_kernel(
    heads,
    start_ref,
    mlx_ref,
    mwx_ref,
    q_ref,
    do_ref,
    k_ref,
    v_ref,
    a_ref,
    mixed_ref,
    dqkv_ref,
    sums_ref,
    gml_ref,
    gmw_ref,
    dk_acc,
    dv_acc,
    dq_acc,
    dz_all,
    q_all,
    do_all,
):
    block = pl.program_id(0)
    start = start_ref[block]
    width = q_ref.shape[1]

    @pl.when(block == 0)
    def _():
        for ref in (dk_acc, dv_acc, gml_ref, gmw_ref):
            ref[...] = jnp.zeros_like(ref)

    def body(blocks):
        span = blocks * QB
        offset = pl.multiple_of(start * QB, QB)
        values = v_ref[pl.ds(offset, span), :]
        keys = k_ref[pl.ds(offset, span), :]
        q = q_ref[...].astype(F32)
        do = do_ref[...].astype(F32)

        def fold(x):
            return jnp.sum(x.reshape(QB // 8, 8, width), axis=0)

        def dsoft(first):
            part = stacked(do, mwx_ref, first)
            do_all[first * QB : (first + GROUP) * QB, :] = part
            return dot_t(part, values)

        def finish(first, side):
            total = None
            for n in range(GROUP):
                g = first + n
                own = side[n * QB : (n + 1) * QB, :]
                term = own * mlx_ref[g : g + 1, :]
                total = term if total is None else total + term
                gml_ref[g] += fold(q * own)
                gmw_ref[g] += fold(do * mixed_ref[g].astype(F32))
            if first == 0:
                dq_acc[...] = total
            else:
                dq_acc[...] += total

        grads = dsoft(0)
        before = None
        for first in range(0, heads, GROUP):
            rows = slice(first * QB, (first + GROUP) * QB)
            following = dsoft(first + GROUP) if first + GROUP < heads else None
            wide = a_ref[0, rows, 0:span].astype(F32)
            product = wide * grads
            dz = (product - wide * jnp.sum(product, axis=-1, keepdims=True)).astype(BF)
            dz_all[rows, 0:span] = dz
            q_all[rows, :] = stacked(q, mlx_ref, first)
            side = dot(dz, keys)
            if before is not None:
                finish(first - GROUP, before)
            before = side
            grads = following
        dv_acc[pl.ds(offset, span), :] += dot_l(a_ref[0, :, 0:span], do_all[...])
        finish(heads - GROUP, before)
        dk_acc[pl.ds(offset, span), :] += dot_l(dz_all[:, 0:span], q_all[...])
        dqkv_ref[pl.ds(pl.multiple_of(block * QB, QB), QB), 0:width] = dq_acc[...].astype(BF)

    for blocks in range(1, REACH // QB + 2):
        pl.when(block - start + 1 == blocks)(functools.partial(body, blocks))

    @pl.when(block == pl.num_programs(0) - 1)
    def _():
        dqkv_ref[:, width : 2 * width] = dk_acc[...].astype(BF)
        dqkv_ref[:, 2 * width :] = dv_acc[...].astype(BF)
        for g in range(heads):
            sums_ref[0, g : g + 1, :] = jnp.sum(gml_ref[g], axis=0, keepdims=True)
            sums_ref[1, g : g + 1, :] = jnp.sum(gmw_ref[g], axis=0, keepdims=True)


def attend_back(start, mlx, mwx, q, do, k, v, soft, mixed):
    length, width = q.shape
    heads = mlx.shape[0]
    steps = length // QB
    most = REACH + QB
    rows = pl.BlockSpec((QB, width), lambda i, s: (i, 0))
    return pl.pallas_call(
        functools.partial(attend_back_kernel, heads),
        grid_spec=pltpu.PrefetchScalarGridSpec(
            num_scalar_prefetch=1,
            grid=(steps,),
            in_specs=[
                whole((heads, width)),
                whole((heads, width)),
                rows,
                rows,
                whole((length, width)),
                whole((length, width)),
                pl.BlockSpec((1, heads * QB, most), lambda i, s: (i, 0, 0)),
                pl.BlockSpec((heads, QB, width), lambda i, s: (0, i, 0)),
            ],
            out_specs=[whole((length, 3 * width)), whole((2, heads, width))],
            scratch_shapes=[
                pltpu.VMEM((heads, 8, width), F32),
                pltpu.VMEM((heads, 8, width), F32),
                pltpu.VMEM((length, width), F32),
                pltpu.VMEM((length, width), F32),
                pltpu.VMEM((QB, width), F32),
                pltpu.VMEM((heads * QB, most), BF),
                pltpu.VMEM((heads * QB, width), BF),
                pltpu.VMEM((heads * QB, width), BF),
            ],
        ),
        out_shape=[
            jax.ShapeDtypeStruct((length, 3 * width), BF),
            jax.ShapeDtypeStruct((2, heads, width), F32),
        ],
        compiler_params=params(),
        cost_estimate=pl.CostEstimate(
            flops=length * most * width * heads, bytes_accessed=8 << 20, transcendentals=0
        ),
        name="attend_back",
    )(start, mlx, mwx, q, do, k, v, soft, mixed)


def gelu_both(b):
    root = math.sqrt(2.0 / math.pi)
    square = b * b
    t = jnp.tanh(b * (root + (root * 0.044715) * square))
    half = 0.5 * t + 0.5
    value = b * half
    return value, half + (value * (1.0 - t)) * (root + (3.0 * root * 0.044715) * square)


FFB = 512


def feed_kernel(
    x_ref, o_ref, gain_ref, wo_ref, wi_ref, wb_ref, y_ref, middle_ref, normed_ref, slope_ref, hidden_ref, total
):
    blocks = [slice(r, r + ROWB) for r in range(0, x_ref.shape[0], ROWB)]

    @pl.when(pl.program_id(0) == 0)
    def _():
        for own in blocks:
            middle = x_ref[own, :].astype(F32) + dot_t(o_ref[own, :], wo_ref[...])
            middle_ref[own, :] = middle
            total[own, :] = middle
            scale = lax.rsqrt(jnp.mean(middle * middle, axis=-1, keepdims=True) + EPS)
            normed_ref[own, :] = (middle * scale * gain_ref[...]).astype(BF)

    before = dot(normed_ref[blocks[0], :], wi_ref[...])
    for n, own in enumerate(blocks):
        following = dot(normed_ref[blocks[n + 1], :], wi_ref[...]) if n + 1 < len(blocks) else None
        hidden, slope = gelu_both(before)
        hidden = hidden.astype(BF)
        hidden_ref[own, :] = hidden
        slope_ref[own, :] = slope.astype(BF)
        total[own, :] += dot_t(hidden, wb_ref[...])
        before = following

    @pl.when(pl.program_id(0) == pl.num_programs(0) - 1)
    def _():
        y_ref[...] = total[...].astype(BF)


def feed(x, o, gain, w, place_out, place_in, place_back):
    length, width = x.shape
    wide = 4 * width
    steps = wide // FFB
    chunk = pl.BlockSpec((length, FFB), lambda i: (0, i))
    flat = jax.ShapeDtypeStruct((length, width), BF)
    flat_wide = jax.ShapeDtypeStruct((length, wide), BF)
    all_rows = whole((length, width))
    return pl.pallas_call(
        feed_kernel,
        grid=(steps,),
        in_specs=[
            all_rows,
            all_rows,
            whole((1, width)),
            column((width, width), place_out),
            pl.BlockSpec((width, FFB), lambda i: (0, place_in * steps + i)),
            pl.BlockSpec((width, FFB), lambda i: (0, place_back * steps + i)),
        ],
        out_specs=[all_rows, all_rows, all_rows, chunk, chunk],
        out_shape=[flat, jax.ShapeDtypeStruct((length, width), F32), flat, flat_wide, flat_wide],
        scratch_shapes=[pltpu.VMEM((length, width), F32)],
        compiler_params=params(),
        cost_estimate=pl.CostEstimate(
            flops=18 * length * width * width, bytes_accessed=30 << 20, transcendentals=length * wide
        ),
        name="feed",
    )(x, o, gain, w, w, w)


def norm_back(values, gain, grad):
    scale = lax.rsqrt(jnp.mean(values * values, axis=-1, keepdims=True) + EPS)
    unit = values * scale
    dn = grad * gain
    return scale * (dn - unit * jnp.mean(dn * unit, axis=-1, keepdims=True))


def feed_back_kernel(
    dy_ref, slope_ref, middle_ref, gain_ref, wo_ref, wi_ref, wb_ref, gf_ref, dmiddle_ref, ga_ref, do_ref, total
):
    blocks = [slice(r, r + ROWB) for r in range(0, dy_ref.shape[0], ROWB)]

    @pl.when(pl.program_id(0) == 0)
    def _():
        total[...] = jnp.zeros_like(total)

    before = dot(dy_ref[blocks[0], :], wb_ref[...])
    for n, own in enumerate(blocks):
        following = dot(dy_ref[blocks[n + 1], :], wb_ref[...]) if n + 1 < len(blocks) else None
        gf = (before * slope_ref[own, :].astype(F32)).astype(BF)
        gf_ref[own, :] = gf
        total[own, :] += dot_t(gf, wi_ref[...])
        before = following

    @pl.when(pl.program_id(0) == pl.num_programs(0) - 1)
    def _():
        for own in blocks:
            dmiddle = dy_ref[own, :].astype(F32) + norm_back(middle_ref[own, :], gain_ref[...], total[own, :])
            dmiddle_ref[own, :] = dmiddle
            ga = dmiddle.astype(BF)
            ga_ref[own, :] = ga
            do_ref[own, :] = dot(ga, wo_ref[...]).astype(BF)


def feed_back(dy, slope, middle, gain, w, place_out, place_in, place_back):
    length, width = dy.shape
    wide = 4 * width
    steps = wide // FFB
    chunk = pl.BlockSpec((length, FFB), lambda i: (0, i))
    all_rows = whole((length, width))
    flat = jax.ShapeDtypeStruct((length, width), BF)
    return pl.pallas_call(
        feed_back_kernel,
        grid=(steps,),
        in_specs=[
            all_rows,
            chunk,
            all_rows,
            whole((1, width)),
            column((width, width), place_out),
            pl.BlockSpec((width, FFB), lambda i: (0, place_in * steps + i)),
            pl.BlockSpec((width, FFB), lambda i: (0, place_back * steps + i)),
        ],
        out_specs=[chunk, all_rows, all_rows, all_rows],
        out_shape=[
            jax.ShapeDtypeStruct((length, wide), BF),
            jax.ShapeDtypeStruct((length, width), F32),
            flat,
            flat,
        ],
        scratch_shapes=[pltpu.VMEM((length, width), F32)],
        compiler_params=params(),
        cost_estimate=pl.CostEstimate(flops=18 * length * width * width, bytes_accessed=40 << 20, transcendentals=0),
        name="feed_back",
    )(dy, slope, middle, gain, w, w, w)


def project_back_kernel(count, dqkv_ref, x_ref, dmiddle_ref, gain_ref, *refs):
    dx_ref = refs[-1]
    width = x_ref.shape[1]

    def body(pieces):
        dnormed = None
        for i, own in enumerate(pieces):
            for at, w_ref, start, columns in own:
                first = i * width + at
                term = dot_t(dqkv_ref[:, first : first + columns], w_ref[:, start : start + columns])
                dnormed = term if dnormed is None else dnormed + term
        dx_ref[...] = (dmiddle_ref[...] + norm_back(x_ref[...].astype(F32), gain_ref[...], dnormed)).astype(BF)

    with_weights(count, width, refs[:-1], body)


def project_back(dqkv, x, dmiddle, gain, weights):
    length, width = x.shape
    rows = pl.BlockSpec((ROWB, width), lambda i: (i, 0))
    specs, operands = weight_specs(weights, width)
    return pl.pallas_call(
        functools.partial(project_back_kernel, weights[0]),
        grid=(length // ROWB,),
        in_specs=[pl.BlockSpec((ROWB, 3 * width), lambda i: (i, 0)), rows, rows, whole((1, width))] + specs,
        out_specs=rows,
        out_shape=jax.ShapeDtypeStruct((length, width), BF),
        compiler_params=params(),
        cost_estimate=pl.CostEstimate(flops=length * width, bytes_accessed=1 << 16, transcendentals=0),
        name="project_back",
    )(dqkv, x, dmiddle, gain, *operands)


def grads_kernel(jobs, tiled, half_ref, *refs):
    out_ref = refs[-1]
    step = pl.program_id(0)
    first, at = 0, 0
    for n, (columns, tiles) in enumerate(jobs):
        left, right = refs[2 * n], refs[2 * n + 1]

        def body(left=left, right=right, first=first, at=at, columns=columns):
            grad = lax.dot_general(
                left[...], right[...], (((0,), (0,)), ((), ())), preferred_element_type=F32
            ).astype(BF)
            if tiled:
                out_ref[...] = grad
            else:
                place = pl.multiple_of(at + (step - first) * columns, 128)
                out_ref[:, pl.ds(place, columns)] = grad

        pl.when((step >= first) & (step < first + tiles))(body)
        first += tiles
        at += columns * tiles


def packed_grads(jobs, half, name):
    length, width = jobs[0][0].shape
    total = sum(columns * tiles for _, _, columns, tiles in jobs)
    steps = sum(tiles for _, _, _, tiles in jobs)
    tiled = len({columns for _, _, columns, _ in jobs}) == 1
    specs, operands, first = [], [], 0
    for left, right, columns, tiles in jobs:
        specs.append(whole((length, width)))
        specs.append(
            pl.BlockSpec(
                (length, columns),
                lambda i, h, first=first, tiles=tiles: (0, h[0] * tiles + jnp.clip(i - first, 0, tiles - 1)),
            )
        )
        operands += [left, right]
        first += tiles
    out_spec = pl.BlockSpec((width, jobs[0][2]), lambda i, h: (0, i)) if tiled else whole((width, total))
    return pl.pallas_call(
        functools.partial(grads_kernel, [(columns, tiles) for _, _, columns, tiles in jobs], tiled),
        grid_spec=pltpu.PrefetchScalarGridSpec(num_scalar_prefetch=1, grid=(steps,), in_specs=specs, out_specs=out_spec),
        out_shape=jax.ShapeDtypeStruct((width, total), BF),
        compiler_params=params(),
        cost_estimate=pl.CostEstimate(
            flops=2 * length * width * total, bytes_accessed=2 * (length + width) * (total + width), transcendentals=0
        ),
        name=name,
    )(half, *operands)


def mix_tables(mix_logits, mix_weights, size):
    logits = jnp.repeat(mix_logits.T * size ** (-0.5), size, axis=1)
    return logits * LOG2E, logits, jnp.repeat(mix_weights, size, axis=1)


def layer_forward(x, seg, weights, tables, projected, meanwhile):
    gains, _, w_rest, places = weights
    start, segc, segr = seg
    normed, q, k, v = projected
    o, soft, mixed = attend(start, tables[2], tables[0], q, k, v, segc, segr)
    o, meanwhile = lax.optimization_barrier((o, meanwhile))
    y, middle, normed_two, slope, hidden = feed(x, o, gains[1], w_rest, *places)
    return y, (x, normed, q, None, k, v, o, soft, mixed, middle, normed_two, slope, hidden), meanwhile


def windows(seg):
    length = seg.shape[0]
    last = seg[QB - 1 :: QB]
    first = seg[::QB]
    start = jnp.sum((last[None, :] < first[:, None]).astype(jnp.int32), axis=1)
    return start, seg[:, None], seg[None, :]


AXES = ("dp", "section")


def swap(x):
    return lax.ppermute(x, "section", [(0, 1), (1, 0)])


def partners(x, mask):
    return lax.ppermute(x, "dp", [(i, i ^ mask) for i in range(lax.axis_size("dp"))])


def bit_groups():
    bits = lax.axis_size("dp").bit_length() - 1
    return [(at, 1 << min(2, bits - at)) for at in range(0, bits, 2)]


def gather_rows(own, meanwhile):
    share, columns = own.shape
    place = lax.axis_index("dp")
    done = own[None]
    for n, (shift, members) in enumerate(reversed(bit_groups())):
        if n == 1:
            done, meanwhile = lax.optimization_barrier((done, meanwhile))
        me = (place >> shift) & (members - 1)
        out = jnp.zeros((done.shape[0], members, share, columns), own.dtype)
        for other in range(members):
            piece = done if other == 0 else partners(done, other << shift)
            out = lax.dynamic_update_slice(out, piece[:, None], (0, me ^ other, 0, 0))
        done = out.reshape(-1, share, columns)
    return done.reshape(-1, columns), meanwhile


def gather_under(own, kernel):
    rows, results = gather_rows(own, kernel())
    return results, rows


def send_parts(held, group):
    shift, members = group
    share, columns = held.shape[1:]
    me = (lax.axis_index("dp") >> shift) & (members - 1)
    held = held.reshape(-1, members, share, columns)
    parts = [lax.dynamic_index_in_dim(held, me ^ other, 1, keepdims=False) for other in range(members)]
    return [parts[0]] + [partners(part.astype(BF), other << shift) for other, part in enumerate(parts) if other]


def add_parts(parts):
    return sum(part.astype(F32) for part in parts)


def shares_of(rows):
    size = lax.axis_size("dp")
    return rows.reshape(size, rows.shape[0] // size, rows.shape[1])


def finish_sum(parts, groups):
    total = add_parts(parts)
    for group in groups:
        total = add_parts(send_parts(total, group))
    return total[0]


def sum_masks(x, masks):
    for mask in masks:
        x = x + partners(x, mask)
    return x


def on_device(
    tokens,
    segments,
    cotangent,
    gain_attn,
    gain_ffn,
    w_query,
    w_key,
    w_value,
    w_out,
    w_in,
    w_back,
    mix_logits,
    mix_weights,
):
    section = lax.axis_index("section")
    first = section == 0
    width = tokens.shape[2]
    heads = mix_logits.shape[1]
    size = width // heads
    share = w_query.shape[1]
    half = share // 2
    wide = w_in.shape[2]
    middle = 3 * width // 2

    x0 = lax.dynamic_index_in_dim(tokens, section, 0, keepdims=False)
    seg = windows(lax.dynamic_index_in_dim(segments, section, 0, keepdims=False))
    cot = lax.dynamic_index_in_dim(cotangent, section, 0, keepdims=False)

    gains = jnp.concatenate([gain_attn, gain_ffn], 0).astype(BF)
    gain_columns = jnp.pad(gains.T, ((0, 0), (0, 126)))
    qkv = jnp.concatenate([w_query[0], w_key[0], w_value[0]], 1).astype(BF)
    low = jnp.concatenate([qkv[:, :middle], gain_columns], 1)
    high = jnp.concatenate([qkv[:, middle:], gain_columns], 1)
    arrived = swap(jnp.where(first, high, low))
    own_half, (x0, seg, cot) = gather_rows(jnp.where(first, low, arrived), (x0, seg, cot))
    other_half = swap(own_half)

    late = jnp.concatenate([w_in[0].astype(BF), w_back[0].T.astype(BF), w_out[0].T.astype(BF)], 1)

    def halves(own):
        other = swap(jnp.where(first, own[half:], own[:half]))
        return jnp.where(first, own[:half], other), jnp.where(first, other, own[half:])

    late0, late1 = halves(late)
    second = lax.all_gather(late0, AXES, axis=0, tiled=True)
    third = lax.all_gather(late1, AXES, axis=0, tiled=True)

    own_mix = jnp.concatenate([mix_logits, mix_weights], 0)
    other_mix = swap(own_mix)
    mix0 = jnp.where(first, own_mix, other_mix)
    mix1 = jnp.where(first, other_mix, own_mix)
    tables = [mix_tables(m[0], m[1], size) for m in (mix0, mix1)]

    def gain_rows(columns):
        rows = columns[:, :2].astype(F32).T
        return rows[0:1], rows[1:2]

    at_out = 2 * wide // width
    qkv0 = (2, (section.astype(jnp.int32).reshape(1), own_half, other_half), ())
    weights0 = (gain_rows(own_half[:, middle:]), qkv0, second, (at_out, 0, 1))

    projected, own_half = gather_under(
        jnp.where(first, arrived, high), lambda: project(x0, weights0[0][0], qkv0)
    )
    y0, kept0, own_half = layer_forward(x0, seg, weights0, tables[0], projected, own_half)
    qkv1 = (2, (section.astype(jnp.int32).reshape(1), own_half, swap(own_half)), ())
    weights1 = (gain_rows(own_half[:, middle:]), qkv1, third, (at_out, 0, 1))
    y1, kept1, _ = layer_forward(y0, seg, weights1, tables[1], project(y0, weights1[0][0], qkv1), ())

    def back_feed(dy, kept, weights):
        slope, middle_rows = kept[11], kept[9]
        return feed_back(dy, slope, middle_rows, weights[0][1], weights[2], *weights[3])

    def back_attend(do, kept, table):
        _, _, q, _, k, v, _, soft, mixed = kept[:9]
        return attend_back(seg[0], table[1], table[2], q, do, k, v, soft, mixed)

    groups = bit_groups()
    masks = [1 << bit for bit in range(lax.axis_size("dp").bit_length() - 1)]
    barrier = lax.optimization_barrier
    here = section.astype(jnp.int32).reshape(1)
    away = 1 - here

    def outputs(own0, own1, other0, other1):
        return jnp.where(first, jnp.stack([own0, other0]), jnp.stack([other1, own1]))[None]

    def to_first(x):
        return lax.ppermute(x, "section", [(1, 0)])

    def to_second(x):
        return lax.ppermute(x, "section", [(0, 1)])

    def both_halves(jobs, name):
        arrived = swap(packed_grads(jobs, away, name + "_away"))
        return packed_grads(jobs, here, name + "_here"), arrived

    def added(halves):
        return shares_of(halves[0].astype(F32) + halves[1].astype(F32))

    def projection_jobs(normed, dqkv):
        return [(normed, dqkv, dqkv.shape[1] // 6, 3)]

    y_other = to_first(y0), to_second(y1)
    (gf, dmiddle, ga, do), y_other = barrier((back_feed(cot, kept1, weights1), y_other))
    packed1 = packed_grads(
        [(kept1[10], gf, width, 4), (cot, kept1[12], width, 4), (ga, kept1[6], width, 1)],
        jnp.zeros((1,), jnp.int32),
        "grads_feed",
    )
    do, packed1 = barrier((do, packed1))
    sums1 = lax.psum_scatter(packed1, AXES, scatter_dimension=0, tiled=True)
    dqkv, sums_mix1 = back_attend(do, kept1, tables[1])
    halves = both_halves(projection_jobs(kept1[1], dqkv), "grads_project")
    dx1 = project_back(dqkv, kept1[0], dmiddle, weights1[0][0], qkv1)
    dx1, halves = barrier((dx1, halves))
    parts1 = send_parts(added(halves), groups[0])

    dx1_other = to_second(dx1)
    fed, parts1, dx1_other = barrier((back_feed(dx1, kept0, weights0), parts1, dx1_other))
    gf, dmiddle, ga, do = fed
    parts1 = send_parts(add_parts(parts1), groups[1])
    halves = both_halves(
        [(kept0[10], gf, width, 2), (dx1, kept0[12], width, 2), (ga, kept0[6], width // 2, 1)], "grads_feed"
    )
    do, halves, parts1 = barrier((do, halves, parts1))
    proj1 = finish_sum(parts1, groups[2:])
    held = added(halves).astype(BF)
    do, held, proj1 = barrier((do, held, proj1))
    parts0 = send_parts(held, groups[0])
    (dqkv, sums_mix0), parts0[:2], sums1 = barrier((back_attend(do, kept0, tables[0]), parts0[:2], sums1))
    mixes = jnp.sum(jnp.stack([sums_mix0, sums_mix1]).reshape(2, 2, heads, heads, size), axis=4)
    mixes = sum_masks(mixes + swap(mixes), masks[:2])
    dqkv, parts0, mixes = barrier((dqkv, parts0, mixes))
    held = add_parts(parts0).astype(BF)
    parts0 = send_parts(held, groups[1])
    gone = packed_grads(projection_jobs(kept0[1], dqkv), away, "grads_project_away")
    dqkv, gone, held = barrier((dqkv, gone, held))
    halves = packed_grads(projection_jobs(kept0[1], dqkv), here, "grads_project_here"), swap(gone)
    held = added(halves).astype(BF)
    dqkv, held = barrier((dqkv, held))
    parts = send_parts(held, groups[0])
    dx0 = project_back(dqkv, kept0[0], dmiddle, weights0[0][0], qkv0)
    dx0, y0, y1, y_other, mixes, sums1 = barrier((dx0, y0, y1, y_other, mixes, sums1))
    section_out = outputs(y0, y1, *y_other)
    dx0, parts, parts0, section_out, mixes = barrier((dx0, parts, parts0, section_out, mixes))
    held = add_parts(parts).astype(BF)
    dx0, held, parts0, mixes, sums1 = barrier((dx0, held, parts0, mixes, sums1))
    parts = send_parts(held, groups[1])
    parts[:2], dx0, parts0, mixes, sums1 = barrier((parts[:2], dx0, parts0, mixes, sums1))
    dx0_other = to_first(dx0)
    ffn0 = finish_sum(parts0, groups[2:])
    mixes = sum_masks(mixes, masks[2:])
    mixes = jnp.where(first, mixes[0], mixes[1])
    proj0 = finish_sum(parts, groups[2:])

    ffn0_other = lax.ppermute(ffn0, "section", [(1, 0)])
    sums1_other = lax.ppermute(sums1, "section", [(0, 1)])
    proj_other = swap(jnp.where(first, proj1, proj0))
    sums1 = jnp.concatenate([sums1_other, sums1], 0).astype(F32)
    cuts = (0, wide // 2, wide, wide + width // 2)

    def join(i):
        return jnp.concatenate([ffn0[:, cuts[i] : cuts[i + 1]], ffn0_other[:, cuts[i] : cuts[i + 1]]], 1)

    grad_in = jnp.where(first, join(0), sums1[:, :wide])
    grad_back = jnp.where(first, join(1), sums1[:, wide : 2 * wide])
    grad_out = jnp.where(first, join(2), sums1[:, 2 * wide :])
    grad_qkv = jnp.concatenate([jnp.where(first, proj0, proj_other), jnp.where(first, proj_other, proj1)], 1)

    def gain_grad(pairs, gain):
        total = sum(jnp.sum(w.astype(BF).astype(F32) * g, axis=1) for w, g in pairs)
        return (total / gain[0].astype(BF).astype(F32))[None]

    parts = [grad_qkv[:, i * width : (i + 1) * width] for i in range(3)]
    gg_attn = gain_grad(list(zip((w_query[0], w_key[0], w_value[0]), parts)), gain_attn)
    gg_ffn = gain_grad([(w_in[0], grad_in)], gain_ffn)

    return (
        section_out,
        outputs(dx0, dx1, dx0_other, dx1_other),
        gg_attn,
        gg_ffn,
        parts[0][None],
        parts[1][None],
        parts[2][None],
        grad_out.T[None],
        grad_in[None],
        grad_back.T[None],
        mixes[0].T[None] * size ** (-0.5),
        mixes[1][None],
    )


def solution(mesh):
    rows = P("dp", None, None)
    by_row = P("section", "dp", None)
    by_column = P("section", None, "dp")
    shared = P("section", None, None)
    gain = P("section", "dp")
    return jax.shard_map(
        on_device,
        mesh=mesh,
        in_specs=(
            rows,
            P("dp", None),
            rows,
            gain,
            gain,
            by_row,
            by_row,
            by_row,
            by_column,
            by_row,
            by_column,
            shared,
            shared,
        ),
        out_specs=(
            P("section", "dp", None, None),
            P("section", "dp", None, None),
            gain,
            gain,
            by_row,
            by_row,
            by_row,
            by_column,
            by_row,
            by_column,
            shared,
            shared,
        ),
        check_vma=False,
    )
```
